32 devices in a mesh: dp: 2 (over x), ctx: 16 (over z, y, core).
Axes of the slice: x: 2, y: 2, z: 4, core: 2. Of those that a mesh axis runs over, the one named last changes fastest.
Arguments:
- q_proj: float32 [8192, 512], P(('dp', 'ctx')), parts along dimension 0, may hold values from -6 to 6
- k_proj: float32 [8192, 512], P(('dp', 'ctx')), parts along dimension 0, may hold values from -6 to 6
- v_proj: float32 [8192, 512], P(('dp', 'ctx')), parts along dimension 0, may hold values from -6 to 6
- short_filter: float32 [3, 3, 512], replicated, may hold values from -3 to 3
- skip_gain: float32 [512], replicated, may hold values from -4 to 4
- filter_spec: float32 [2, 8192, 512], P(None, 'ctx'), may hold values from -6 to 6
Outputs:
- gated: float32 [8192, 512], P(('dp', 'ctx')), parts along dimension 0
The draws below stay inside these ranges and needn't reach their ends.
There are 2 independent parts, one for each index of `dp`. The reference program is written for one: setup_inputs(seed, part) draws one part's arguments, and reference() takes and returns one part's arrays. A program takes and returns all parts, laid end to end along the dimension named above; an argument that names none is the same for every part. Nothing has to cross between parts.
All inputs are finite; a program needn't handle non-finite values.
Results may differ from the reference program's by a relative error of at most 0.000061.
Values sent between devices are 32-bit elements; how exact they have to be, the bound alone decides.
No kernel may reach another device: no remote copies, remote signals or barrier semaphores. Data moves between devices by JAX's collectives and lax.ppermute only.
A program may use at most 64 MiB of HBM per device.

```python
import jax
import jax.numpy as jnp
from jax import lax

CH = 512
SEQ = 4096
FREQ = 8192


def level_of(stream_key, dims, shards, smallest, top_value):
    level, own = 1.0, jax.random.fold_in(stream_key, 6)
    for axis_at, parts in shards:
        steps = jnp.exp(jax.random.uniform(jax.random.fold_in(own, axis_at), (parts,), jnp.float32, smallest / len(shards), top_value / len(shards)))
        level = level * jnp.repeat(steps, dims[axis_at] // parts).reshape([-1 if axis == axis_at else 1 for axis in range(len(dims))])
    return level


def bell_draw(rng, shape, width, bound, cuts=(), held_as=jnp.bfloat16):
    array = jax.random.normal(rng, shape, jnp.float32) * width
    if len(cuts) > 0:
        array = level_of(rng, shape, cuts, -0.22, 0.18) * array
    return jnp.clip(array, min=-bound, max=bound).astype(held_as)


def setup_inputs(seed: int = 0, part: int = 0) -> dict:
    key_list = jax.random.split(jax.random.key(seed), 7)
    part_splits = jax.random.split(jax.random.fold_in(key_list[6], part), 7)
    return {
        "q_proj": bell_draw(part_splits[0], (SEQ, CH), 1.0, 6.0, ((0, 16),), jnp.float32),
        "k_proj": bell_draw(part_splits[1], (SEQ, CH), 1.0, 6.0, ((0, 16),), jnp.float32),
        "v_proj": bell_draw(part_splits[2], (SEQ, CH), 1.0, 6.0, ((0, 16),), jnp.float32),
        "short_filter": bell_draw(key_list[3], (3, 3, CH), 0.6, 3.0, (), jnp.float32),
        "skip_gain": bell_draw(key_list[4], (CH,), 1.0, 4.0, (), jnp.float32),
        "filter_spec": bell_draw(key_list[5], (2, FREQ, CH), 1.0, 6.0, ((1, 16),), jnp.float32),
    }


def causal_short(signal, tap_gains):
    padded = jnp.concatenate([jnp.zeros((2, signal.shape[1]), jnp.float32), signal], axis=0)
    return tap_gains[0] * signal + tap_gains[1] * padded[1:-1] + tap_gains[2] * padded[:-2]


def reference(q_proj, k_proj, v_proj, short_filter, skip_gain, filter_spec):
    query_seq = causal_short(q_proj, short_filter[0])
    key_seq = causal_short(k_proj, short_filter[1])
    value_seq = causal_short(v_proj, short_filter[2])
    mixed_in = key_seq * value_seq
    spectrum = jnp.fft.fft(mixed_in, n=FREQ, axis=0)
    response = lax.complex(filter_spec[0], filter_spec[1])
    conv_full = jnp.fft.ifft(spectrum * response, axis=0)
    conv_out = jnp.real(conv_full[:SEQ])
    return query_seq * (conv_out + skip_gain[None, :] * mixed_in)
```

```python
import functools
import math

import jax
import jax.numpy as jnp
import numpy as np
from jax import lax
from jax.experimental import pallas as pl
from jax.experimental.pallas import tpu as pltpu
from jax.sharding import PartitionSpec as P

precise_mode = lax.Precision.HIGHEST
LANES = 128
BF16 = jnp.bfloat16
F32 = jnp.float32


def causal_short(signal, rim_rows, tap_gains):
    padded = jnp.concatenate([rim_rows, signal], axis=0)
    return tap_gains[0] * signal + tap_gains[1] * padded[1:-1] + tap_gains[2] * padded[:-2]


def shifted(block, axis, distance):
    devices = range(lax.axis_size(axis))
    route = [(i - distance, i) for i in devices if i - distance in devices]
    return lax.ppermute(block, axis, route)


def channel_conv(mixed_in, filter_spec, devices):
    local_rows = mixed_in.shape[0]
    seq_len = local_rows * devices
    freq_len = 2 * seq_len
    outer_len = 2 * devices
    half_inner = local_rows // 2
    columns = lax.all_to_all(mixed_in, "ctx", split_axis=1, concat_axis=0, tiled=True)
    spec_cols = lax.all_to_all(filter_spec, "ctx", split_axis=2, concat_axis=1, tiled=True)
    few_channels = columns.shape[1]
    grid = columns.reshape(half_inner, outer_len, few_channels)
    row_index = lax.iota(jnp.int32, half_inner)
    inner_freq = lax.iota(jnp.int32, local_rows)
    outer_index = lax.iota(jnp.int32, outer_len)

    def cos_sin(left, right, period):
        turns = (left[:, None] * right[None, :] % period).astype(F32) / period
        return jnp.cos(2.0 * math.pi * turns), jnp.sin(2.0 * math.pi * turns)

    first_cos, first_sin = cos_sin(row_index, inner_freq, local_rows)
    twist_cos, twist_sin = cos_sin(inner_freq, outer_index, freq_len)
    twist_cos, twist_sin = twist_cos[:, :, None], twist_sin[:, :, None]
    last_cos, last_sin = cos_sin(outer_index, outer_index, outer_len)
    dots = functools.partial(jnp.einsum, precision=precise_mode)
    section_re = dots("bk,bac->kac", first_cos, grid)
    section_im = -dots("bk,bac->kac", first_sin, grid)
    turned_re = section_re * twist_cos + section_im * twist_sin
    turned_im = section_im * twist_cos - section_re * twist_sin
    fore = "kac,aj->kjc"
    spec_re = dots(fore, turned_re, last_cos) + dots(fore, turned_im, last_sin)
    spec_im = dots(fore, turned_im, last_cos) - dots(fore, turned_re, last_sin)
    resp = jnp.transpose(spec_cols.reshape(2, outer_len, local_rows, few_channels), (0, 2, 1, 3))
    prod_re = spec_re * resp[0] - spec_im * resp[1]
    prod_im = spec_re * resp[1] + spec_im * resp[0]
    back = "kjc,aj->kac"
    undo_re = dots(back, prod_re, last_cos) - dots(back, prod_im, last_sin)
    undo_im = dots(back, prod_im, last_cos) + dots(back, prod_re, last_sin)
    back_re = undo_re * twist_cos - undo_im * twist_sin
    back_im = undo_im * twist_cos + undo_re * twist_sin
    signal_out = dots("bk,kac->bac", first_cos, back_re) - dots("bk,kac->bac", first_sin, back_im)
    conv_cols = signal_out.reshape(seq_len, few_channels) / freq_len
    return lax.all_to_all(conv_cols, "ctx", split_axis=0, concat_axis=1, tiled=True)


def per_device_general(q_proj, k_proj, v_proj, short_filter, skip_gain, filter_spec):
    devices = lax.axis_size("ctx")
    tail_rows = jnp.stack([q_proj[-2:], k_proj[-2:], v_proj[-2:]])
    rim_rows = shifted(tail_rows, "ctx", 1)
    query_seq = causal_short(q_proj, rim_rows[0], short_filter[0])
    key_seq = causal_short(k_proj, rim_rows[1], short_filter[1])
    value_seq = causal_short(v_proj, rim_rows[2], short_filter[2])
    mixed_in = key_seq * value_seq
    conv_out = channel_conv(mixed_in, filter_spec, devices)
    return query_seq * (conv_out + skip_gain[None, :] * mixed_in)


def split_np(table):
    high = table.astype(BF16)
    low = (table - high.astype(np.float64)).astype(BF16)
    return high, low


@functools.lru_cache(maxsize=None)
def tables(parts, devices, rows):
    outer, seq = 2 * devices, devices * rows
    freq = 2 * seq
    p, s, r = np.arange(devices), np.arange(outer), np.arange(rows)
    chunks = rows * 2 // parts // 64
    low_bit, chunk, part, dev = np.meshgrid(
        np.arange(2), np.arange(chunks), np.arange(parts), np.arange(devices), indexing="ij"
    )
    k = (dev * (2 * rows // outer) + part * (2 * rows // parts // outer) + 2 * chunk + low_bit).ravel()

    def angle(left, right, period):
        return 2.0 * np.pi * (np.outer(left, right) % period) / period

    first = angle(s, p, outer)
    w1h, w1l = split_np(np.concatenate([np.cos(first), -np.sin(first)]))
    w1 = np.concatenate([w1h, w1h, w1l], axis=1)
    last = np.concatenate([np.cos(first.T), -np.sin(first.T)], axis=1) / freq
    w2h, w2l = split_np(last)
    w2 = np.concatenate([w2h, w2h, w2l], axis=1)
    twist = angle(s, r, freq)
    inner = angle(r, k, rows)
    c, d = np.cos(inner), np.sin(inner)
    fore = split_np(np.block([[c, -d], [d, c]]))
    back = split_np(np.block([[c.T, d.T], [-d.T, c.T]]))
    return (w1, w2, np.cos(twist).astype(np.float32), np.sin(twist).astype(np.float32), *fore, *back)


def split(x):
    high = x.astype(BF16)
    return high, (x - high.astype(F32)).astype(BF16)


def dot(a, b):
    return jnp.dot(a, b, preferred_element_type=F32)


def causal(x, rim, taps):
    row = lax.broadcasted_iota(jnp.int32, x.shape, 0)
    one = jnp.where(row == 0, rim[1:2], pltpu.roll(x, 1, 0))
    two = jnp.where(row == 0, rim[0:1], jnp.where(row == 1, rim[1:2], pltpu.roll(x, 2, 0)))
    return taps[0:1] * x + taps[1:2] * one + taps[2:3] * two


def spec_kernel(few, part_ref, spec_ref, out_ref):
    del part_ref
    for m in range(spec_ref.shape[1] // 64):
        both = jnp.concatenate(
            [spec_ref[0, 64 * m : 64 * m + 64], spec_ref[1, 64 * m : 64 * m + 64]], axis=0
        )
        out_ref[:, few * m : few * m + few, :] = both.T.reshape(LANES // few, few, LANES)


def mixed_kernel(few, k_ref, v_ref, rim_ref, taps_ref, held_ref, out_ref):
    del held_ref
    key_seq = causal(k_ref[...], rim_ref[2:4], taps_ref[1])
    value_seq = causal(v_ref[...], rim_ref[4:6], taps_ref[2])
    mixed_in = key_seq * value_seq
    for h in range(mixed_in.shape[0] // LANES):
        turned = mixed_in[LANES * h : LANES * h + LANES].T
        out_ref[:, few * h : few * h + few, :] = turned.reshape(LANES // few, few, LANES)


def local_kernel(q_ref, k_ref, v_ref, rim_ref, taps_ref, gain_ref, query_ref, direct_ref):
    query_seq = causal(q_ref[...], rim_ref[0:2], taps_ref[0])
    key_seq = causal(k_ref[...], rim_ref[2:4], taps_ref[1])
    value_seq = causal(v_ref[...], rim_ref[4:6], taps_ref[2])
    query_ref[...] = query_seq
    direct_ref[...] = query_seq * (gain_ref[...] * (key_seq * value_seq))


def gate_kernel(conv_ref, query_ref, direct_ref, out_ref):
    few, rows = conv_ref.shape[1:]
    conv = conv_ref[...].reshape(conv_ref.shape[0] * few, rows)
    out_ref[...] = query_ref[...] * conv.T + direct_ref[...]


def conv_kernel(
    parts, few, chunks, in_ref, w1_ref, w2_ref, cos_ref, sin_ref, fh_ref, fl_ref, bh_ref, bl_ref,
    out_ref, yh, yl, ph, pq,
):
    devices = in_ref.shape[0] // parts
    outer = 2 * devices
    rows = out_ref.shape[2]
    base = few * chunks
    cosines, sines = cos_ref[...], sin_ref[...]

    def keep(high_ref, low_ref, at, real, imag):
        for col, x in ((0, real), (rows, imag)):
            high, low = split(x)
            high_ref[at : at + outer, col : col + rows] = high
            low_ref[at : at + outer, col : col + rows] = low

    for c in range(few):
        for q in range(parts):
            block = slice(q * devices, (q + 1) * devices)
            x = jnp.concatenate(
                [in_ref[block, base + few * h + c, :] for h in range(rows // LANES)], axis=1
            )
            high, low = split(x)
            y = dot(w1_ref[...], jnp.concatenate([high, low, high], axis=0))
            re, im = y[:outer], y[outer:]
            keep(yh, yl, (c * parts + q) * outer, re * cosines + im * sines, im * cosines - re * sines)

    group = 4
    step = group * parts * outer
    for g in range(few // group):
        span = slice(g * step, (g + 1) * step)
        spec = dot(yh[span], fh_ref[...]) + dot(yl[span], fh_ref[...]) + dot(yh[span], fl_ref[...])
        for i in range(group):
            c = g * group + i
            resp = jnp.concatenate([in_ref[:, few * m + c, :] for m in range(chunks)], axis=0).T
            h_re = jnp.concatenate([resp[:outer], resp[outer : 2 * outer]], axis=1)
            h_im = jnp.concatenate([resp[2 * outer : 3 * outer], resp[3 * outer :]], axis=1)
            for q in range(parts):
                at = (i * parts + q) * outer
                re, im = spec[at : at + outer, :rows], spec[at : at + outer, rows:]
                keep(ph, pq, g * step + at, re * h_re - im * h_im, re * h_im + im * h_re)
        undo = dot(ph[span], bh_ref[...]) + dot(pq[span], bh_ref[...]) + dot(ph[span], bl_ref[...])
        for i in range(group):
            c = g * group + i
            for q in range(parts):
                at = (i * parts + q) * outer
                re, im = undo[at : at + outer, :rows], undo[at : at + outer, rows:]
                turned = jnp.concatenate([re * cosines - im * sines, im * cosines + re * sines], axis=0)
                high, low = split(turned)
                y = dot(w2_ref[...], jnp.concatenate([high, low, high], axis=0))
                out_ref[q * devices : (q + 1) * devices, c, :] = y


def per_device_tiled(q_proj, k_proj, v_proj, short_filter, skip_gain, filter_spec):
    parts, devices = lax.axis_size("dp"), lax.axis_size("ctx")
    everyone = parts * devices
    rows, channels = q_proj.shape
    few = channels // everyone
    chunks = 2 * rows // parts // 64
    halves = rows // LANES
    blocks = channels // LANES
    near = LANES // few
    depth = few * (chunks + halves)
    outer = 2 * devices
    whole = pl.BlockSpec(memory_space=pltpu.VMEM)

    tails = jnp.concatenate([q_proj[-2:], k_proj[-2:], v_proj[-2:]], axis=0)
    rim = shifted(tails, "ctx", 1)

    part = lax.axis_index("dp").reshape(1)
    packed = jax.ShapeDtypeStruct((everyone, depth, LANES), F32)
    held = pl.pallas_call(
        functools.partial(spec_kernel, few),
        out_shape=packed,
        grid_spec=pltpu.PrefetchScalarGridSpec(
            num_scalar_prefetch=1,
            grid=(blocks,),
            in_specs=[pl.BlockSpec((2, 64 * chunks, LANES), lambda i, s: (0, s[0], i))],
            out_specs=pl.BlockSpec((near, few * chunks, LANES), lambda i, s: (i, 0, 0)),
        ),
        cost_estimate=pl.CostEstimate(flops=0, bytes_accessed=1 << 21, transcendentals=0),
    )(part, filter_spec)

    column = pl.BlockSpec((rows, LANES), lambda i: (0, i))
    rim_spec = pl.BlockSpec((6, LANES), lambda i: (0, i))
    taps_spec = pl.BlockSpec((3, 3, LANES), lambda i: (0, 0, i))
    sent = pl.pallas_call(
        functools.partial(mixed_kernel, few),
        out_shape=packed,
        grid=(blocks,),
        in_specs=[column, column, rim_spec, taps_spec, pl.BlockSpec(memory_space=pl.ANY)],
        out_specs=pl.BlockSpec((near, few * halves, LANES), lambda i: (i, chunks // halves, 0)),
        input_output_aliases={4: 0},
        cost_estimate=pl.CostEstimate(flops=0, bytes_accessed=3 << 19, transcendentals=0),
    )(k_proj, v_proj, rim, short_filter, held)

    come = lax.all_to_all(sent, ("dp", "ctx"), 0, 0, tiled=True)

    query_seq, direct = pl.pallas_call(
        local_kernel,
        out_shape=[jax.ShapeDtypeStruct((rows, channels), F32)] * 2,
        grid=(blocks,),
        in_specs=[column, column, column, rim_spec, taps_spec, pl.BlockSpec((1, LANES), lambda i: (0, i))],
        out_specs=[column, column],
        cost_estimate=pl.CostEstimate(flops=0, bytes_accessed=5 << 19, transcendentals=0),
    )(q_proj, k_proj, v_proj, rim, short_filter, skip_gain[None, :])

    total = few * parts * outer
    conv = pl.pallas_call(
        functools.partial(conv_kernel, parts, few, chunks),
        out_shape=jax.ShapeDtypeStruct((everyone, few, rows), F32),
        in_specs=[whole] * 9,
        out_specs=whole,
        scratch_shapes=[pltpu.VMEM((total, 2 * rows), BF16)] * 4,
        compiler_params=pltpu.CompilerParams(vmem_limit_bytes=48 << 20),
        cost_estimate=pl.CostEstimate(flops=0, bytes_accessed=4 << 20, transcendentals=0),
    )(come, *(jnp.asarray(t) for t in tables(parts, devices, rows)))

    back = lax.all_to_all(conv, ("dp", "ctx"), 0, 0, tiled=True)
    return pl.pallas_call(
        gate_kernel,
        out_shape=jax.ShapeDtypeStruct((rows, channels), F32),
        grid=(blocks,),
        in_specs=[pl.BlockSpec((near, few, rows), lambda i: (i, 0, 0)), column, column],
        out_specs=column,
        cost_estimate=pl.CostEstimate(flops=0, bytes_accessed=1 << 21, transcendentals=0),
    )(back, query_seq, direct)


def fits_tiles(mesh, rows, channels):
    parts, devices = mesh.shape["dp"], mesh.shape["ctx"]
    few, rest = divmod(channels, parts * devices)
    chunks = 2 * rows // parts // 64
    return (
        rest == 0
        and few % 8 == 0
        and 2 * devices == 32
        and rows % LANES == 0
        and parts * devices * chunks == LANES
        and chunks % (rows // LANES) == 0
    )


def solution(mesh):
    placed = (
        P(("dp", "ctx"), None),
        P(("dp", "ctx"), None),
        P(("dp", "ctx"), None),
        P(),
        P(),
        P(None, "ctx", None),
    )

    def per_device(q_proj, *rest):
        form = per_device_tiled if fits_tiles(mesh, *q_proj.shape) else per_device_general
        return form(q_proj, *rest)

    return jax.shard_map(
        per_device, mesh=mesh, in_specs=placed, out_specs=P(("dp", "ctx"), None), check_vma=False
    )
```

```python
import functools
import math

import jax
import jax.numpy as jnp
import numpy as np
from jax import lax
from jax.experimental import pallas as pl
from jax.experimental.pallas import tpu as pltpu
from jax.sharding import PartitionSpec as P

precise_mode = lax.Precision.HIGHEST
LANES = 128
BF16 = jnp.bfloat16
F32 = jnp.float32


def causal_short(signal, rim_rows, tap_gains):
    padded = jnp.concatenate([rim_rows, signal], axis=0)
    return tap_gains[0] * signal + tap_gains[1] * padded[1:-1] + tap_gains[2] * padded[:-2]


def shifted(block, axis, distance):
    devices = range(lax.axis_size(axis))
    route = [(i - distance, i) for i in devices if i - distance in devices]
    return lax.ppermute(block, axis, route)


def channel_conv(mixed_in, filter_spec, devices):
    local_rows = mixed_in.shape[0]
    seq_len = local_rows * devices
    freq_len = 2 * seq_len
    outer_len = 2 * devices
    half_inner = local_rows // 2
    columns = lax.all_to_all(mixed_in, "ctx", split_axis=1, concat_axis=0, tiled=True)
    spec_cols = lax.all_to_all(filter_spec, "ctx", split_axis=2, concat_axis=1, tiled=True)
    few_channels = columns.shape[1]
    grid = columns.reshape(half_inner, outer_len, few_channels)
    row_index = lax.iota(jnp.int32, half_inner)
    inner_freq = lax.iota(jnp.int32, local_rows)
    outer_index = lax.iota(jnp.int32, outer_len)

    def cos_sin(left, right, period):
        turns = (left[:, None] * right[None, :] % period).astype(F32) / period
        return jnp.cos(2.0 * math.pi * turns), jnp.sin(2.0 * math.pi * turns)

    first_cos, first_sin = cos_sin(row_index, inner_freq, local_rows)
    twist_cos, twist_sin = cos_sin(inner_freq, outer_index, freq_len)
    twist_cos, twist_sin = twist_cos[:, :, None], twist_sin[:, :, None]
    last_cos, last_sin = cos_sin(outer_index, outer_index, outer_len)
    dots = functools.partial(jnp.einsum, precision=precise_mode)
    section_re = dots("bk,bac->kac", first_cos, grid)
    section_im = -dots("bk,bac->kac", first_sin, grid)
    turned_re = section_re * twist_cos + section_im * twist_sin
    turned_im = section_im * twist_cos - section_re * twist_sin
    fore = "kac,aj->kjc"
    spec_re = dots(fore, turned_re, last_cos) + dots(fore, turned_im, last_sin)
    spec_im = dots(fore, turned_im, last_cos) - dots(fore, turned_re, last_sin)
    resp = jnp.transpose(spec_cols.reshape(2, outer_len, local_rows, few_channels), (0, 2, 1, 3))
    prod_re = spec_re * resp[0] - spec_im * resp[1]
    prod_im = spec_re * resp[1] + spec_im * resp[0]
    back = "kjc,aj->kac"
    undo_re = dots(back, prod_re, last_cos) - dots(back, prod_im, last_sin)
    undo_im = dots(back, prod_im, last_cos) + dots(back, prod_re, last_sin)
    back_re = undo_re * twist_cos - undo_im * twist_sin
    back_im = undo_im * twist_cos + undo_re * twist_sin
    signal_out = dots("bk,kac->bac", first_cos, back_re) - dots("bk,kac->bac", first_sin, back_im)
    conv_cols = signal_out.reshape(seq_len, few_channels) / freq_len
    return lax.all_to_all(conv_cols, "ctx", split_axis=0, concat_axis=1, tiled=True)


def per_device_general(q_proj, k_proj, v_proj, short_filter, skip_gain, filter_spec):
    devices = lax.axis_size("ctx")
    tail_rows = jnp.stack([q_proj[-2:], k_proj[-2:], v_proj[-2:]])
    rim_rows = shifted(tail_rows, "ctx", 1)
    query_seq = causal_short(q_proj, rim_rows[0], short_filter[0])
    key_seq = causal_short(k_proj, rim_rows[1], short_filter[1])
    value_seq = causal_short(v_proj, rim_rows[2], short_filter[2])
    mixed_in = key_seq * value_seq
    conv_out = channel_conv(mixed_in, filter_spec, devices)
    return query_seq * (conv_out + skip_gain[None, :] * mixed_in)


def split_np(table):
    high = table.astype(BF16)
    low = (table - high.astype(np.float64)).astype(BF16)
    return high, low


@functools.lru_cache(maxsize=None)
def tables(parts, devices, rows):
    outer, seq = 2 * devices, devices * rows
    freq = 2 * seq
    p, s, r = np.arange(devices), np.arange(outer), np.arange(rows)
    chunks = rows * 2 // parts // 64
    low_bit, chunk, part, dev = np.meshgrid(
        np.arange(2), np.arange(chunks), np.arange(parts), np.arange(devices), indexing="ij"
    )
    k = (dev * (2 * rows // outer) + part * (2 * rows // parts // outer) + 2 * chunk + low_bit).ravel()

    def angle(left, right, period):
        return 2.0 * np.pi * (np.outer(left, right) % period) / period

    first = angle(s, p, outer)
    w1h, w1l = split_np(np.concatenate([np.cos(first), -np.sin(first)]))
    w1 = np.concatenate([w1h, w1h, w1l], axis=1)
    last = np.concatenate([np.cos(first.T), -np.sin(first.T)], axis=1) / freq
    w2h, w2l = split_np(last)
    w2 = np.concatenate([w2h, w2h, w2l], axis=1)
    twist = angle(s, r, freq)
    inner = angle(r, k, rows)
    c, d = np.cos(inner), np.sin(inner)
    fore = split_np(np.block([[c, -d], [d, c]]))
    back = split_np(np.block([[c.T, d.T], [-d.T, c.T]]))
    return (w1, w2, np.cos(twist).astype(np.float32), np.sin(twist).astype(np.float32), *fore, *back)


def split(x):
    high = x.astype(BF16)
    return high, (x - high.astype(F32)).astype(BF16)


def dot(a, b):
    return jnp.dot(a, b, preferred_element_type=F32)


def causal(x, rim, taps):
    row = lax.broadcasted_iota(jnp.int32, x.shape, 0)
    one = jnp.where(row == 0, rim[1:2], pltpu.roll(x, 1, 0))
    two = jnp.where(row == 0, rim[0:1], jnp.where(row == 1, rim[1:2], pltpu.roll(x, 2, 0)))
    return taps[0:1] * x + taps[1:2] * one + taps[2:3] * two


def tail_kernel(q_ref, k_ref, v_ref, out_ref, buf, sems):
    rows = q_ref.shape[0]
    copies = [
        pltpu.make_async_copy(ref.at[rows - 8 : rows], buf.at[i], sems.at[i])
        for i, ref in enumerate((q_ref, k_ref, v_ref))
    ]
    for copy in copies:
        copy.start()
    for i, copy in enumerate(copies):
        copy.wait()
        out_ref[2 * i : 2 * i + 2] = buf[i, 6:8]


def spec_kernel(few, chunks, part_ref, spec_ref, out_ref, buf, sems):
    blocks = spec_ref.shape[2] // LANES
    near = LANES // few
    start = pl.multiple_of(part_ref[0] * (64 * chunks), 64 * chunks)
    copies = [
        pltpu.make_async_copy(
            spec_ref.at[:, pl.ds(start + 64 * m, 64), :], buf.at[m], sems.at[m]
        )
        for m in range(chunks)
    ]
    for copy in copies:
        copy.start()
    for m, copy in enumerate(copies):
        copy.wait()
        for i in range(blocks):
            both = buf[m, :, :, LANES * i : LANES * i + LANES].reshape(LANES, LANES)
            out_ref[near * i : near * i + near, few * m : few * m + few, :] = both.T.reshape(near, few, LANES)


def mixed_kernel(few, chunks, k_ref, v_ref, rim_ref, taps_ref, held_ref, out_ref):
    del held_ref
    near = LANES // few
    base = few * chunks
    for i in range(k_ref.shape[1] // LANES):
        col = slice(LANES * i, LANES * i + LANES)
        key_seq = causal(k_ref[:, col], rim_ref[2:4, col], taps_ref[1, :, col])
        value_seq = causal(v_ref[:, col], rim_ref[4:6, col], taps_ref[2, :, col])
        mixed_in = key_seq * value_seq
        for h in range(mixed_in.shape[0] // LANES):
            turned = mixed_in[LANES * h : LANES * h + LANES].T
            at = base + few * h
            out_ref[near * i : near * i + near, at : at + few, :] = turned.reshape(near, few, LANES)


def local_kernel(q_ref, k_ref, v_ref, rim_ref, taps_ref, gain_ref, query_ref, direct_ref):
    for i in range(q_ref.shape[1] // LANES):
        col = slice(LANES * i, LANES * i + LANES)
        query_seq = causal(q_ref[:, col], rim_ref[0:2, col], taps_ref[0, :, col])
        key_seq = causal(k_ref[:, col], rim_ref[2:4, col], taps_ref[1, :, col])
        value_seq = causal(v_ref[:, col], rim_ref[4:6, col], taps_ref[2, :, col])
        query_ref[:, col] = query_seq
        direct_ref[:, col] = query_seq * (gain_ref[:, col] * (key_seq * value_seq))


def gate_kernel(conv_ref, query_ref, direct_ref, out_ref):
    few = conv_ref.shape[1]
    near = LANES // few
    for i in range(conv_ref.shape[0] // near):
        col = slice(LANES * i, LANES * i + LANES)
        for h in range(conv_ref.shape[2] // LANES):
            row = slice(LANES * h, LANES * h + LANES)
            conv = conv_ref[near * i : near * i + near, :, row].reshape(LANES, LANES)
            out_ref[row, col] = query_ref[row, col] * conv.T + direct_ref[row, col]


def conv_kernel(
    parts, few, chunks, in_ref, w1_ref, w2_ref, cos_ref, sin_ref, fh_ref, fl_ref, bh_ref, bl_ref,
    out_ref, yh, yl, ph, pq,
):
    devices = in_ref.shape[0] // parts
    outer = 2 * devices
    rows = out_ref.shape[2]
    base = few * chunks
    cosines, sines = cos_ref[...], sin_ref[...]

    def keep(high_ref, low_ref, at, real, imag):
        for col, x in ((0, real), (rows, imag)):
            high, low = split(x)
            high_ref[at : at + outer, col : col + rows] = high
            low_ref[at : at + outer, col : col + rows] = low

    for c in range(few):
        for q in range(parts):
            block = slice(q * devices, (q + 1) * devices)
            x = jnp.concatenate(
                [in_ref[block, base + few * h + c, :] for h in range(rows // LANES)], axis=1
            )
            high, low = split(x)
            y = dot(w1_ref[...], jnp.concatenate([high, low, high], axis=0))
            re, im = y[:outer], y[outer:]
            keep(yh, yl, (c * parts + q) * outer, re * cosines + im * sines, im * cosines - re * sines)

    group = 4
    step = group * parts * outer
    for g in range(few // group):
        span = slice(g * step, (g + 1) * step)
        spec = dot(yh[span], fh_ref[...]) + dot(yl[span], fh_ref[...]) + dot(yh[span], fl_ref[...])
        for i in range(group):
            c = g * group + i
            resp = jnp.concatenate([in_ref[:, few * m + c, :] for m in range(chunks)], axis=0).T
            h_re = jnp.concatenate([resp[:outer], resp[outer : 2 * outer]], axis=1)
            h_im = jnp.concatenate([resp[2 * outer : 3 * outer], resp[3 * outer :]], axis=1)
            for q in range(parts):
                at = (i * parts + q) * outer
                re, im = spec[at : at + outer, :rows], spec[at : at + outer, rows:]
                keep(ph, pq, g * step + at, re * h_re - im * h_im, re * h_im + im * h_re)
        undo = dot(ph[span], bh_ref[...]) + dot(pq[span], bh_ref[...]) + dot(ph[span], bl_ref[...])
        for i in range(group):
            c = g * group + i
            for q in range(parts):
                at = (i * parts + q) * outer
                re, im = undo[at : at + outer, :rows], undo[at : at + outer, rows:]
                turned = jnp.concatenate([re * cosines - im * sines, im * cosines + re * sines], axis=0)
                high, low = split(turned)
                y = dot(w2_ref[...], jnp.concatenate([high, low, high], axis=0))
                out_ref[q * devices : (q + 1) * devices, c, :] = y


def per_device_tiled(q_proj, k_proj, v_proj, short_filter, skip_gain, filter_spec):
    parts, devices = lax.axis_size("dp"), lax.axis_size("ctx")
    everyone = parts * devices
    rows, channels = q_proj.shape
    few = channels // everyone
    chunks = 2 * rows // parts // 64
    halves = rows // LANES
    depth = few * (chunks + halves)
    outer = 2 * devices
    whole = pl.BlockSpec(memory_space=pltpu.VMEM)

    small = pltpu.CompilerParams(vmem_limit_bytes=16 << 20)
    in_hbm = pl.BlockSpec(memory_space=pltpu.HBM)
    tails = pl.pallas_call(
        tail_kernel,
        out_shape=jax.ShapeDtypeStruct((6, channels), F32),
        in_specs=[in_hbm] * 3,
        out_specs=whole,
        compiler_params=small,
        scratch_shapes=[pltpu.VMEM((3, 8, channels), F32), pltpu.SemaphoreType.DMA((3,))],
    )(q_proj, k_proj, v_proj)
    rim = shifted(tails, "ctx", 1)

    part = lax.axis_index("dp").reshape(1)
    packed = jax.ShapeDtypeStruct((everyone, depth, LANES), F32)
    held = pl.pallas_call(
        functools.partial(spec_kernel, few, chunks),
        out_shape=packed,
        in_specs=[pl.BlockSpec(memory_space=pltpu.SMEM), in_hbm],
        out_specs=whole,
        scratch_shapes=[pltpu.VMEM((chunks, 2, 64, channels), F32), pltpu.SemaphoreType.DMA((chunks,))],
        compiler_params=small,
        cost_estimate=pl.CostEstimate(flops=0, bytes_accessed=1 << 21, transcendentals=0),
    )(part, filter_spec)

    sent = pl.pallas_call(
        functools.partial(mixed_kernel, few, chunks),
        out_shape=packed,
        in_specs=[whole] * 5,
        out_specs=whole,
        input_output_aliases={4: 0},
        compiler_params=small,
        cost_estimate=pl.CostEstimate(flops=0, bytes_accessed=3 << 19, transcendentals=0),
    )(k_proj, v_proj, rim, short_filter, held)

    come = lax.all_to_all(sent, ("dp", "ctx"), 0, 0, tiled=True)

    query_seq, direct = pl.pallas_call(
        local_kernel,
        out_shape=[jax.ShapeDtypeStruct((rows, channels), F32)] * 2,
        in_specs=[whole] * 6,
        out_specs=[whole] * 2,
        compiler_params=small,
        cost_estimate=pl.CostEstimate(flops=0, bytes_accessed=5 << 19, transcendentals=0),
    )(q_proj, k_proj, v_proj, rim, short_filter, skip_gain[None, :])

    total = few * parts * outer
    conv = pl.pallas_call(
        functools.partial(conv_kernel, parts, few, chunks),
        out_shape=jax.ShapeDtypeStruct((everyone, few, rows), F32),
        in_specs=[whole] * 9,
        out_specs=whole,
        scratch_shapes=[pltpu.VMEM((total, 2 * rows), BF16)] * 4,
        compiler_params=small,
        cost_estimate=pl.CostEstimate(flops=0, bytes_accessed=4 << 20, transcendentals=0),
    )(come, *(jnp.asarray(t) for t in tables(parts, devices, rows)))

    back = lax.all_to_all(conv, ("dp", "ctx"), 0, 0, tiled=True)
    return pl.pallas_call(
        gate_kernel,
        out_shape=jax.ShapeDtypeStruct((rows, channels), F32),
        in_specs=[whole] * 3,
        out_specs=whole,
        compiler_params=small,
        cost_estimate=pl.CostEstimate(flops=0, bytes_accessed=1 << 21, transcendentals=0),
    )(back, query_seq, direct)


def fits_tiles(mesh, rows, channels):
    parts, devices = mesh.shape["dp"], mesh.shape["ctx"]
    few, rest = divmod(channels, parts * devices)
    chunks = 2 * rows // parts // 64
    return (
        rest == 0
        and few % 8 == 0
        and 2 * devices == 32
        and rows % LANES == 0
        and parts * devices * chunks == LANES
        and chunks % (rows // LANES) == 0
    )


def solution(mesh):
    placed = (
        P(("dp", "ctx"), None),
        P(("dp", "ctx"), None),
        P(("dp", "ctx"), None),
        P(),
        P(),
        P(None, "ctx", None),
    )

    def per_device(q_proj, *rest):
        form = per_device_tiled if fits_tiles(mesh, *q_proj.shape) else per_device_general
        return form(q_proj, *rest)

    return jax.shard_map(
        per_device, mesh=mesh, in_specs=placed, out_specs=P(("dp", "ctx"), None), check_vma=False
    )
```

```python
import functools
import math

import jax
import jax.numpy as jnp
import numpy as np
from jax import lax
from jax.experimental import pallas as pl
from jax.experimental.pallas import tpu as pltpu
from jax.sharding import PartitionSpec as P

precise_mode = lax.Precision.HIGHEST
LANES = 128
BF16 = jnp.bfloat16
F32 = jnp.float32


def causal_short(signal, rim_rows, tap_gains):
    padded = jnp.concatenate([rim_rows, signal], axis=0)
    return tap_gains[0] * signal + tap_gains[1] * padded[1:-1] + tap_gains[2] * padded[:-2]


def shifted(block, axis, distance):
    devices = range(lax.axis_size(axis))
    route = [(i - distance, i) for i in devices if i - distance in devices]
    return lax.ppermute(block, axis, route)


def channel_conv(mixed_in, filter_spec, devices):
    local_rows = mixed_in.shape[0]
    seq_len = local_rows * devices
    freq_len = 2 * seq_len
    outer_len = 2 * devices
    half_inner = local_rows // 2
    columns = lax.all_to_all(mixed_in, "ctx", split_axis=1, concat_axis=0, tiled=True)
    spec_cols = lax.all_to_all(filter_spec, "ctx", split_axis=2, concat_axis=1, tiled=True)
    few_channels = columns.shape[1]
    grid = columns.reshape(half_inner, outer_len, few_channels)
    row_index = lax.iota(jnp.int32, half_inner)
    inner_freq = lax.iota(jnp.int32, local_rows)
    outer_index = lax.iota(jnp.int32, outer_len)

    def cos_sin(left, right, period):
        turns = (left[:, None] * right[None, :] % period).astype(F32) / period
        return jnp.cos(2.0 * math.pi * turns), jnp.sin(2.0 * math.pi * turns)

    first_cos, first_sin = cos_sin(row_index, inner_freq, local_rows)
    twist_cos, twist_sin = cos_sin(inner_freq, outer_index, freq_len)
    twist_cos, twist_sin = twist_cos[:, :, None], twist_sin[:, :, None]
    last_cos, last_sin = cos_sin(outer_index, outer_index, outer_len)
    dots = functools.partial(jnp.einsum, precision=precise_mode)
    section_re = dots("bk,bac->kac", first_cos, grid)
    section_im = -dots("bk,bac->kac", first_sin, grid)
    turned_re = section_re * twist_cos + section_im * twist_sin
    turned_im = section_im * twist_cos - section_re * twist_sin
    fore = "kac,aj->kjc"
    spec_re = dots(fore, turned_re, last_cos) + dots(fore, turned_im, last_sin)
    spec_im = dots(fore, turned_im, last_cos) - dots(fore, turned_re, last_sin)
    resp = jnp.transpose(spec_cols.reshape(2, outer_len, local_rows, few_channels), (0, 2, 1, 3))
    prod_re = spec_re * resp[0] - spec_im * resp[1]
    prod_im = spec_re * resp[1] + spec_im * resp[0]
    back = "kjc,aj->kac"
    undo_re = dots(back, prod_re, last_cos) - dots(back, prod_im, last_sin)
    undo_im = dots(back, prod_im, last_cos) + dots(back, prod_re, last_sin)
    back_re = undo_re * twist_cos - undo_im * twist_sin
    back_im = undo_im * twist_cos + undo_re * twist_sin
    signal_out = dots("bk,kac->bac", first_cos, back_re) - dots("bk,kac->bac", first_sin, back_im)
    conv_cols = signal_out.reshape(seq_len, few_channels) / freq_len
    return lax.all_to_all(conv_cols, "ctx", split_axis=0, concat_axis=1, tiled=True)


def per_device_general(q_proj, k_proj, v_proj, short_filter, skip_gain, filter_spec):
    devices = lax.axis_size("ctx")
    tail_rows = jnp.stack([q_proj[-2:], k_proj[-2:], v_proj[-2:]])
    rim_rows = shifted(tail_rows, "ctx", 1)
    query_seq = causal_short(q_proj, rim_rows[0], short_filter[0])
    key_seq = causal_short(k_proj, rim_rows[1], short_filter[1])
    value_seq = causal_short(v_proj, rim_rows[2], short_filter[2])
    mixed_in = key_seq * value_seq
    conv_out = channel_conv(mixed_in, filter_spec, devices)
    return query_seq * (conv_out + skip_gain[None, :] * mixed_in)


def split_np(table):
    high = table.astype(BF16)
    low = (table - high.astype(np.float64)).astype(BF16)
    return high, low


@functools.lru_cache(maxsize=None)
def tables(parts, devices, rows):
    outer, seq = 2 * devices, devices * rows
    freq = 2 * seq
    p, s, r = np.arange(devices), np.arange(outer), np.arange(rows)
    chunks = rows * 2 // parts // 64
    low_bit, chunk, part, dev = np.meshgrid(
        np.arange(2), np.arange(chunks), np.arange(parts), np.arange(devices), indexing="ij"
    )
    k = (dev * (2 * rows // outer) + part * (2 * rows // parts // outer) + 2 * chunk + low_bit).ravel()

    def angle(left, right, period):
        return 2.0 * np.pi * (np.outer(left, right) % period) / period

    first = angle(s, p, outer)
    w1h, w1l = split_np(np.concatenate([np.cos(first), -np.sin(first)]))
    w1 = np.concatenate([w1h, w1h, w1l], axis=1)
    last = np.concatenate([np.cos(first.T), -np.sin(first.T)], axis=1) / freq
    w2h, w2l = split_np(last)
    w2 = np.concatenate([w2h, w2h, w2l], axis=1)
    twist = angle(s, r, freq)
    inner = angle(r, k, rows)
    c, d = np.cos(inner), np.sin(inner)
    fore = split_np(np.block([[c, -d], [d, c]]))
    back = split_np(np.block([[c.T, d.T], [-d.T, c.T]]))
    return (w1, w2, np.cos(twist).astype(np.float32), np.sin(twist).astype(np.float32), *fore, *back)


def split(x):
    high = x.astype(BF16)
    return high, (x - high.astype(F32)).astype(BF16)


def dot(a, b):
    return jnp.dot(a, b, preferred_element_type=F32)


def causal(x, rim, taps):
    row = lax.broadcasted_iota(jnp.int32, x.shape, 0)
    one = jnp.where(row == 0, rim[1:2], pltpu.roll(x, 1, 0))
    two = jnp.where(row == 0, rim[0:1], jnp.where(row == 1, rim[1:2], pltpu.roll(x, 2, 0)))
    return taps[0:1] * x + taps[1:2] * one + taps[2:3] * two


def load_kernel(chunks, part_ref, q_ref, k_ref, v_ref, spec_ref, tail_ref, held_ref, buf, sems, held_sem):
    rows = q_ref.shape[0]
    copies = [
        pltpu.make_async_copy(ref.at[rows - 8 : rows], buf.at[i], sems.at[i])
        for i, ref in enumerate((q_ref, k_ref, v_ref))
    ]
    span = 64 * chunks
    start = pl.multiple_of(part_ref[0] * span, span)
    filter_copy = pltpu.make_async_copy(spec_ref.at[:, pl.ds(start, span), :], held_ref, held_sem)
    for copy in copies:
        copy.start()
    filter_copy.start()
    for i, copy in enumerate(copies):
        copy.wait()
        tail_ref[2 * i : 2 * i + 2] = buf[i, 6:8]
    filter_copy.wait()


def spec_kernel(few, spec_ref, out_ref):
    near = LANES // few
    for m in range(spec_ref.shape[1] // 64):
        for i in range(spec_ref.shape[2] // LANES):
            both = spec_ref[:, 64 * m : 64 * m + 64, LANES * i : LANES * i + LANES].reshape(LANES, LANES)
            out_ref[near * i : near * i + near, few * m : few * m + few, :] = both.T.reshape(near, few, LANES)


def mixed_kernel(few, chunks, k_ref, v_ref, rim_ref, taps_ref, held_ref, out_ref):
    del held_ref
    near = LANES // few
    base = few * chunks
    for i in range(k_ref.shape[1] // LANES):
        col = slice(LANES * i, LANES * i + LANES)
        key_seq = causal(k_ref[:, col], rim_ref[2:4, col], taps_ref[1, :, col])
        value_seq = causal(v_ref[:, col], rim_ref[4:6, col], taps_ref[2, :, col])
        mixed_in = key_seq * value_seq
        for h in range(mixed_in.shape[0] // LANES):
            turned = mixed_in[LANES * h : LANES * h + LANES].T
            at = base + few * h
            out_ref[near * i : near * i + near, at : at + few, :] = turned.reshape(near, few, LANES)


def local_kernel(q_ref, k_ref, v_ref, rim_ref, taps_ref, gain_ref, query_ref, direct_ref):
    for i in range(q_ref.shape[1] // LANES):
        col = slice(LANES * i, LANES * i + LANES)
        query_seq = causal(q_ref[:, col], rim_ref[0:2, col], taps_ref[0, :, col])
        key_seq = causal(k_ref[:, col], rim_ref[2:4, col], taps_ref[1, :, col])
        value_seq = causal(v_ref[:, col], rim_ref[4:6, col], taps_ref[2, :, col])
        query_ref[:, col] = query_seq
        direct_ref[:, col] = query_seq * (gain_ref[:, col] * (key_seq * value_seq))


def gate_kernel(conv_ref, query_ref, direct_ref, out_ref):
    few = conv_ref.shape[1]
    near = LANES // few
    for i in range(conv_ref.shape[0] // near):
        col = slice(LANES * i, LANES * i + LANES)
        for h in range(conv_ref.shape[2] // LANES):
            row = slice(LANES * h, LANES * h + LANES)
            conv = conv_ref[near * i : near * i + near, :, row].reshape(LANES, LANES)
            out_ref[row, col] = query_ref[row, col] * conv.T + direct_ref[row, col]


def conv_kernel(
    parts, few, chunks, in_ref, w1_ref, w2_ref, cos_ref, sin_ref, fh_ref, fl_ref, bh_ref, bl_ref,
    out_ref, yh, yl, ph, pq,
):
    devices = in_ref.shape[0] // parts
    outer = 2 * devices
    rows = out_ref.shape[2]
    base = few * chunks
    cosines, sines = cos_ref[...], sin_ref[...]

    def keep(high_ref, low_ref, at, real, imag):
        for col, x in ((0, real), (rows, imag)):
            high, low = split(x)
            high_ref[at : at + outer, col : col + rows] = high
            low_ref[at : at + outer, col : col + rows] = low

    for c in range(few):
        for q in range(parts):
            block = slice(q * devices, (q + 1) * devices)
            x = jnp.concatenate(
                [in_ref[block, base + few * h + c, :] for h in range(rows // LANES)], axis=1
            )
            high, low = split(x)
            y = dot(w1_ref[...], jnp.concatenate([high, low, high], axis=0))
            re, im = y[:outer], y[outer:]
            keep(yh, yl, (c * parts + q) * outer, re * cosines + im * sines, im * cosines - re * sines)

    group = 4
    step = group * parts * outer
    for g in range(few // group):
        span = slice(g * step, (g + 1) * step)
        spec = dot(yh[span], fh_ref[...]) + dot(yl[span], fh_ref[...]) + dot(yh[span], fl_ref[...])
        for i in range(group):
            c = g * group + i
            resp = jnp.concatenate([in_ref[:, few * m + c, :] for m in range(chunks)], axis=0).T
            h_re = jnp.concatenate([resp[:outer], resp[outer : 2 * outer]], axis=1)
            h_im = jnp.concatenate([resp[2 * outer : 3 * outer], resp[3 * outer :]], axis=1)
            for q in range(parts):
                at = (i * parts + q) * outer
                re, im = spec[at : at + outer, :rows], spec[at : at + outer, rows:]
                keep(ph, pq, g * step + at, re * h_re - im * h_im, re * h_im + im * h_re)
        undo = dot(ph[span], bh_ref[...]) + dot(pq[span], bh_ref[...]) + dot(ph[span], bl_ref[...])
        for i in range(group):
            c = g * group + i
            for q in range(parts):
                at = (i * parts + q) * outer
                re, im = undo[at : at + outer, :rows], undo[at : at + outer, rows:]
                turned = jnp.concatenate([re * cosines - im * sines, im * cosines + re * sines], axis=0)
                high, low = split(turned)
                y = dot(w2_ref[...], jnp.concatenate([high, low, high], axis=0))
                out_ref[q * devices : (q + 1) * devices, c, :] = y


def per_device_tiled(q_proj, k_proj, v_proj, short_filter, skip_gain, filter_spec):
    parts, devices = lax.axis_size("dp"), lax.axis_size("ctx")
    everyone = parts * devices
    rows, channels = q_proj.shape
    few = channels // everyone
    chunks = 2 * rows // parts // 64
    halves = rows // LANES
    depth = few * (chunks + halves)
    outer = 2 * devices
    whole = pl.BlockSpec(memory_space=pltpu.VMEM)

    small = pltpu.CompilerParams(vmem_limit_bytes=16 << 20)
    in_hbm = pl.BlockSpec(memory_space=pltpu.HBM)
    part = lax.axis_index("dp").reshape(1)
    kept = [pltpu.with_memory_space_constraint(x, pltpu.HBM) for x in (q_proj, k_proj, v_proj, filter_spec)]
    tails, own_spec = pl.pallas_call(
        functools.partial(load_kernel, chunks),
        out_shape=[
            jax.ShapeDtypeStruct((6, channels), F32),
            jax.ShapeDtypeStruct((2, 64 * chunks, channels), F32),
        ],
        in_specs=[pl.BlockSpec(memory_space=pltpu.SMEM)] + [in_hbm] * 4,
        out_specs=[whole] * 2,
        compiler_params=small,
        scratch_shapes=[
            pltpu.VMEM((3, 8, channels), F32),
            pltpu.SemaphoreType.DMA((3,)),
            pltpu.SemaphoreType.DMA,
        ],
    )(part, *kept)
    rim = shifted(tails, "ctx", 1)

    packed = jax.ShapeDtypeStruct((everyone, depth, LANES), F32)
    held = pl.pallas_call(
        functools.partial(spec_kernel, few),
        out_shape=packed,
        in_specs=[whole],
        out_specs=whole,
        compiler_params=small,
        cost_estimate=pl.CostEstimate(flops=0, bytes_accessed=1 << 21, transcendentals=0),
    )(own_spec)

    sent = pl.pallas_call(
        functools.partial(mixed_kernel, few, chunks),
        out_shape=packed,
        in_specs=[whole] * 5,
        out_specs=whole,
        input_output_aliases={4: 0},
        compiler_params=small,
        cost_estimate=pl.CostEstimate(flops=0, bytes_accessed=3 << 19, transcendentals=0),
    )(k_proj, v_proj, rim, short_filter, held)

    come = lax.all_to_all(sent, ("dp", "ctx"), 0, 0, tiled=True)

    query_seq, direct = pl.pallas_call(
        local_kernel,
        out_shape=[jax.ShapeDtypeStruct((rows, channels), F32)] * 2,
        in_specs=[whole] * 6,
        out_specs=[whole] * 2,
        compiler_params=small,
        cost_estimate=pl.CostEstimate(flops=0, bytes_accessed=5 << 19, transcendentals=0),
    )(q_proj, k_proj, v_proj, rim, short_filter, skip_gain[None, :])

    total = few * parts * outer
    conv = pl.pallas_call(
        functools.partial(conv_kernel, parts, few, chunks),
        out_shape=jax.ShapeDtypeStruct((everyone, few, rows), F32),
        in_specs=[whole] * 9,
        out_specs=whole,
        scratch_shapes=[pltpu.VMEM((total, 2 * rows), BF16)] * 4,
        compiler_params=small,
        cost_estimate=pl.CostEstimate(flops=0, bytes_accessed=4 << 20, transcendentals=0),
    )(come, *(jnp.asarray(t) for t in tables(parts, devices, rows)))

    back = lax.all_to_all(conv, ("dp", "ctx"), 0, 0, tiled=True)
    return pl.pallas_call(
        gate_kernel,
        out_shape=jax.ShapeDtypeStruct((rows, channels), F32),
        in_specs=[whole] * 3,
        out_specs=whole,
        compiler_params=small,
        cost_estimate=pl.CostEstimate(flops=0, bytes_accessed=1 << 21, transcendentals=0),
    )(back, query_seq, direct)


def fits_tiles(mesh, rows, channels):
    parts, devices = mesh.shape["dp"], mesh.shape["ctx"]
    few, rest = divmod(channels, parts * devices)
    chunks = 2 * rows // parts // 64
    return (
        rest == 0
        and few % 8 == 0
        and 2 * devices == 32
        and rows % LANES == 0
        and parts * devices * chunks == LANES
        and chunks % (rows // LANES) == 0
    )


def solution(mesh):
    placed = (
        P(("dp", "ctx"), None),
        P(("dp", "ctx"), None),
        P(("dp", "ctx"), None),
        P(),
        P(),
        P(None, "ctx", None),
    )

    def per_device(q_proj, *rest):
        form = per_device_tiled if fits_tiles(mesh, *q_proj.shape) else per_device_general
        return form(q_proj, *rest)

    return jax.shard_map(
        per_device, mesh=mesh, in_specs=placed, out_specs=P(("dp", "ctx"), None), check_vma=False
    )
```

```python
import functools
import math

import jax
import jax.numpy as jnp
import numpy as np
from jax import lax
from jax.experimental import pallas as pl
from jax.experimental.pallas import tpu as pltpu
from jax.sharding import PartitionSpec as P

precise_mode = lax.Precision.HIGHEST
LANES = 128
BF16 = jnp.bfloat16
F32 = jnp.float32


def causal_short(signal, rim_rows, tap_gains):
    padded = jnp.concatenate([rim_rows, signal], axis=0)
    return tap_gains[0] * signal + tap_gains[1] * padded[1:-1] + tap_gains[2] * padded[:-2]


def shifted(block, axis, distance):
    devices = range(lax.axis_size(axis))
    route = [(i - distance, i) for i in devices if i - distance in devices]
    return lax.ppermute(block, axis, route)


def channel_conv(mixed_in, filter_spec, devices):
    local_rows = mixed_in.shape[0]
    seq_len = local_rows * devices
    freq_len = 2 * seq_len
    outer_len = 2 * devices
    half_inner = local_rows // 2
    columns = lax.all_to_all(mixed_in, "ctx", split_axis=1, concat_axis=0, tiled=True)
    spec_cols = lax.all_to_all(filter_spec, "ctx", split_axis=2, concat_axis=1, tiled=True)
    few_channels = columns.shape[1]
    grid = columns.reshape(half_inner, outer_len, few_channels)
    row_index = lax.iota(jnp.int32, half_inner)
    inner_freq = lax.iota(jnp.int32, local_rows)
    outer_index = lax.iota(jnp.int32, outer_len)

    def cos_sin(left, right, period):
        turns = (left[:, None] * right[None, :] % period).astype(F32) / period
        return jnp.cos(2.0 * math.pi * turns), jnp.sin(2.0 * math.pi * turns)

    first_cos, first_sin = cos_sin(row_index, inner_freq, local_rows)
    twist_cos, twist_sin = cos_sin(inner_freq, outer_index, freq_len)
    twist_cos, twist_sin = twist_cos[:, :, None], twist_sin[:, :, None]
    last_cos, last_sin = cos_sin(outer_index, outer_index, outer_len)
    dots = functools.partial(jnp.einsum, precision=precise_mode)
    section_re = dots("bk,bac->kac", first_cos, grid)
    section_im = -dots("bk,bac->kac", first_sin, grid)
    turned_re = section_re * twist_cos + section_im * twist_sin
    turned_im = section_im * twist_cos - section_re * twist_sin
    fore = "kac,aj->kjc"
    spec_re = dots(fore, turned_re, last_cos) + dots(fore, turned_im, last_sin)
    spec_im = dots(fore, turned_im, last_cos) - dots(fore, turned_re, last_sin)
    resp = jnp.transpose(spec_cols.reshape(2, outer_len, local_rows, few_channels), (0, 2, 1, 3))
    prod_re = spec_re * resp[0] - spec_im * resp[1]
    prod_im = spec_re * resp[1] + spec_im * resp[0]
    back = "kjc,aj->kac"
    undo_re = dots(back, prod_re, last_cos) - dots(back, prod_im, last_sin)
    undo_im = dots(back, prod_im, last_cos) + dots(back, prod_re, last_sin)
    back_re = undo_re * twist_cos - undo_im * twist_sin
    back_im = undo_im * twist_cos + undo_re * twist_sin
    signal_out = dots("bk,kac->bac", first_cos, back_re) - dots("bk,kac->bac", first_sin, back_im)
    conv_cols = signal_out.reshape(seq_len, few_channels) / freq_len
    return lax.all_to_all(conv_cols, "ctx", split_axis=0, concat_axis=1, tiled=True)


def per_device_general(q_proj, k_proj, v_proj, short_filter, skip_gain, filter_spec):
    devices = lax.axis_size("ctx")
    tail_rows = jnp.stack([q_proj[-2:], k_proj[-2:], v_proj[-2:]])
    rim_rows = shifted(tail_rows, "ctx", 1)
    query_seq = causal_short(q_proj, rim_rows[0], short_filter[0])
    key_seq = causal_short(k_proj, rim_rows[1], short_filter[1])
    value_seq = causal_short(v_proj, rim_rows[2], short_filter[2])
    mixed_in = key_seq * value_seq
    conv_out = channel_conv(mixed_in, filter_spec, devices)
    return query_seq * (conv_out + skip_gain[None, :] * mixed_in)


def split_np(table):
    high = table.astype(BF16)
    low = (table - high.astype(np.float64)).astype(BF16)
    return high, low


@functools.lru_cache(maxsize=None)
def tables(parts, devices, rows):
    outer, seq = 2 * devices, devices * rows
    freq = 2 * seq
    chunks = rows * 2 // parts // 64
    low_bit, chunk, part, dev = np.meshgrid(
        np.arange(2), np.arange(chunks), np.arange(parts), np.arange(devices), indexing="ij"
    )
    k = (dev * (2 * rows // outer) + part * (2 * rows // parts // outer) + 2 * chunk + low_bit).ravel()

    def angle(left, right, period):
        return 2.0 * np.pi * (np.outer(left, right) % period) / period

    s, r = np.arange(devices + 1), np.arange(rows)
    twist = angle(s, r, freq)
    weight = np.where((s % 2 == 1) | (s % devices == 0), 2.0, 1.0)[:, None] / (2 * freq)
    turns = [np.cos(twist), np.sin(twist), weight * np.cos(twist), weight * np.sin(twist)]
    inner = angle(r, k, rows)
    c, d = np.cos(inner), np.sin(inner)

    def tripled(table):
        high, low = split_np(table)
        return np.concatenate([high, high, low])

    fore = tripled(np.block([[c, -d], [d, c]]))
    back = tripled(np.block([[c.T, d.T], [-d.T, c.T]]))
    turned = np.eye(LANES)[::-1].astype(BF16)
    return (np.stack(turns).astype(np.float32), fore, back, turned)


def split(x):
    high = x.astype(BF16)
    return high, (x - high.astype(F32)).astype(BF16)


def dot(a, b):
    return jnp.dot(a, b, preferred_element_type=F32)


def plus(a, b):
    return b if a is None else a if b is None else a + b


def minus(a, b):
    return a if b is None else -b if a is None else a - b


def times(a, scale):
    if a is None or abs(scale) < 1e-12:
        return None
    return a if scale == 1.0 else -a if scale == -1.0 else a * scale


def c_add(a, b):
    return plus(a[0], b[0]), plus(a[1], b[1])


def c_sub(a, b):
    return minus(a[0], b[0]), minus(a[1], b[1])


def c_conj(a):
    return a[0], None if a[1] is None else -a[1]


def c_turn(a, turn):
    c, d = math.cos(2 * math.pi * turn), math.sin(2 * math.pi * turn)
    c, d = (float(round(v)) if abs(v - round(v)) < 1e-12 else v for v in (c, d))
    return minus(times(a[0], c), times(a[1], d)), plus(times(a[0], d), times(a[1], c))


def fft_complex(z, sign):
    n = len(z)
    if n == 1:
        return z
    even, odd = fft_complex(z[::2], sign), fft_complex(z[1::2], sign)
    odd = [c_turn(v, sign * t / n) for t, v in enumerate(odd)]
    return [c_add(e, o) for e, o in zip(even, odd)] + [c_sub(e, o) for e, o in zip(even, odd)]


def fft_real(x):
    n = len(x)
    if n == 1:
        return [(x[0], None)]
    half = n // 2
    even, odd = fft_real(x[::2]), fft_real(x[1::2])
    out = [None] * (half + 1)
    for t, (e, o) in enumerate(zip(even, odd)):
        o = c_turn(o, -t / n)
        out[half - t] = c_conj(c_sub(e, o))
        out[t] = c_add(e, o)
    return out


def fft_to_real(z):
    half = len(z) - 1
    n = 2 * half
    if n == 2:
        return [plus(z[0][0], z[1][0]), minus(z[0][0], z[1][0])]
    even, odd = [], []
    for t in range(half // 2 + 1):
        other = c_conj(z[half - t])
        even.append(c_add(z[t], other))
        odd.append(c_turn(c_sub(z[t], other), t / n))
    out = [None] * n
    out[::2], out[1::2] = fft_to_real(even), fft_to_real(odd)
    return out


def spread(x):
    n = len(x)
    turned = [c_turn((v, None), -p / (2 * n)) for p, v in enumerate(x)]
    even, odd = fft_complex(turned[::2], -1), fft_complex(turned[1::2], -1)
    out = [None] * (n + 1)
    out[::2] = fft_real(x)
    out[1::2] = [c_add(e, c_turn(o, -t / n)) for t, (e, o) in enumerate(zip(even, odd))]
    return out


def gather(z):
    n = len(z) - 1
    ends = [(z[0][0], None), *z[2:n:2], (z[n][0], None)]
    even = fft_to_real(ends)
    odd = [None] * n
    odd[::2] = fft_complex(z[1::2], 1)
    odd[1::2] = fft_complex([c_turn(v, t / n) for t, v in enumerate(z[1::2])], 1)
    return [plus(e, c_turn(o, p / (2 * n))[0]) for p, (e, o) in enumerate(zip(even, odd))]


def causal(x, rim, taps):
    row = lax.broadcasted_iota(jnp.int32, x.shape, 0)
    one = jnp.where(row == 0, rim[1:2], pltpu.roll(x, 1, 0))
    two = jnp.where(row == 0, rim[0:1], jnp.where(row == 1, rim[1:2], pltpu.roll(x, 2, 0)))
    return taps[0:1] * x + taps[1:2] * one + taps[2:3] * two


def load_kernel(chunks, part_ref, q_ref, k_ref, v_ref, spec_ref, tail_ref, held_ref, buf, sems, held_sem):
    rows = q_ref.shape[0]
    copies = [
        pltpu.make_async_copy(ref.at[rows - 8 : rows], buf.at[i], sems.at[i])
        for i, ref in enumerate((q_ref, k_ref, v_ref))
    ]
    span = 64 * chunks
    start = pl.multiple_of(part_ref[0] * span, span)
    filter_copy = pltpu.make_async_copy(spec_ref.at[:, pl.ds(start, span), :], held_ref, held_sem)
    for copy in copies:
        copy.start()
    filter_copy.start()
    for i, copy in enumerate(copies):
        copy.wait()
        tail_ref[2 * i : 2 * i + 2] = buf[i, 6:8]
    filter_copy.wait()


def spec_kernel(few, spec_ref, out_ref):
    near = LANES // few
    for m in range(spec_ref.shape[1] // 64):
        for i in range(spec_ref.shape[2] // LANES):
            both = spec_ref[:, 64 * m : 64 * m + 64, LANES * i : LANES * i + LANES].reshape(LANES, LANES)
            out_ref[near * i : near * i + near, few * m : few * m + few, :] = both.T.reshape(near, few, LANES)


def mixed_kernel(few, chunks, k_ref, v_ref, rim_ref, taps_ref, held_ref, out_ref):
    del held_ref
    near = LANES // few
    base = few * chunks
    for i in range(k_ref.shape[1] // LANES):
        col = slice(LANES * i, LANES * i + LANES)
        key_seq = causal(k_ref[:, col], rim_ref[2:4, col], taps_ref[1, :, col])
        value_seq = causal(v_ref[:, col], rim_ref[4:6, col], taps_ref[2, :, col])
        mixed_in = key_seq * value_seq
        for h in range(mixed_in.shape[0] // LANES):
            turned = mixed_in[LANES * h : LANES * h + LANES].T
            at = base + few * h
            out_ref[near * i : near * i + near, at : at + few, :] = turned.reshape(near, few, LANES)


def local_kernel(q_ref, k_ref, v_ref, rim_ref, taps_ref, gain_ref, query_ref, direct_ref):
    for i in range(q_ref.shape[1] // LANES):
        col = slice(LANES * i, LANES * i + LANES)
        query_seq = causal(q_ref[:, col], rim_ref[0:2, col], taps_ref[0, :, col])
        key_seq = causal(k_ref[:, col], rim_ref[2:4, col], taps_ref[1, :, col])
        value_seq = causal(v_ref[:, col], rim_ref[4:6, col], taps_ref[2, :, col])
        query_ref[:, col] = query_seq
        direct_ref[:, col] = query_seq * (gain_ref[:, col] * (key_seq * value_seq))


def gate_kernel(conv_ref, query_ref, direct_ref, out_ref):
    few = conv_ref.shape[1]
    near = LANES // few
    for i in range(conv_ref.shape[0] // near):
        col = slice(LANES * i, LANES * i + LANES)
        for h in range(conv_ref.shape[2] // LANES):
            row = slice(LANES * h, LANES * h + LANES)
            conv = conv_ref[near * i : near * i + near, :, row].reshape(LANES, LANES)
            out_ref[row, col] = query_ref[row, col] * conv.T + direct_ref[row, col]


def conv_kernel(parts, few, chunks, in_ref, turn_ref, fore_ref, back_ref, flip_ref, out_ref, spec, triple, undo):
    devices = in_ref.shape[0] // parts
    outer, rows = 2 * devices, out_ref.shape[2]
    kept = devices + 1
    base = few * chunks
    wide = 2 * rows

    def keep(at, col, value):
        high, low = split(value)
        span = slice(at, at + few)
        for j, part in enumerate((high, low, high)):
            triple[span, wide * j + col : wide * j + col + value.shape[1]] = part

    def row_of(s, q):
        return (s * parts + q) * few

    for c in range(few):
        own = jnp.concatenate([in_ref[:, few * m + c, :] for m in range(chunks)], axis=0)
        spec[:, c, :] = own.T

    for q in range(parts):
        for h in range(rows // LANES):
            lane = slice(LANES * h, LANES * h + LANES)
            at = base + few * h
            x = [in_ref[q * devices + p, at : at + few, :] for p in range(devices)]
            for s, (re, im) in enumerate(spread(x)):
                cosine, sine = turn_ref[0, s : s + 1, lane], turn_ref[1, s : s + 1, lane]
                if im is None:
                    turned = re * cosine, -re * sine
                else:
                    turned = re * cosine + im * sine, im * cosine - re * sine
                keep(row_of(s, q), LANES * h, turned[0])
                keep(row_of(s, q), rows + LANES * h, turned[1])

    other = [[None, None], [None, None]]
    count = outer - kept
    for i in range(2):
        for low_bit in range(2):
            first = (2 * i + low_bit) * outer + kept
            high, low = split(spec[first : first + count].reshape(count * few, LANES))
            other[i][low_bit] = dot(high, flip_ref[...]) + dot(low, flip_ref[...])

    def response(i, s):
        cols = []
        for low_bit in range(2):
            own = spec[(2 * i + low_bit) * outer + s]
            if 0 < s < devices:
                at = (outer - s - kept) * few
                mirror = other[i][1 - low_bit][at : at + few]
                own = own - mirror if i else own + mirror
            cols.append(own)
        return jnp.concatenate(cols, axis=1)

    cuts = (0, kept // 2, kept)
    for begin, end in zip(cuts[:-1], cuts[1:]):
        span = slice(row_of(begin, 0), row_of(end, 0))
        freq = dot(triple[span], fore_ref[...])
        for s in range(begin, end):
            h_re, h_im = response(0, s), response(1, s)
            for q in range(parts):
                at = row_of(s - begin, q)
                re, im = freq[at : at + few, :rows], freq[at : at + few, rows:]
                keep(row_of(s, q), 0, re * h_re - im * h_im)
                keep(row_of(s, q), rows, re * h_im + im * h_re)
        undo[span] = dot(triple[span], back_ref[...])

    for q in range(parts):
        for h in range(rows // LANES):
            lane = slice(LANES * h, LANES * h + LANES)
            z = []
            for s in range(kept):
                at = row_of(s, q)
                re = undo[at : at + few, LANES * h : LANES * h + LANES]
                im = undo[at : at + few, rows + LANES * h : rows + LANES * h + LANES]
                cosine, sine = turn_ref[2, s : s + 1, lane], turn_ref[3, s : s + 1, lane]
                z.append((re * cosine - im * sine, im * cosine + re * sine))
            for p, y in enumerate(gather(z)):
                out_ref[q * devices + p, :, lane] = y


def per_device_tiled(q_proj, k_proj, v_proj, short_filter, skip_gain, filter_spec):
    parts, devices = lax.axis_size("dp"), lax.axis_size("ctx")
    everyone = parts * devices
    rows, channels = q_proj.shape
    few = channels // everyone
    chunks = 2 * rows // parts // 64
    halves = rows // LANES
    depth = few * (chunks + halves)
    outer = 2 * devices
    whole = pl.BlockSpec(memory_space=pltpu.VMEM)

    small = pltpu.CompilerParams(vmem_limit_bytes=16 << 20)
    in_hbm = pl.BlockSpec(memory_space=pltpu.HBM)
    part = lax.axis_index("dp").reshape(1)
    kept = [pltpu.with_memory_space_constraint(x, pltpu.HBM) for x in (q_proj, k_proj, v_proj, filter_spec)]
    tails, own_spec = pl.pallas_call(
        functools.partial(load_kernel, chunks),
        out_shape=[
            jax.ShapeDtypeStruct((6, channels), F32),
            jax.ShapeDtypeStruct((2, 64 * chunks, channels), F32),
        ],
        in_specs=[pl.BlockSpec(memory_space=pltpu.SMEM)] + [in_hbm] * 4,
        out_specs=[whole] * 2,
        compiler_params=small,
        scratch_shapes=[
            pltpu.VMEM((3, 8, channels), F32),
            pltpu.SemaphoreType.DMA((3,)),
            pltpu.SemaphoreType.DMA,
        ],
    )(part, *kept)
    rim = shifted(tails, "ctx", 1)

    packed = jax.ShapeDtypeStruct((everyone, depth, LANES), F32)
    held = pl.pallas_call(
        functools.partial(spec_kernel, few),
        out_shape=packed,
        in_specs=[whole],
        out_specs=whole,
        compiler_params=small,
        cost_estimate=pl.CostEstimate(flops=0, bytes_accessed=1 << 21, transcendentals=0),
    )(own_spec)

    sent = pl.pallas_call(
        functools.partial(mixed_kernel, few, chunks),
        out_shape=packed,
        in_specs=[whole] * 5,
        out_specs=whole,
        input_output_aliases={4: 0},
        compiler_params=small,
        cost_estimate=pl.CostEstimate(flops=0, bytes_accessed=3 << 19, transcendentals=0),
    )(k_proj, v_proj, rim, short_filter, held)

    come = lax.all_to_all(sent, ("dp", "ctx"), 0, 0, tiled=True)

    query_seq, direct = pl.pallas_call(
        local_kernel,
        out_shape=[jax.ShapeDtypeStruct((rows, channels), F32)] * 2,
        in_specs=[whole] * 6,
        out_specs=[whole] * 2,
        compiler_params=small,
        cost_estimate=pl.CostEstimate(flops=0, bytes_accessed=5 << 19, transcendentals=0),
    )(q_proj, k_proj, v_proj, rim, short_filter, skip_gain[None, :])

    total = few * parts * (devices + 1)
    conv = pl.pallas_call(
        functools.partial(conv_kernel, parts, few, chunks),
        out_shape=jax.ShapeDtypeStruct((everyone, few, rows), F32),
        in_specs=[whole] * 5,
        out_specs=whole,
        scratch_shapes=[
            pltpu.VMEM((4 * outer, few, LANES), F32),
            pltpu.VMEM((total, 6 * rows), BF16),
            pltpu.VMEM((total, 2 * rows), F32),
        ],
        compiler_params=small,
        cost_estimate=pl.CostEstimate(flops=0, bytes_accessed=4 << 20, transcendentals=0),
    )(come, *(jnp.asarray(t) for t in tables(parts, devices, rows)))

    back = lax.all_to_all(conv, ("dp", "ctx"), 0, 0, tiled=True)
    return pl.pallas_call(
        gate_kernel,
        out_shape=jax.ShapeDtypeStruct((rows, channels), F32),
        in_specs=[whole] * 3,
        out_specs=whole,
        compiler_params=small,
        cost_estimate=pl.CostEstimate(flops=0, bytes_accessed=1 << 21, transcendentals=0),
    )(back, query_seq, direct)


def fits_tiles(mesh, rows, channels):
    parts, devices = mesh.shape["dp"], mesh.shape["ctx"]
    few, rest = divmod(channels, parts * devices)
    chunks = 2 * rows // parts // 64
    return (
        rest == 0
        and few % 16 == 0
        and devices == 16
        and rows % LANES == 0
        and parts * devices * chunks == LANES
        and chunks % (rows // LANES) == 0
    )


def solution(mesh):
    placed = (
        P(("dp", "ctx"), None),
        P(("dp", "ctx"), None),
        P(("dp", "ctx"), None),
        P(),
        P(),
        P(None, "ctx", None),
    )

    def per_device(q_proj, *rest):
        form = per_device_tiled if fits_tiles(mesh, *q_proj.shape) else per_device_general
        return form(q_proj, *rest)

    return jax.shard_map(
        per_device, mesh=mesh, in_specs=placed, out_specs=P(("dp", "ctx"), None), check_vma=False
    )
```

```python
import functools
import math

import jax
import jax.numpy as jnp
import numpy as np
from jax import lax
from jax.experimental import pallas as pl
from jax.experimental.pallas import tpu as pltpu
from jax.sharding import PartitionSpec as P

precise_mode = lax.Precision.HIGHEST
LANES = 128
BF16 = jnp.bfloat16
F32 = jnp.float32


def causal_short(signal, rim_rows, tap_gains):
    padded = jnp.concatenate([rim_rows, signal], axis=0)
    return tap_gains[0] * signal + tap_gains[1] * padded[1:-1] + tap_gains[2] * padded[:-2]


def shifted(block, axis, distance):
    devices = range(lax.axis_size(axis))
    route = [(i - distance, i) for i in devices if i - distance in devices]
    return lax.ppermute(block, axis, route)


def channel_conv(mixed_in, filter_spec, devices):
    local_rows = mixed_in.shape[0]
    seq_len = local_rows * devices
    freq_len = 2 * seq_len
    outer_len = 2 * devices
    half_inner = local_rows // 2
    columns = lax.all_to_all(mixed_in, "ctx", split_axis=1, concat_axis=0, tiled=True)
    spec_cols = lax.all_to_all(filter_spec, "ctx", split_axis=2, concat_axis=1, tiled=True)
    few_channels = columns.shape[1]
    grid = columns.reshape(half_inner, outer_len, few_channels)
    row_index = lax.iota(jnp.int32, half_inner)
    inner_freq = lax.iota(jnp.int32, local_rows)
    outer_index = lax.iota(jnp.int32, outer_len)

    def cos_sin(left, right, period):
        turns = (left[:, None] * right[None, :] % period).astype(F32) / period
        return jnp.cos(2.0 * math.pi * turns), jnp.sin(2.0 * math.pi * turns)

    first_cos, first_sin = cos_sin(row_index, inner_freq, local_rows)
    twist_cos, twist_sin = cos_sin(inner_freq, outer_index, freq_len)
    twist_cos, twist_sin = twist_cos[:, :, None], twist_sin[:, :, None]
    last_cos, last_sin = cos_sin(outer_index, outer_index, outer_len)
    dots = functools.partial(jnp.einsum, precision=precise_mode)
    section_re = dots("bk,bac->kac", first_cos, grid)
    section_im = -dots("bk,bac->kac", first_sin, grid)
    turned_re = section_re * twist_cos + section_im * twist_sin
    turned_im = section_im * twist_cos - section_re * twist_sin
    fore = "kac,aj->kjc"
    spec_re = dots(fore, turned_re, last_cos) + dots(fore, turned_im, last_sin)
    spec_im = dots(fore, turned_im, last_cos) - dots(fore, turned_re, last_sin)
    resp = jnp.transpose(spec_cols.reshape(2, outer_len, local_rows, few_channels), (0, 2, 1, 3))
    prod_re = spec_re * resp[0] - spec_im * resp[1]
    prod_im = spec_re * resp[1] + spec_im * resp[0]
    back = "kjc,aj->kac"
    undo_re = dots(back, prod_re, last_cos) - dots(back, prod_im, last_sin)
    undo_im = dots(back, prod_im, last_cos) + dots(back, prod_re, last_sin)
    back_re = undo_re * twist_cos - undo_im * twist_sin
    back_im = undo_im * twist_cos + undo_re * twist_sin
    signal_out = dots("bk,kac->bac", first_cos, back_re) - dots("bk,kac->bac", first_sin, back_im)
    conv_cols = signal_out.reshape(seq_len, few_channels) / freq_len
    return lax.all_to_all(conv_cols, "ctx", split_axis=0, concat_axis=1, tiled=True)


def per_device_general(q_proj, k_proj, v_proj, short_filter, skip_gain, filter_spec):
    devices = lax.axis_size("ctx")
    tail_rows = jnp.stack([q_proj[-2:], k_proj[-2:], v_proj[-2:]])
    rim_rows = shifted(tail_rows, "ctx", 1)
    query_seq = causal_short(q_proj, rim_rows[0], short_filter[0])
    key_seq = causal_short(k_proj, rim_rows[1], short_filter[1])
    value_seq = causal_short(v_proj, rim_rows[2], short_filter[2])
    mixed_in = key_seq * value_seq
    conv_out = channel_conv(mixed_in, filter_spec, devices)
    return query_seq * (conv_out + skip_gain[None, :] * mixed_in)


def split_np(table):
    high = table.astype(BF16)
    low = (table - high.astype(np.float64)).astype(BF16)
    return high, low


@functools.lru_cache(maxsize=None)
def tables(parts, devices, rows):
    outer, seq = 2 * devices, devices * rows
    freq = 2 * seq
    chunks = rows * 2 // parts // 64
    low_bit, chunk, part, dev = np.meshgrid(
        np.arange(2), np.arange(chunks), np.arange(parts), np.arange(devices), indexing="ij"
    )
    k = (dev * (2 * rows // outer) + part * (2 * rows // parts // outer) + 2 * chunk + low_bit).ravel()

    def angle(left, right, period):
        return 2.0 * np.pi * (np.outer(left, right) % period) / period

    s, r, half = np.arange(devices + 1), np.arange(rows), rows // 2
    twist = angle(s, r, freq)
    weight = np.where((s % 2 == 1) | (s % devices == 0), 2.0, 1.0)[:, None] / (2 * freq)
    turns = [np.cos(twist), np.sin(twist), weight * np.cos(twist), weight * np.sin(twist)]
    parity = angle([1], r[:half], rows)
    inner = angle(r[:half], k[:half] // 2, half)
    c, d = np.cos(inner), np.sin(inner)

    def tripled(table):
        high, low = split_np(table)
        return np.concatenate([high, high, low])

    fore = tripled(np.block([[c, -d], [d, c]]))
    back = tripled(np.block([[c.T, d.T], [-d.T, c.T]]))
    flip = np.concatenate([np.eye(LANES)[::-1]] * 2).astype(BF16)
    turns = np.stack(turns).astype(np.float32)
    parity = np.concatenate([np.cos(parity), np.sin(parity)]).astype(np.float32)
    return turns, parity, fore, back, flip


def split(x):
    high = x.astype(BF16)
    return high, (x - high.astype(F32)).astype(BF16)


def dot(a, b):
    return jnp.dot(a, b, preferred_element_type=F32)


def plus(a, b):
    return b if a is None else a if b is None else a + b


def minus(a, b):
    return a if b is None else -b if a is None else a - b


def times(a, scale):
    if a is None or abs(scale) < 1e-12:
        return None
    return a if scale == 1.0 else -a if scale == -1.0 else a * scale


def c_add(a, b):
    return plus(a[0], b[0]), plus(a[1], b[1])


def c_sub(a, b):
    return minus(a[0], b[0]), minus(a[1], b[1])


def c_conj(a):
    return a[0], None if a[1] is None else -a[1]


def c_turn(a, turn):
    c, d = math.cos(2 * math.pi * turn), math.sin(2 * math.pi * turn)
    c, d = (float(round(v)) if abs(v - round(v)) < 1e-12 else v for v in (c, d))
    return minus(times(a[0], c), times(a[1], d)), plus(times(a[0], d), times(a[1], c))


def fft_complex(z, sign):
    n = len(z)
    if n == 1:
        return z
    even, odd = fft_complex(z[::2], sign), fft_complex(z[1::2], sign)
    odd = [c_turn(v, sign * t / n) for t, v in enumerate(odd)]
    return [c_add(e, o) for e, o in zip(even, odd)] + [c_sub(e, o) for e, o in zip(even, odd)]


def fft_real(x):
    n = len(x)
    if n == 1:
        return [(x[0], None)]
    half = n // 2
    even, odd = fft_real(x[::2]), fft_real(x[1::2])
    out = [None] * (half + 1)
    for t, (e, o) in enumerate(zip(even, odd)):
        o = c_turn(o, -t / n)
        out[half - t] = c_conj(c_sub(e, o))
        out[t] = c_add(e, o)
    return out


def fft_to_real(z):
    half = len(z) - 1
    n = 2 * half
    if n == 2:
        return [plus(z[0][0], z[1][0]), minus(z[0][0], z[1][0])]
    even, odd = [], []
    for t in range(half // 2 + 1):
        other = c_conj(z[half - t])
        even.append(c_add(z[t], other))
        odd.append(c_turn(c_sub(z[t], other), t / n))
    out = [None] * n
    out[::2], out[1::2] = fft_to_real(even), fft_to_real(odd)
    return out


def spread(x):
    n = len(x)
    turned = [c_turn((v, None), -p / (2 * n)) for p, v in enumerate(x)]
    even, odd = fft_complex(turned[::2], -1), fft_complex(turned[1::2], -1)
    out = [None] * (n + 1)
    out[::2] = fft_real(x)
    out[1::2] = [c_add(e, c_turn(o, -t / n)) for t, (e, o) in enumerate(zip(even, odd))]
    return out


def gather(z):
    n = len(z) - 1
    ends = [(z[0][0], None), *z[2:n:2], (z[n][0], None)]
    even = fft_to_real(ends)
    odd = [None] * n
    odd[::2] = fft_complex(z[1::2], 1)
    odd[1::2] = fft_complex([c_turn(v, t / n) for t, v in enumerate(z[1::2])], 1)
    return [plus(e, c_turn(o, p / (2 * n))[0]) for p, (e, o) in enumerate(zip(even, odd))]


def causal(x, rim, taps):
    row = lax.broadcasted_iota(jnp.int32, x.shape, 0)
    one = jnp.where(row == 0, rim[1:2], pltpu.roll(x, 1, 0))
    two = jnp.where(row == 0, rim[0:1], jnp.where(row == 1, rim[1:2], pltpu.roll(x, 2, 0)))
    return taps[0:1] * x + taps[1:2] * one + taps[2:3] * two


def load_kernel(chunks, part_ref, q_ref, k_ref, v_ref, spec_ref, tail_ref, held_ref, buf, sems, held_sem):
    rows = q_ref.shape[0]
    copies = [
        pltpu.make_async_copy(ref.at[rows - 8 : rows], buf.at[i], sems.at[i])
        for i, ref in enumerate((q_ref, k_ref, v_ref))
    ]
    span = 64 * chunks
    start = pl.multiple_of(part_ref[0] * span, span)
    filter_copy = pltpu.make_async_copy(spec_ref.at[:, pl.ds(start, span), :], held_ref, held_sem)
    for copy in copies:
        copy.start()
    filter_copy.start()
    for i, copy in enumerate(copies):
        copy.wait()
        tail_ref[2 * i : 2 * i + 2] = buf[i, 6:8]
    filter_copy.wait()


def spec_kernel(few, spec_ref, out_ref):
    near = LANES // few
    for m in range(spec_ref.shape[1] // 64):
        for i in range(spec_ref.shape[2] // LANES):
            both = spec_ref[:, 64 * m : 64 * m + 64, LANES * i : LANES * i + LANES].reshape(LANES, LANES)
            out_ref[near * i : near * i + near, few * m : few * m + few, :] = both.T.reshape(near, few, LANES)


def mixed_kernel(few, chunks, k_ref, v_ref, rim_ref, taps_ref, held_ref, out_ref):
    del held_ref
    near = LANES // few
    base = few * chunks
    for i in range(k_ref.shape[1] // LANES):
        col = slice(LANES * i, LANES * i + LANES)
        key_seq = causal(k_ref[:, col], rim_ref[2:4, col], taps_ref[1, :, col])
        value_seq = causal(v_ref[:, col], rim_ref[4:6, col], taps_ref[2, :, col])
        mixed_in = key_seq * value_seq
        for h in range(mixed_in.shape[0] // LANES):
            turned = mixed_in[LANES * h : LANES * h + LANES].T
            at = base + few * h
            out_ref[near * i : near * i + near, at : at + few, :] = turned.reshape(near, few, LANES)


def local_kernel(q_ref, k_ref, v_ref, rim_ref, taps_ref, gain_ref, query_ref, direct_ref):
    for i in range(q_ref.shape[1] // LANES):
        col = slice(LANES * i, LANES * i + LANES)
        query_seq = causal(q_ref[:, col], rim_ref[0:2, col], taps_ref[0, :, col])
        key_seq = causal(k_ref[:, col], rim_ref[2:4, col], taps_ref[1, :, col])
        value_seq = causal(v_ref[:, col], rim_ref[4:6, col], taps_ref[2, :, col])
        query_ref[:, col] = query_seq
        direct_ref[:, col] = query_seq * (gain_ref[:, col] * (key_seq * value_seq))


def gate_kernel(conv_ref, query_ref, direct_ref, out_ref):
    few = conv_ref.shape[1]
    near = LANES // few
    for i in range(conv_ref.shape[0] // near):
        col = slice(LANES * i, LANES * i + LANES)
        for h in range(conv_ref.shape[2] // LANES):
            row = slice(LANES * h, LANES * h + LANES)
            conv = conv_ref[near * i : near * i + near, :, row].reshape(LANES, LANES)
            out_ref[row, col] = query_ref[row, col] * conv.T + direct_ref[row, col]


def conv_kernel(
    parts, few, chunks, in_ref, turn_ref, parity_ref, fore_ref, back_ref, flip_ref, out_ref, spec, triple, freq, undo
):
    devices = in_ref.shape[0] // parts
    outer = 2 * devices
    kept = devices + 1
    base, pitch = few * chunks, few + 1
    left, right = slice(0, LANES), slice(LANES, 2 * LANES)
    odd_cos, odd_sin = parity_ref[0:1], parity_ref[1:2]

    def row_of(low_bit, s, q):
        at = ((low_bit * kept + s) * parts + q) * few
        return slice(at, at + few)

    def keep(span, real, imag):
        for col, value in ((0, real), (LANES, imag)):
            high, low = split(value)
            for j, part in enumerate((high, low, high)):
                at = 2 * LANES * j + col
                triple[span, at : at + LANES] = part

    for q in range(parts):
        tiles = []
        for h in range(2):
            at = base + few * h
            tiles.append(spread([in_ref[q * devices + p, at : at + few, :] for p in range(devices)]))
        for s in range(kept):
            turned = []
            for (re, im), lane in zip((tiles[0][s], tiles[1][s]), (left, right)):
                cosine, sine = turn_ref[0, s : s + 1, lane], turn_ref[1, s : s + 1, lane]
                if im is None:
                    turned.append((re * cosine, -re * sine))
                else:
                    turned.append((re * cosine + im * sine, im * cosine - re * sine))
            keep(row_of(0, s, q), *c_add(*turned))
            re, im = c_sub(*turned)
            keep(row_of(1, s, q), re * odd_cos + im * odd_sin, im * odd_cos - re * odd_sin)

    freq[...] = dot(triple[...], fore_ref[...])

    for c in range(few):
        own = jnp.concatenate([in_ref[:, few * m + c, :] for m in range(chunks)], axis=0)
        spec[pl.ds(c, 4 * outer, stride=pitch), :] = own.T

    other = [[None, None], [None, None]]
    count = outer - kept
    for i in range(2):
        for low_bit in range(2):
            first = (2 * i + low_bit) * outer + kept
            pair = split(spec[first * pitch : (first + count) * pitch])
            other[i][low_bit] = dot(jnp.concatenate(pair, axis=1), flip_ref[...])

    def response(i, low_bit, s):
        at = ((2 * i + low_bit) * outer + s) * pitch
        own = spec[at : at + few]
        if 0 < s < devices:
            at = (outer - s - kept) * pitch
            mirror = other[i][1 - low_bit][at : at + few]
            own = own - mirror if i else own + mirror
        return own

    for low_bit in range(2):
        for s in range(kept):
            h_re, h_im = response(0, low_bit, s), response(1, low_bit, s)
            for q in range(parts):
                span = row_of(low_bit, s, q)
                re, im = freq[span, left], freq[span, right]
                keep(span, re * h_re - im * h_im, re * h_im + im * h_re)

    undo[...] = dot(triple[...], back_ref[...])

    for q in range(parts):
        tiles = [], []
        for s in range(kept):
            even, odd = row_of(0, s, q), row_of(1, s, q)
            base_value = undo[even, left], undo[even, right]
            re, im = undo[odd, left], undo[odd, right]
            odd_value = re * odd_cos - im * odd_sin, im * odd_cos + re * odd_sin
            both = c_add(base_value, odd_value), c_sub(base_value, odd_value)
            for tile, (re, im), lane in zip(tiles, both, (left, right)):
                cosine, sine = turn_ref[2, s : s + 1, lane], turn_ref[3, s : s + 1, lane]
                tile.append((re * cosine - im * sine, im * cosine + re * sine))
        for tile, lane in zip(tiles, (left, right)):
            for p, y in enumerate(gather(tile)):
                out_ref[q * devices + p, :, lane] = y


def per_device_tiled(q_proj, k_proj, v_proj, short_filter, skip_gain, filter_spec):
    parts, devices = lax.axis_size("dp"), lax.axis_size("ctx")
    everyone = parts * devices
    rows, channels = q_proj.shape
    few = channels // everyone
    chunks = 2 * rows // parts // 64
    halves = rows // LANES
    depth = few * (chunks + halves)
    outer = 2 * devices
    whole = pl.BlockSpec(memory_space=pltpu.VMEM)

    small = pltpu.CompilerParams(vmem_limit_bytes=16 << 20)
    in_hbm = pl.BlockSpec(memory_space=pltpu.HBM)
    part = lax.axis_index("dp").reshape(1)
    kept = [pltpu.with_memory_space_constraint(x, pltpu.HBM) for x in (q_proj, k_proj, v_proj, filter_spec)]
    tails, own_spec = pl.pallas_call(
        functools.partial(load_kernel, chunks),
        out_shape=[
            jax.ShapeDtypeStruct((6, channels), F32),
            jax.ShapeDtypeStruct((2, 64 * chunks, channels), F32),
        ],
        in_specs=[pl.BlockSpec(memory_space=pltpu.SMEM)] + [in_hbm] * 4,
        out_specs=[whole] * 2,
        compiler_params=small,
        scratch_shapes=[
            pltpu.VMEM((3, 8, channels), F32),
            pltpu.SemaphoreType.DMA((3,)),
            pltpu.SemaphoreType.DMA,
        ],
    )(part, *kept)
    rim = shifted(tails, "ctx", 1)

    packed = jax.ShapeDtypeStruct((everyone, depth, LANES), F32)
    held = pl.pallas_call(
        functools.partial(spec_kernel, few),
        out_shape=packed,
        in_specs=[whole],
        out_specs=whole,
        compiler_params=small,
        cost_estimate=pl.CostEstimate(flops=0, bytes_accessed=1 << 21, transcendentals=0),
    )(own_spec)

    sent = pl.pallas_call(
        functools.partial(mixed_kernel, few, chunks),
        out_shape=packed,
        in_specs=[whole] * 5,
        out_specs=whole,
        input_output_aliases={4: 0},
        compiler_params=small,
        cost_estimate=pl.CostEstimate(flops=0, bytes_accessed=3 << 19, transcendentals=0),
    )(k_proj, v_proj, rim, short_filter, held)

    come = lax.all_to_all(sent, ("dp", "ctx"), 0, 0, tiled=True)

    query_seq, direct = pl.pallas_call(
        local_kernel,
        out_shape=[jax.ShapeDtypeStruct((rows, channels), F32)] * 2,
        in_specs=[whole] * 6,
        out_specs=[whole] * 2,
        compiler_params=small,
        cost_estimate=pl.CostEstimate(flops=0, bytes_accessed=5 << 19, transcendentals=0),
    )(q_proj, k_proj, v_proj, rim, short_filter, skip_gain[None, :])

    total = 2 * few * parts * (devices + 1)
    conv = pl.pallas_call(
        functools.partial(conv_kernel, parts, few, chunks),
        out_shape=jax.ShapeDtypeStruct((everyone, few, rows), F32),
        in_specs=[whole] * 6,
        out_specs=whole,
        scratch_shapes=[
            pltpu.VMEM((4 * outer * (few + 1), LANES), F32),
            pltpu.VMEM((total, 6 * LANES), BF16),
            pltpu.VMEM((total, 2 * LANES), F32),
            pltpu.VMEM((total, 2 * LANES), F32),
        ],
        compiler_params=small,
        cost_estimate=pl.CostEstimate(flops=0, bytes_accessed=4 << 20, transcendentals=0),
    )(come, *(jnp.asarray(t) for t in tables(parts, devices, rows)))

    back = lax.all_to_all(conv, ("dp", "ctx"), 0, 0, tiled=True)
    return pl.pallas_call(
        gate_kernel,
        out_shape=jax.ShapeDtypeStruct((rows, channels), F32),
        in_specs=[whole] * 3,
        out_specs=whole,
        compiler_params=small,
        cost_estimate=pl.CostEstimate(flops=0, bytes_accessed=1 << 21, transcendentals=0),
    )(back, query_seq, direct)


def fits_tiles(mesh, rows, channels):
    parts, devices = mesh.shape["dp"], mesh.shape["ctx"]
    few, rest = divmod(channels, parts * devices)
    chunks = 2 * rows // parts // 64
    return (
        rest == 0
        and few % 16 == 0
        and devices == 16
        and rows == 2 * LANES
        and parts * devices * chunks == LANES
        and chunks % 2 == 0
    )


def solution(mesh):
    placed = (
        P(("dp", "ctx"), None),
        P(("dp", "ctx"), None),
        P(("dp", "ctx"), None),
        P(),
        P(),
        P(None, "ctx", None),
    )

    def per_device(q_proj, *rest):
        form = per_device_tiled if fits_tiles(mesh, *q_proj.shape) else per_device_general
        return form(q_proj, *rest)

    return jax.shard_map(
        per_device, mesh=mesh, in_specs=placed, out_specs=P(("dp", "ctx"), None), check_vma=False
    )
```

```python
import functools
import math

import jax
import jax.numpy as jnp
import numpy as np
from jax import lax
from jax.experimental import pallas as pl
from jax.experimental.pallas import tpu as pltpu
from jax.sharding import PartitionSpec as P

precise_mode = lax.Precision.HIGHEST
LANES = 128
BF16 = jnp.bfloat16
F32 = jnp.float32


def causal_short(signal, rim_rows, tap_gains):
    padded = jnp.concatenate([rim_rows, signal], axis=0)
    return tap_gains[0] * signal + tap_gains[1] * padded[1:-1] + tap_gains[2] * padded[:-2]


def shifted(block, axis, distance):
    devices = range(lax.axis_size(axis))
    route = [(i - distance, i) for i in devices if i - distance in devices]
    return lax.ppermute(block, axis, route)


def channel_conv(mixed_in, filter_spec, devices):
    local_rows = mixed_in.shape[0]
    seq_len = local_rows * devices
    freq_len = 2 * seq_len
    outer_len = 2 * devices
    half_inner = local_rows // 2
    columns = lax.all_to_all(mixed_in, "ctx", split_axis=1, concat_axis=0, tiled=True)
    spec_cols = lax.all_to_all(filter_spec, "ctx", split_axis=2, concat_axis=1, tiled=True)
    few_channels = columns.shape[1]
    grid = columns.reshape(half_inner, outer_len, few_channels)
    row_index = lax.iota(jnp.int32, half_inner)
    inner_freq = lax.iota(jnp.int32, local_rows)
    outer_index = lax.iota(jnp.int32, outer_len)

    def cos_sin(left, right, period):
        turns = (left[:, None] * right[None, :] % period).astype(F32) / period
        return jnp.cos(2.0 * math.pi * turns), jnp.sin(2.0 * math.pi * turns)

    first_cos, first_sin = cos_sin(row_index, inner_freq, local_rows)
    twist_cos, twist_sin = cos_sin(inner_freq, outer_index, freq_len)
    twist_cos, twist_sin = twist_cos[:, :, None], twist_sin[:, :, None]
    last_cos, last_sin = cos_sin(outer_index, outer_index, outer_len)
    dots = functools.partial(jnp.einsum, precision=precise_mode)
    section_re = dots("bk,bac->kac", first_cos, grid)
    section_im = -dots("bk,bac->kac", first_sin, grid)
    turned_re = section_re * twist_cos + section_im * twist_sin
    turned_im = section_im * twist_cos - section_re * twist_sin
    fore = "kac,aj->kjc"
    spec_re = dots(fore, turned_re, last_cos) + dots(fore, turned_im, last_sin)
    spec_im = dots(fore, turned_im, last_cos) - dots(fore, turned_re, last_sin)
    resp = jnp.transpose(spec_cols.reshape(2, outer_len, local_rows, few_channels), (0, 2, 1, 3))
    prod_re = spec_re * resp[0] - spec_im * resp[1]
    prod_im = spec_re * resp[1] + spec_im * resp[0]
    back = "kjc,aj->kac"
    undo_re = dots(back, prod_re, last_cos) - dots(back, prod_im, last_sin)
    undo_im = dots(back, prod_im, last_cos) + dots(back, prod_re, last_sin)
    back_re = undo_re * twist_cos - undo_im * twist_sin
    back_im = undo_im * twist_cos + undo_re * twist_sin
    signal_out = dots("bk,kac->bac", first_cos, back_re) - dots("bk,kac->bac", first_sin, back_im)
    conv_cols = signal_out.reshape(seq_len, few_channels) / freq_len
    return lax.all_to_all(conv_cols, "ctx", split_axis=0, concat_axis=1, tiled=True)


def per_device_general(q_proj, k_proj, v_proj, short_filter, skip_gain, filter_spec):
    devices = lax.axis_size("ctx")
    tail_rows = jnp.stack([q_proj[-2:], k_proj[-2:], v_proj[-2:]])
    rim_rows = shifted(tail_rows, "ctx", 1)
    query_seq = causal_short(q_proj, rim_rows[0], short_filter[0])
    key_seq = causal_short(k_proj, rim_rows[1], short_filter[1])
    value_seq = causal_short(v_proj, rim_rows[2], short_filter[2])
    mixed_in = key_seq * value_seq
    conv_out = channel_conv(mixed_in, filter_spec, devices)
    return query_seq * (conv_out + skip_gain[None, :] * mixed_in)


def split_np(table):
    high = table.astype(BF16)
    low = (table - high.astype(np.float64)).astype(BF16)
    return high, low


@functools.lru_cache(maxsize=None)
def tables(parts, devices, rows):
    outer, seq = 2 * devices, devices * rows
    freq = 2 * seq
    chunks = rows * 2 // parts // 64
    low_bit, chunk, part, dev = np.meshgrid(
        np.arange(2), np.arange(chunks), np.arange(parts), np.arange(devices), indexing="ij"
    )
    k = (dev * (2 * rows // outer) + part * (2 * rows // parts // outer) + 2 * chunk + low_bit).ravel()

    def angle(left, right, period):
        return 2.0 * np.pi * (np.outer(left, right) % period) / period

    s, r, half = np.arange(devices + 1), np.arange(rows), rows // 2
    twist = angle(s, r, freq)
    weight = np.where((s % 2 == 1) | (s % devices == 0), 2.0, 1.0)[:, None] / (2 * freq)
    turns = [np.cos(twist), np.sin(twist), weight * np.cos(twist), weight * np.sin(twist)]
    parity = angle([1], r[:half], rows)
    inner = angle(r[:half], k[:half] // 2, half)
    c, d = np.cos(inner), np.sin(inner)

    def tripled(table):
        high, low = split_np(table)
        return np.concatenate([high, high, low])

    fore = tripled(np.block([[c, -d], [d, c]]))
    back = tripled(np.block([[c.T, d.T], [-d.T, c.T]]))
    flip = np.concatenate([np.eye(LANES)[::-1]] * 2).astype(BF16)
    turns = np.stack(turns).astype(np.float32)
    parity = np.concatenate([np.cos(parity), np.sin(parity)]).astype(np.float32)
    return turns, parity, fore, back, flip


def split(x):
    high = x.astype(BF16)
    return high, (x - high.astype(F32)).astype(BF16)


def dot(a, b):
    return jnp.dot(a, b, preferred_element_type=F32)


def plus(a, b):
    return b if a is None else a if b is None else a + b


def minus(a, b):
    return a if b is None else -b if a is None else a - b


def times(a, scale):
    if a is None or abs(scale) < 1e-12:
        return None
    return a if scale == 1.0 else -a if scale == -1.0 else a * scale


def c_add(a, b):
    return plus(a[0], b[0]), plus(a[1], b[1])


def c_sub(a, b):
    return minus(a[0], b[0]), minus(a[1], b[1])


def c_conj(a):
    return a[0], None if a[1] is None else -a[1]


def c_turn(a, turn):
    c, d = math.cos(2 * math.pi * turn), math.sin(2 * math.pi * turn)
    c, d = (float(round(v)) if abs(v - round(v)) < 1e-12 else v for v in (c, d))
    return minus(times(a[0], c), times(a[1], d)), plus(times(a[0], d), times(a[1], c))


def fft_complex(z, sign):
    n = len(z)
    if n == 1:
        return z
    even, odd = fft_complex(z[::2], sign), fft_complex(z[1::2], sign)
    odd = [c_turn(v, sign * t / n) for t, v in enumerate(odd)]
    return [c_add(e, o) for e, o in zip(even, odd)] + [c_sub(e, o) for e, o in zip(even, odd)]


def fft_real(x):
    n = len(x)
    if n == 1:
        return [(x[0], None)]
    half = n // 2
    even, odd = fft_real(x[::2]), fft_real(x[1::2])
    out = [None] * (half + 1)
    for t, (e, o) in enumerate(zip(even, odd)):
        o = c_turn(o, -t / n)
        out[half - t] = c_conj(c_sub(e, o))
        out[t] = c_add(e, o)
    return out


def fft_to_real(z):
    half = len(z) - 1
    n = 2 * half
    if n == 2:
        return [plus(z[0][0], z[1][0]), minus(z[0][0], z[1][0])]
    even, odd = [], []
    for t in range(half // 2 + 1):
        other = c_conj(z[half - t])
        even.append(c_add(z[t], other))
        odd.append(c_turn(c_sub(z[t], other), t / n))
    out = [None] * n
    out[::2], out[1::2] = fft_to_real(even), fft_to_real(odd)
    return out


def spread(x):
    n = len(x)
    turned = [c_turn((v, None), -p / (2 * n)) for p, v in enumerate(x)]
    even, odd = fft_complex(turned[::2], -1), fft_complex(turned[1::2], -1)
    out = [None] * (n + 1)
    out[::2] = fft_real(x)
    out[1::2] = [c_add(e, c_turn(o, -t / n)) for t, (e, o) in enumerate(zip(even, odd))]
    return out


def gather(z):
    n = len(z) - 1
    ends = [(z[0][0], None), *z[2:n:2], (z[n][0], None)]
    even = fft_to_real(ends)
    odd = [None] * n
    odd[::2] = fft_complex(z[1::2], 1)
    odd[1::2] = fft_complex([c_turn(v, t / n) for t, v in enumerate(z[1::2])], 1)
    return [plus(e, c_turn(o, p / (2 * n))[0]) for p, (e, o) in enumerate(zip(even, odd))]


def causal(x, taps):
    return taps[0:1] * x + taps[1:2] * pltpu.roll(x, 1, 0) + taps[2:3] * pltpu.roll(x, 2, 0)


def block_turn(x, few):
    row = lax.broadcasted_iota(jnp.int32, x.shape, 0)
    block = lax.broadcasted_iota(jnp.int32, x.shape, 1) // few
    out = x
    for d in range(1, 8):
        moved = pltpu.roll(pltpu.roll(x, LANES - few * d, 1), d, 0)
        out = jnp.where((row - block + 8) % 8 == d, moved, out)
    return out


def pack_kernel(
    few, chunks, part_ref, q_ref, k_ref, v_ref, taps_ref, gain_ref, spec_ref,
    out_ref, ends, keys, values, taps, gain, held, sems, held_sems,
):
    rows = q_ref.shape[0]
    near = LANES // few
    start = pl.multiple_of(part_ref[0] * (64 * chunks), 64 * chunks)
    small = [
        pltpu.make_async_copy(src, dst, sems.at[i])
        for i, (src, dst) in enumerate(
            (
                (taps_ref, taps),
                (gain_ref, gain),
                (q_ref.at[0:8], ends.at[0:8]),
                (q_ref.at[rows - 8 : rows], ends.at[8:16]),
                (k_ref, keys),
                (v_ref, values),
            )
        )
    ]
    large = [
        pltpu.make_async_copy(spec_ref.at[:, pl.ds(start + 64 * m, 64), :], held.at[m], held_sems.at[m])
        for m in range(chunks)
    ]
    for copy in small + large:
        copy.start()
    for copy in small:
        copy.wait()
    blocks = k_ref.shape[1] // LANES
    base = few * chunks
    for i in range(blocks):
        col = slice(LANES * i, LANES * i + LANES)
        dests = slice(near * i, near * i + near)
        mixed_in = causal(keys[:, col], taps[1, :, col]) * causal(values[:, col], taps[2, :, col])
        for h in range(rows // LANES):
            turned = mixed_in[LANES * h : LANES * h + LANES].T
            at = base + few * h
            out_ref[dests, at : at + few, :] = turned.reshape(near, few, LANES)

        def known(first, last, j):
            t0, t1, t2 = taps[j, 0:1, col], taps[j, 1:2, col], taps[j, 2:3, col]
            own = t0 * first[0:1], t0 * first[1:2] + t1 * first[0:1]
            following = t1 * last[1:2] + t2 * last[0:1], t2 * last[1:2]
            return *own, *following

        k0, k1, next_k0, next_k1 = known(keys[0:2, col], keys[rows - 2 : rows, col], 1)
        v0, v1, next_v0, next_v1 = known(values[0:2, col], values[rows - 2 : rows, col], 2)
        q0, q1, next_q0, next_q1 = known(ends[0:2, col], ends[14:16, col], 0)
        nothing = jnp.zeros_like(q0)
        at = base + few * (rows // LANES)
        pairs = jnp.concatenate([k0, v0, k1, v1, next_k0, next_v0, next_k1, next_v1], axis=0)
        others = [q0, q1, next_q0, next_q1, gain[:, col], nothing, nothing, nothing]
        out_ref[dests, at, :] = block_turn(pairs, few)
        out_ref[dests, at + 1, :] = block_turn(jnp.concatenate(others, axis=0), few)
        for j in range(2, 8):
            out_ref[dests, at + j, :] = jnp.zeros((near, LANES), F32)
    for m, copy in enumerate(large):
        copy.wait()
        for i in range(blocks):
            both = held[m, :, :, LANES * i : LANES * i + LANES].reshape(LANES, LANES)
            out_ref[near * i : near * i + near, few * m : few * m + few, :] = both.T.reshape(near, few, LANES)


def local_kernel(q_ref, k_ref, v_ref, taps_ref, gain_ref, query_ref, direct_ref):
    for i in range(q_ref.shape[1] // LANES):
        col = slice(LANES * i, LANES * i + LANES)
        query_seq = causal(q_ref[:, col], taps_ref[0, :, col])
        key_seq = causal(k_ref[:, col], taps_ref[1, :, col])
        value_seq = causal(v_ref[:, col], taps_ref[2, :, col])
        direct = query_seq * (gain_ref[:, col] * (key_seq * value_seq))
        row = lax.broadcasted_iota(jnp.int32, direct.shape, 0)
        query_ref[:, col] = jnp.where(row < 2, 1.0, query_seq)
        direct_ref[:, col] = jnp.where(row < 2, 0.0, direct)


def gate_kernel(conv_ref, query_ref, direct_ref, out_ref):
    few = conv_ref.shape[1]
    near = LANES // few
    for i in range(conv_ref.shape[0] // near):
        col = slice(LANES * i, LANES * i + LANES)
        for h in range(conv_ref.shape[2] // LANES):
            row = slice(LANES * h, LANES * h + LANES)
            conv = conv_ref[near * i : near * i + near, :, row].reshape(LANES, LANES)
            out_ref[row, col] = query_ref[row, col] * conv.T + direct_ref[row, col]


def conv_kernel(
    parts, few, chunks, in_ref, turn_ref, parity_ref, fore_ref, back_ref, flip_ref, out_ref, spec, triple, freq, undo
):
    devices = in_ref.shape[0] // parts
    outer = 2 * devices
    kept = devices + 1
    base, pitch = few * chunks, few + 1
    left, right = slice(0, LANES), slice(LANES, 2 * LANES)
    lane_of = lax.broadcasted_iota(jnp.int32, (few, LANES), 1)

    everyone = in_ref.shape[0]
    begins = lax.broadcasted_iota(jnp.int32, (everyone, LANES), 0) % devices == 0
    pairs, others = in_ref[:, base + 2 * few, :], in_ref[:, base + 2 * few + 1, :]

    def before(x, lanes):
        moved = pltpu.roll(pltpu.roll(x, 1, 0), LANES - lanes, 1)
        return jnp.where(begins, 0.0, moved)

    pairs = pairs + before(pairs, 4 * few)
    query = others + before(others, 2 * few)
    mixed = pairs * pltpu.roll(pairs, LANES - few, 1)
    gain = pltpu.roll(others, LANES - 4 * few, 1)
    mixed_second = pltpu.roll(mixed, LANES - 2 * few, 1)
    query_second = pltpu.roll(query, LANES - few, 1)
    ends = [mixed, mixed_second, query, query_second, query * gain * mixed, query_second * gain * mixed_second]
    ends = [x.T[:few] for x in ends]

    def first_lanes(pair, at):
        first, second = (x[:, at : at + 1] for x in pair)
        return jnp.where(lane_of == 0, first, second)

    odd_cos, odd_sin = parity_ref[0:1], parity_ref[1:2]

    def row_of(low_bit, s, q):
        at = ((low_bit * kept + s) * parts + q) * few
        return slice(at, at + few)

    def keep(span, real, imag):
        for col, value in ((0, real), (LANES, imag)):
            high, low = split(value)
            for j, part in enumerate((high, low, high)):
                at = 2 * LANES * j + col
                triple[span, at : at + LANES] = part

    for q in range(parts):
        tiles = []
        for h in range(2):
            at = base + few * h
            x = [in_ref[q * devices + p, at : at + few, :] for p in range(devices)]
            if h == 0:
                x = [
                    jnp.where(lane_of < 2, first_lanes(ends[:2], q * devices + p), own)
                    for p, own in enumerate(x)
                ]
            tiles.append(spread(x))
        for s in range(kept):
            turned = []
            for (re, im), lane in zip((tiles[0][s], tiles[1][s]), (left, right)):
                cosine, sine = turn_ref[0, s : s + 1, lane], turn_ref[1, s : s + 1, lane]
                if im is None:
                    turned.append((re * cosine, -re * sine))
                else:
                    turned.append((re * cosine + im * sine, im * cosine - re * sine))
            keep(row_of(0, s, q), *c_add(*turned))
            re, im = c_sub(*turned)
            keep(row_of(1, s, q), re * odd_cos + im * odd_sin, im * odd_cos - re * odd_sin)

    freq[...] = dot(triple[...], fore_ref[...])

    for c in range(few):
        own = jnp.concatenate([in_ref[:, few * m + c, :] for m in range(chunks)], axis=0)
        spec[pl.ds(c, 4 * outer, stride=pitch), :] = own.T

    other = [[None, None], [None, None]]
    count = outer - kept
    for i in range(2):
        for low_bit in range(2):
            first = (2 * i + low_bit) * outer + kept
            pair = split(spec[first * pitch : (first + count) * pitch])
            other[i][low_bit] = dot(jnp.concatenate(pair, axis=1), flip_ref[...])

    def response(i, low_bit, s):
        at = ((2 * i + low_bit) * outer + s) * pitch
        own = spec[at : at + few]
        if 0 < s < devices:
            at = (outer - s - kept) * pitch
            mirror = other[i][1 - low_bit][at : at + few]
            own = own - mirror if i else own + mirror
        return own

    for low_bit in range(2):
        for s in range(kept):
            h_re, h_im = response(0, low_bit, s), response(1, low_bit, s)
            for q in range(parts):
                span = row_of(low_bit, s, q)
                re, im = freq[span, left], freq[span, right]
                keep(span, re * h_re - im * h_im, re * h_im + im * h_re)

    undo[...] = dot(triple[...], back_ref[...])

    for q in range(parts):
        tiles = [], []
        for s in range(kept):
            even, odd = row_of(0, s, q), row_of(1, s, q)
            base_value = undo[even, left], undo[even, right]
            re, im = undo[odd, left], undo[odd, right]
            odd_value = re * odd_cos - im * odd_sin, im * odd_cos + re * odd_sin
            both = c_add(base_value, odd_value), c_sub(base_value, odd_value)
            for tile, (re, im), lane in zip(tiles, both, (left, right)):
                cosine, sine = turn_ref[2, s : s + 1, lane], turn_ref[3, s : s + 1, lane]
                tile.append((re * cosine - im * sine, im * cosine + re * sine))
        for tile, lane in zip(tiles, (left, right)):
            for p, y in enumerate(gather(tile)):
                at = q * devices + p
                if lane == left:
                    finished = first_lanes(ends[2:4], at) * y + first_lanes(ends[4:], at)
                    y = jnp.where(lane_of < 2, finished, y)
                out_ref[at, :, lane] = y


def per_device_tiled(q_proj, k_proj, v_proj, short_filter, skip_gain, filter_spec):
    parts, devices = lax.axis_size("dp"), lax.axis_size("ctx")
    everyone = parts * devices
    rows, channels = q_proj.shape
    few = channels // everyone
    chunks = 2 * rows // parts // 64
    halves = rows // LANES
    depth = few * (chunks + halves) + 8
    outer = 2 * devices
    whole = pl.BlockSpec(memory_space=pltpu.VMEM)
    in_hbm = pl.BlockSpec(memory_space=pltpu.HBM)
    small = pltpu.CompilerParams(vmem_limit_bytes=16 << 20)
    gain_row = skip_gain[None, :]

    part = lax.axis_index("dp").reshape(1)
    sources = (q_proj, k_proj, v_proj, short_filter, gain_row, filter_spec)
    sent = pl.pallas_call(
        functools.partial(pack_kernel, few, chunks),
        out_shape=jax.ShapeDtypeStruct((everyone, depth, LANES), F32),
        in_specs=[pl.BlockSpec(memory_space=pltpu.SMEM)] + [in_hbm] * 6,
        out_specs=whole,
        compiler_params=small,
        scratch_shapes=[
            pltpu.VMEM((16, channels), F32),
            pltpu.VMEM((rows, channels), F32),
            pltpu.VMEM((rows, channels), F32),
            pltpu.VMEM((3, 3, channels), F32),
            pltpu.VMEM((1, channels), F32),
            pltpu.VMEM((chunks, 2, 64, channels), F32),
            pltpu.SemaphoreType.DMA((6,)),
            pltpu.SemaphoreType.DMA((chunks,)),
        ],
        cost_estimate=pl.CostEstimate(flops=0, bytes_accessed=1 << 22, transcendentals=0),
    )(part, *(pltpu.with_memory_space_constraint(x, pltpu.HBM) for x in sources))

    come = lax.all_to_all(sent, ("dp", "ctx"), 0, 0, tiled=True)

    query_seq, direct = pl.pallas_call(
        local_kernel,
        out_shape=[jax.ShapeDtypeStruct((rows, channels), F32)] * 2,
        in_specs=[whole] * 5,
        out_specs=[whole] * 2,
        compiler_params=small,
        cost_estimate=pl.CostEstimate(flops=0, bytes_accessed=5 << 19, transcendentals=0),
    )(q_proj, k_proj, v_proj, short_filter, gain_row)

    total = 2 * few * parts * (devices + 1)
    conv = pl.pallas_call(
        functools.partial(conv_kernel, parts, few, chunks),
        out_shape=jax.ShapeDtypeStruct((everyone, few, rows), F32),
        in_specs=[whole] * 6,
        out_specs=whole,
        scratch_shapes=[
            pltpu.VMEM((4 * outer * (few + 1), LANES), F32),
            pltpu.VMEM((total, 6 * LANES), BF16),
            pltpu.VMEM((total, 2 * LANES), F32),
            pltpu.VMEM((total, 2 * LANES), F32),
        ],
        compiler_params=small,
        cost_estimate=pl.CostEstimate(flops=0, bytes_accessed=4 << 20, transcendentals=0),
    )(come, *(jnp.asarray(t) for t in tables(parts, devices, rows)))

    back = lax.all_to_all(conv, ("dp", "ctx"), 0, 0, tiled=True)
    return pl.pallas_call(
        gate_kernel,
        out_shape=jax.ShapeDtypeStruct((rows, channels), F32),
        in_specs=[whole] * 3,
        out_specs=whole,
        compiler_params=small,
        cost_estimate=pl.CostEstimate(flops=0, bytes_accessed=1 << 21, transcendentals=0),
    )(back, query_seq, direct)


def fits_tiles(mesh, rows, channels):
    parts, devices = mesh.shape["dp"], mesh.shape["ctx"]
    few, rest = divmod(channels, parts * devices)
    chunks = 2 * rows // parts // 64
    return (
        rest == 0
        and few == 16
        and devices == 16
        and rows == 2 * LANES
        and parts * devices * chunks == LANES
        and chunks % 2 == 0
    )


def solution(mesh):
    placed = (
        P(("dp", "ctx"), None),
        P(("dp", "ctx"), None),
        P(("dp", "ctx"), None),
        P(),
        P(),
        P(None, "ctx", None),
    )

    def per_device(q_proj, *rest):
        form = per_device_tiled if fits_tiles(mesh, *q_proj.shape) else per_device_general
        return form(q_proj, *rest)

    return jax.shard_map(
        per_device, mesh=mesh, in_specs=placed, out_specs=P(("dp", "ctx"), None), check_vma=False
    )
```

```python
import functools
import itertools
import math

import jax
import jax.numpy as jnp
import numpy as np
from jax import lax
from jax.experimental import pallas as pl
from jax.experimental.pallas import tpu as pltpu
from jax.sharding import PartitionSpec as P

precise_mode = lax.Precision.HIGHEST
LANES = 128
BF16 = jnp.bfloat16
F32 = jnp.float32


def causal_short(signal, rim_rows, tap_gains):
    padded = jnp.concatenate([rim_rows, signal], axis=0)
    return tap_gains[0] * signal + tap_gains[1] * padded[1:-1] + tap_gains[2] * padded[:-2]


def shifted(block, axis, distance):
    devices = range(lax.axis_size(axis))
    route = [(i - distance, i) for i in devices if i - distance in devices]
    return lax.ppermute(block, axis, route)


def channel_conv(mixed_in, filter_spec, devices):
    local_rows = mixed_in.shape[0]
    seq_len = local_rows * devices
    freq_len = 2 * seq_len
    outer_len = 2 * devices
    half_inner = local_rows // 2
    columns = lax.all_to_all(mixed_in, "ctx", split_axis=1, concat_axis=0, tiled=True)
    spec_cols = lax.all_to_all(filter_spec, "ctx", split_axis=2, concat_axis=1, tiled=True)
    few_channels = columns.shape[1]
    grid = columns.reshape(half_inner, outer_len, few_channels)
    row_index = lax.iota(jnp.int32, half_inner)
    inner_freq = lax.iota(jnp.int32, local_rows)
    outer_index = lax.iota(jnp.int32, outer_len)

    def cos_sin(left, right, period):
        turns = (left[:, None] * right[None, :] % period).astype(F32) / period
        return jnp.cos(2.0 * math.pi * turns), jnp.sin(2.0 * math.pi * turns)

    first_cos, first_sin = cos_sin(row_index, inner_freq, local_rows)
    twist_cos, twist_sin = cos_sin(inner_freq, outer_index, freq_len)
    twist_cos, twist_sin = twist_cos[:, :, None], twist_sin[:, :, None]
    last_cos, last_sin = cos_sin(outer_index, outer_index, outer_len)
    dots = functools.partial(jnp.einsum, precision=precise_mode)
    section_re = dots("bk,bac->kac", first_cos, grid)
    section_im = -dots("bk,bac->kac", first_sin, grid)
    turned_re = section_re * twist_cos + section_im * twist_sin
    turned_im = section_im * twist_cos - section_re * twist_sin
    fore = "kac,aj->kjc"
    spec_re = dots(fore, turned_re, last_cos) + dots(fore, turned_im, last_sin)
    spec_im = dots(fore, turned_im, last_cos) - dots(fore, turned_re, last_sin)
    resp = jnp.transpose(spec_cols.reshape(2, outer_len, local_rows, few_channels), (0, 2, 1, 3))
    prod_re = spec_re * resp[0] - spec_im * resp[1]
    prod_im = spec_re * resp[1] + spec_im * resp[0]
    back = "kjc,aj->kac"
    undo_re = dots(back, prod_re, last_cos) - dots(back, prod_im, last_sin)
    undo_im = dots(back, prod_im, last_cos) + dots(back, prod_re, last_sin)
    back_re = undo_re * twist_cos - undo_im * twist_sin
    back_im = undo_im * twist_cos + undo_re * twist_sin
    signal_out = dots("bk,kac->bac", first_cos, back_re) - dots("bk,kac->bac", first_sin, back_im)
    conv_cols = signal_out.reshape(seq_len, few_channels) / freq_len
    return lax.all_to_all(conv_cols, "ctx", split_axis=0, concat_axis=1, tiled=True)


def per_device_general(q_proj, k_proj, v_proj, short_filter, skip_gain, filter_spec):
    devices = lax.axis_size("ctx")
    tail_rows = jnp.stack([q_proj[-2:], k_proj[-2:], v_proj[-2:]])
    rim_rows = shifted(tail_rows, "ctx", 1)
    query_seq = causal_short(q_proj, rim_rows[0], short_filter[0])
    key_seq = causal_short(k_proj, rim_rows[1], short_filter[1])
    value_seq = causal_short(v_proj, rim_rows[2], short_filter[2])
    mixed_in = key_seq * value_seq
    conv_out = channel_conv(mixed_in, filter_spec, devices)
    return query_seq * (conv_out + skip_gain[None, :] * mixed_in)


def split_np(table):
    high = table.astype(BF16)
    low = (table - high.astype(np.float64)).astype(BF16)
    return high, low


@functools.lru_cache(maxsize=None)
def tables(parts, devices, rows):
    outer, seq = 2 * devices, devices * rows
    freq = 2 * seq
    chunks = rows * 2 // parts // 64
    low_bit, chunk, part, dev = np.meshgrid(
        np.arange(2), np.arange(chunks), np.arange(parts), np.arange(devices), indexing="ij"
    )
    k = (dev * (2 * rows // outer) + part * (2 * rows // parts // outer) + 2 * chunk + low_bit).ravel()

    def angle(left, right, period):
        return 2.0 * np.pi * (np.outer(left, right) % period) / period

    s, r, half = np.arange(devices + 1), np.arange(rows), rows // 2
    twist = angle(s, r, freq)
    weight = np.where((s % 2 == 1) | (s % devices == 0), 2.0, 1.0)[:, None] / (2 * freq)
    turns = [np.cos(twist), np.sin(twist), weight * np.cos(twist), weight * np.sin(twist)]
    parity = angle([1], r[:half], rows)
    inner = angle(r[:half], k[:half] // 2, half)
    c, d = np.cos(inner), np.sin(inner)

    def tripled(table):
        high, low = split_np(table)
        return np.concatenate([high, high, low])

    fore = tripled(np.block([[c, -d], [d, c]]))
    back = tripled(np.block([[c.T, d.T], [-d.T, c.T]]))
    flip = np.concatenate([np.eye(LANES)[::-1]] * 2).astype(BF16)
    turns = np.stack(turns).astype(np.float32)
    parity = np.concatenate([np.cos(parity), np.sin(parity)]).astype(np.float32)
    return turns, parity, fore, back, flip


def split(x):
    high = x.astype(BF16)
    return high, (x - high.astype(F32)).astype(BF16)


def dot(a, b):
    return jnp.dot(a, b, preferred_element_type=F32)


def plus(a, b):
    return b if a is None else a if b is None else a + b


def minus(a, b):
    return a if b is None else -b if a is None else a - b


def times(a, scale):
    if a is None or abs(scale) < 1e-12:
        return None
    return a if scale == 1.0 else -a if scale == -1.0 else a * scale


def c_add(a, b):
    return plus(a[0], b[0]), plus(a[1], b[1])


def c_sub(a, b):
    return minus(a[0], b[0]), minus(a[1], b[1])


def c_conj(a):
    return a[0], None if a[1] is None else -a[1]


def c_turn(a, turn):
    c, d = math.cos(2 * math.pi * turn), math.sin(2 * math.pi * turn)
    c, d = (float(round(v)) if abs(v - round(v)) < 1e-12 else v for v in (c, d))
    return minus(times(a[0], c), times(a[1], d)), plus(times(a[0], d), times(a[1], c))


def fft_complex(z, sign):
    n = len(z)
    if n == 1:
        return z
    even, odd = fft_complex(z[::2], sign), fft_complex(z[1::2], sign)
    odd = [c_turn(v, sign * t / n) for t, v in enumerate(odd)]
    return [c_add(e, o) for e, o in zip(even, odd)] + [c_sub(e, o) for e, o in zip(even, odd)]


def fft_real(x):
    n = len(x)
    if n == 1:
        return [(x[0], None)]
    half = n // 2
    even, odd = fft_real(x[::2]), fft_real(x[1::2])
    out = [None] * (half + 1)
    for t, (e, o) in enumerate(zip(even, odd)):
        o = c_turn(o, -t / n)
        out[half - t] = c_conj(c_sub(e, o))
        out[t] = c_add(e, o)
    return out


def fft_to_real(z):
    half = len(z) - 1
    n = 2 * half
    if n == 2:
        return [plus(z[0][0], z[1][0]), minus(z[0][0], z[1][0])]
    even, odd = [], []
    for t in range(half // 2 + 1):
        other = c_conj(z[half - t])
        even.append(c_add(z[t], other))
        odd.append(c_turn(c_sub(z[t], other), t / n))
    out = [None] * n
    out[::2], out[1::2] = fft_to_real(even), fft_to_real(odd)
    return out


def spread(x):
    n = len(x)
    turned = [c_turn((v, None), -p / (2 * n)) for p, v in enumerate(x)]
    even, odd = fft_complex(turned[::2], -1), fft_complex(turned[1::2], -1)
    out = [None] * (n + 1)
    out[::2] = fft_real(x)
    out[1::2] = [c_add(e, c_turn(o, -t / n)) for t, (e, o) in enumerate(zip(even, odd))]
    return out


def gather(z):
    n = len(z) - 1
    ends = [(z[0][0], None), *z[2:n:2], (z[n][0], None)]
    even = fft_to_real(ends)
    odd = [None] * n
    odd[::2] = fft_complex(z[1::2], 1)
    odd[1::2] = fft_complex([c_turn(v, t / n) for t, v in enumerate(z[1::2])], 1)
    return [plus(e, c_turn(o, p / (2 * n))[0]) for p, (e, o) in enumerate(zip(even, odd))]


def causal(x, taps):
    return taps[0:1] * x + taps[1:2] * pltpu.roll(x, 1, 0) + taps[2:3] * pltpu.roll(x, 2, 0)


def block_turn(x, few):
    row = lax.broadcasted_iota(jnp.int32, x.shape, 0)
    block = lax.broadcasted_iota(jnp.int32, x.shape, 1) // few
    out = x
    for d in range(1, 8):
        moved = pltpu.roll(pltpu.roll(x, LANES - few * d, 1), d, 0)
        out = jnp.where((row - block + 8) % 8 == d, moved, out)
    return out


def pack_kernel(
    few, chunks, part_ref, q_ref, k_ref, v_ref, taps_ref, gain_ref, spec_ref,
    out_ref, ends, keys, values, taps, gain, held, sems, held_sems, key_sems,
):
    rows = q_ref.shape[0]
    near = LANES // few
    start = pl.multiple_of(part_ref[0] * (64 * chunks), 64 * chunks)
    blocks = k_ref.shape[1] // LANES
    base = few * chunks

    def columns(i):
        return slice(LANES * i, LANES * i + LANES)

    def chunk_rows(m):
        return spec_ref.at[:, pl.ds(start + 64 * m, 64), :]

    small = [(taps_ref, taps), (gain_ref, gain)]
    small += [(q_ref.at[0:8], ends.at[0:8]), (q_ref.at[rows - 8 : rows], ends.at[8:16])]
    small = [pltpu.make_async_copy(*pair, sems.at[i]) for i, pair in enumerate(small)]
    large = [pltpu.make_async_copy(chunk_rows(m), held.at[m], held_sems.at[m]) for m in range(chunks)]
    inputs = [
        [
            pltpu.make_async_copy(src.at[:, columns(i)], dst.at[:, columns(i)], key_sems.at[j, i])
            for j, (src, dst) in enumerate(((k_ref, keys), (v_ref, values)))
        ]
        for i in range(blocks)
    ]
    for copy in (large[0], *small, *inputs[0], *large[1:], *sum(inputs[1:], [])):
        copy.start()

    def turn_chunk(m):
        large[m].wait()
        for i in range(blocks):
            both = held[m, :, :, columns(i)].reshape(LANES, LANES)
            out_ref[near * i : near * i + near, few * m : few * m + few, :] = both.T.reshape(near, few, LANES)

    turn_chunk(0)
    for copy in small:
        copy.wait()
    for i in range(blocks):
        if i == 1:
            for m in range(1, chunks):
                turn_chunk(m)
        for copy in inputs[i]:
            copy.wait()
        col = columns(i)
        dests = slice(near * i, near * i + near)
        mixed_in = causal(keys[:, col], taps[1, :, col]) * causal(values[:, col], taps[2, :, col])
        for h in range(rows // LANES):
            turned = mixed_in[LANES * h : LANES * h + LANES].T
            at = base + few * h
            out_ref[dests, at : at + few, :] = turned.reshape(near, few, LANES)

        def known(first, last, j):
            t0, t1, t2 = taps[j, 0:1, col], taps[j, 1:2, col], taps[j, 2:3, col]
            own = t0 * first[0:1], t0 * first[1:2] + t1 * first[0:1]
            following = t1 * last[1:2] + t2 * last[0:1], t2 * last[1:2]
            return *own, *following

        k0, k1, next_k0, next_k1 = known(keys[0:2, col], keys[rows - 2 : rows, col], 1)
        v0, v1, next_v0, next_v1 = known(values[0:2, col], values[rows - 2 : rows, col], 2)
        q0, q1, next_q0, next_q1 = known(ends[0:2, col], ends[14:16, col], 0)
        nothing = jnp.zeros_like(q0)
        at = base + few * (rows // LANES)
        pairs = jnp.concatenate([k0, v0, k1, v1, next_k0, next_v0, next_k1, next_v1], axis=0)
        others = [q0, q1, next_q0, next_q1, gain[:, col], nothing, nothing, nothing]
        out_ref[dests, at, :] = block_turn(pairs, few)
        out_ref[dests, at + 1, :] = block_turn(jnp.concatenate(others, axis=0), few)
        for j in range(2, 8):
            out_ref[dests, at + j, :] = jnp.zeros((near, LANES), F32)


def local_kernel(q_ref, k_ref, v_ref, taps_ref, gain_ref, query_ref, direct_ref):
    for i in range(q_ref.shape[1] // LANES):
        col = slice(LANES * i, LANES * i + LANES)
        query_seq = causal(q_ref[:, col], taps_ref[0, :, col])
        key_seq = causal(k_ref[:, col], taps_ref[1, :, col])
        value_seq = causal(v_ref[:, col], taps_ref[2, :, col])
        direct = query_seq * (gain_ref[:, col] * (key_seq * value_seq))
        row = lax.broadcasted_iota(jnp.int32, direct.shape, 0)
        query_ref[:, col] = jnp.where(row < 2, 1.0, query_seq)
        direct_ref[:, col] = jnp.where(row < 2, 0.0, direct)


def gate_kernel(conv_ref, query_ref, direct_ref, out_ref, gated, sems):
    few = conv_ref.shape[1]
    near = LANES // few
    leaving = []
    for h in range(conv_ref.shape[2] // LANES):
        row = slice(LANES * h, LANES * h + LANES)
        for i in range(conv_ref.shape[0] // near):
            col = slice(LANES * i, LANES * i + LANES)
            conv = conv_ref[near * i : near * i + near, :, row].reshape(LANES, LANES)
            gated[row, col] = query_ref[row, col] * conv.T + direct_ref[row, col]
        leaving.append(pltpu.make_async_copy(gated.at[row], out_ref.at[row], sems.at[h]))
        leaving[h].start()
    for copy in leaving:
        copy.wait()


def conv_kernel(
    parts, few, chunks, in_ref, turn_ref, parity_ref, fore_ref, back_ref, flip_ref, out_ref, spec, triple, freq, undo, ends
):
    devices = in_ref.shape[0] // parts
    outer = 2 * devices
    kept = devices + 1
    base, pitch = few * chunks, few + 1
    left, right = slice(0, LANES), slice(LANES, 2 * LANES)
    lane_of = lax.broadcasted_iota(jnp.int32, (few, LANES), 1)

    everyone = in_ref.shape[0]
    begins = lax.broadcasted_iota(jnp.int32, (everyone, LANES), 0) % devices == 0
    pairs, others = in_ref[:, base + 2 * few, :], in_ref[:, base + 2 * few + 1, :]

    def before(x, lanes):
        moved = pltpu.roll(pltpu.roll(x, 1, 0), LANES - lanes, 1)
        return jnp.where(begins, 0.0, moved)

    pairs = pairs + before(pairs, 4 * few)
    query = others + before(others, 2 * few)
    mixed = pairs * pltpu.roll(pairs, LANES - few, 1)
    gain = pltpu.roll(others, LANES - 4 * few, 1)
    mixed_second = pltpu.roll(mixed, LANES - 2 * few, 1)
    query_second = pltpu.roll(query, LANES - few, 1)
    direct = query * gain * mixed, query_second * gain * mixed_second
    for r, group in enumerate(((mixed, query, direct[0]), (mixed_second, query_second, direct[1]))):
        for j, x in enumerate(group):
            ends[pl.ds(2 * everyone * j + r, everyone, stride=2), :] = x
    ends_of = [ends[2 * everyone * j : 2 * everyone * (j + 1)].T[:few] for j in range(3)]

    def first_lanes(j, at):
        wide = jnp.concatenate([ends_of[j]] * (LANES // (2 * everyone)), axis=1)
        return pltpu.roll(wide, (LANES - 2 * at) % LANES, 1) if at else wide

    odd_cos, odd_sin = parity_ref[0:1], parity_ref[1:2]

    def row_of(low_bit, s, q):
        at = ((low_bit * kept + s) * parts + q) * few
        return slice(at, at + few)

    def keep(span, real, imag):
        for col, value in ((0, real), (LANES, imag)):
            high, low = split(value)
            for j, part in enumerate((high, low, high)):
                at = 2 * LANES * j + col
                triple[span, at : at + LANES] = part

    for q in range(parts):
        tiles = []
        for h in range(2):
            at = base + few * h
            x = [in_ref[q * devices + p, at : at + few, :] for p in range(devices)]
            if h == 0:
                x = [
                    jnp.where(lane_of < 2, first_lanes(0, q * devices + p), own)
                    for p, own in enumerate(x)
                ]
            tiles.append(spread(x))
        for s in range(kept):
            turned = []
            for (re, im), lane in zip((tiles[0][s], tiles[1][s]), (left, right)):
                cosine, sine = turn_ref[0, s : s + 1, lane], turn_ref[1, s : s + 1, lane]
                if im is None:
                    turned.append((re * cosine, -re * sine))
                else:
                    turned.append((re * cosine + im * sine, im * cosine - re * sine))
            keep(row_of(0, s, q), *c_add(*turned))
            re, im = c_sub(*turned)
            keep(row_of(1, s, q), re * odd_cos + im * odd_sin, im * odd_cos - re * odd_sin)

    pieces = 4
    size = freq.shape[0] // pieces
    for j in range(pieces):
        span = slice(j * size, (j + 1) * size)
        freq[span] = dot(triple[span], fore_ref[...])
        for c in range(j * few // pieces, (j + 1) * few // pieces):
            own = jnp.concatenate([in_ref[:, few * m + c, :] for m in range(chunks)], axis=0)
            spec[pl.ds(c, 4 * outer, stride=pitch), :] = own.T

    other = [[None, None], [None, None]]
    count = outer - kept
    for i in range(2):
        for low_bit in range(2):
            first = (2 * i + low_bit) * outer + kept
            pair = split(spec[first * pitch : (first + count) * pitch])
            other[i][low_bit] = dot(jnp.concatenate(pair, axis=1), flip_ref[...])

    def response(i, low_bit, s):
        at = ((2 * i + low_bit) * outer + s) * pitch
        own = spec[at : at + few]
        if 0 < s < devices:
            at = (outer - s - kept) * pitch
            mirror = other[i][1 - low_bit][at : at + few]
            own = own - mirror if i else own + mirror
        return own

    cuts = (0, kept // 2, kept)
    for low_bit, (begin, end) in itertools.product(range(2), zip(cuts[:-1], cuts[1:])):
        for s in range(begin, end):
            h_re, h_im = response(0, low_bit, s), response(1, low_bit, s)
            for q in range(parts):
                span = row_of(low_bit, s, q)
                re, im = freq[span, left], freq[span, right]
                keep(span, re * h_re - im * h_im, re * h_im + im * h_re)
        span = slice(row_of(low_bit, begin, 0).start, row_of(low_bit, end, 0).start)
        undo[span] = dot(triple[span], back_ref[...])

    for q in range(parts):
        tiles = [], []
        for s in range(kept):
            even, odd = row_of(0, s, q), row_of(1, s, q)
            base_value = undo[even, left], undo[even, right]
            re, im = undo[odd, left], undo[odd, right]
            odd_value = re * odd_cos - im * odd_sin, im * odd_cos + re * odd_sin
            both = c_add(base_value, odd_value), c_sub(base_value, odd_value)
            for tile, (re, im), lane in zip(tiles, both, (left, right)):
                cosine, sine = turn_ref[2, s : s + 1, lane], turn_ref[3, s : s + 1, lane]
                tile.append((re * cosine - im * sine, im * cosine + re * sine))
        for tile, lane in zip(tiles, (left, right)):
            for p, y in enumerate(gather(tile)):
                at = q * devices + p
                if lane == left:
                    finished = first_lanes(1, at) * y + first_lanes(2, at)
                    y = jnp.where(lane_of < 2, finished, y)
                out_ref[at, :, lane] = y


def per_device_tiled(q_proj, k_proj, v_proj, short_filter, skip_gain, filter_spec):
    parts, devices = lax.axis_size("dp"), lax.axis_size("ctx")
    everyone = parts * devices
    rows, channels = q_proj.shape
    few = channels // everyone
    chunks = 2 * rows // parts // 64
    halves = rows // LANES
    depth = few * (chunks + halves) + 8
    outer = 2 * devices
    whole = pl.BlockSpec(memory_space=pltpu.VMEM)
    in_hbm = pl.BlockSpec(memory_space=pltpu.HBM)
    small = pltpu.CompilerParams(vmem_limit_bytes=16 << 20)
    gain_row = skip_gain[None, :]

    part = lax.axis_index("dp").reshape(1)
    sources = (q_proj, k_proj, v_proj, short_filter, gain_row, filter_spec)
    sent = pl.pallas_call(
        functools.partial(pack_kernel, few, chunks),
        out_shape=jax.ShapeDtypeStruct((everyone, depth, LANES), F32),
        in_specs=[pl.BlockSpec(memory_space=pltpu.SMEM)] + [in_hbm] * 6,
        out_specs=whole,
        compiler_params=small,
        scratch_shapes=[
            pltpu.VMEM((16, channels), F32),
            pltpu.VMEM((rows, channels), F32),
            pltpu.VMEM((rows, channels), F32),
            pltpu.VMEM((3, 3, channels), F32),
            pltpu.VMEM((1, channels), F32),
            pltpu.VMEM((chunks, 2, 64, channels), F32),
            pltpu.SemaphoreType.DMA((4,)),
            pltpu.SemaphoreType.DMA((chunks,)),
            pltpu.SemaphoreType.DMA((2, channels // LANES)),
        ],
        cost_estimate=pl.CostEstimate(flops=0, bytes_accessed=1 << 22, transcendentals=0),
    )(part, *(pltpu.with_memory_space_constraint(x, pltpu.HBM) for x in sources))

    come = lax.all_to_all(sent, ("dp", "ctx"), 0, 0, tiled=True)

    query_seq, direct = pl.pallas_call(
        local_kernel,
        out_shape=[jax.ShapeDtypeStruct((rows, channels), F32)] * 2,
        in_specs=[whole] * 5,
        out_specs=[whole] * 2,
        compiler_params=small,
        cost_estimate=pl.CostEstimate(flops=0, bytes_accessed=5 << 19, transcendentals=0),
    )(q_proj, k_proj, v_proj, short_filter, gain_row)

    total = 2 * few * parts * (devices + 1)
    conv = pl.pallas_call(
        functools.partial(conv_kernel, parts, few, chunks),
        out_shape=jax.ShapeDtypeStruct((everyone, few, rows), F32),
        in_specs=[whole] * 6,
        out_specs=whole,
        scratch_shapes=[
            pltpu.VMEM((4 * outer * (few + 1), LANES), F32),
            pltpu.VMEM((total, 6 * LANES), BF16),
            pltpu.VMEM((total, 2 * LANES), F32),
            pltpu.VMEM((total, 2 * LANES), F32),
            pltpu.VMEM((6 * everyone, LANES), F32),
        ],
        compiler_params=small,
        cost_estimate=pl.CostEstimate(flops=0, bytes_accessed=4 << 20, transcendentals=0),
    )(come, *(jnp.asarray(t) for t in tables(parts, devices, rows)))

    back = lax.all_to_all(conv, ("dp", "ctx"), 0, 0, tiled=True)
    return pl.pallas_call(
        gate_kernel,
        out_shape=jax.ShapeDtypeStruct((rows, channels), F32),
        in_specs=[whole] * 3,
        out_specs=in_hbm,
        scratch_shapes=[pltpu.VMEM((rows, channels), F32), pltpu.SemaphoreType.DMA((halves,))],
        compiler_params=small,
        cost_estimate=pl.CostEstimate(flops=0, bytes_accessed=1 << 21, transcendentals=0),
    )(back, query_seq, direct)


def fits_tiles(mesh, rows, channels):
    parts, devices = mesh.shape["dp"], mesh.shape["ctx"]
    few, rest = divmod(channels, parts * devices)
    chunks = 2 * rows // parts // 64
    return (
        rest == 0
        and few == 16
        and devices == 16
        and rows == 2 * LANES
        and parts * devices * chunks == LANES
        and chunks % 2 == 0
    )


def solution(mesh):
    placed = (
        P(("dp", "ctx"), None),
        P(("dp", "ctx"), None),
        P(("dp", "ctx"), None),
        P(),
        P(),
        P(None, "ctx", None),
    )

    def per_device(q_proj, *rest):
        form = per_device_tiled if fits_tiles(mesh, *q_proj.shape) else per_device_general
        return form(q_proj, *rest)

    return jax.shard_map(
        per_device, mesh=mesh, in_specs=placed, out_specs=P(("dp", "ctx"), None), check_vma=False
    )
```

```python
import functools
import itertools
import math

import jax
import jax.numpy as jnp
import numpy as np
from jax import lax
from jax.experimental import pallas as pl
from jax.experimental.pallas import tpu as pltpu
from jax.sharding import PartitionSpec as P

precise_mode = lax.Precision.HIGHEST
LANES = 128
BF16 = jnp.bfloat16
F32 = jnp.float32


def causal_short(signal, rim_rows, tap_gains):
    padded = jnp.concatenate([rim_rows, signal], axis=0)
    return tap_gains[0] * signal + tap_gains[1] * padded[1:-1] + tap_gains[2] * padded[:-2]


def shifted(block, axis, distance):
    devices = range(lax.axis_size(axis))
    route = [(i - distance, i) for i in devices if i - distance in devices]
    return lax.ppermute(block, axis, route)


def channel_conv(mixed_in, filter_spec, devices):
    local_rows = mixed_in.shape[0]
    seq_len = local_rows * devices
    freq_len = 2 * seq_len
    outer_len = 2 * devices
    half_inner = local_rows // 2
    columns = lax.all_to_all(mixed_in, "ctx", split_axis=1, concat_axis=0, tiled=True)
    spec_cols = lax.all_to_all(filter_spec, "ctx", split_axis=2, concat_axis=1, tiled=True)
    few_channels = columns.shape[1]
    grid = columns.reshape(half_inner, outer_len, few_channels)
    row_index = lax.iota(jnp.int32, half_inner)
    inner_freq = lax.iota(jnp.int32, local_rows)
    outer_index = lax.iota(jnp.int32, outer_len)

    def cos_sin(left, right, period):
        turns = (left[:, None] * right[None, :] % period).astype(F32) / period
        return jnp.cos(2.0 * math.pi * turns), jnp.sin(2.0 * math.pi * turns)

    first_cos, first_sin = cos_sin(row_index, inner_freq, local_rows)
    twist_cos, twist_sin = cos_sin(inner_freq, outer_index, freq_len)
    twist_cos, twist_sin = twist_cos[:, :, None], twist_sin[:, :, None]
    last_cos, last_sin = cos_sin(outer_index, outer_index, outer_len)
    dots = functools.partial(jnp.einsum, precision=precise_mode)
    section_re = dots("bk,bac->kac", first_cos, grid)
    section_im = -dots("bk,bac->kac", first_sin, grid)
    turned_re = section_re * twist_cos + section_im * twist_sin
    turned_im = section_im * twist_cos - section_re * twist_sin
    fore = "kac,aj->kjc"
    spec_re = dots(fore, turned_re, last_cos) + dots(fore, turned_im, last_sin)
    spec_im = dots(fore, turned_im, last_cos) - dots(fore, turned_re, last_sin)
    resp = jnp.transpose(spec_cols.reshape(2, outer_len, local_rows, few_channels), (0, 2, 1, 3))
    prod_re = spec_re * resp[0] - spec_im * resp[1]
    prod_im = spec_re * resp[1] + spec_im * resp[0]
    back = "kjc,aj->kac"
    undo_re = dots(back, prod_re, last_cos) - dots(back, prod_im, last_sin)
    undo_im = dots(back, prod_im, last_cos) + dots(back, prod_re, last_sin)
    back_re = undo_re * twist_cos - undo_im * twist_sin
    back_im = undo_im * twist_cos + undo_re * twist_sin
    signal_out = dots("bk,kac->bac", first_cos, back_re) - dots("bk,kac->bac", first_sin, back_im)
    conv_cols = signal_out.reshape(seq_len, few_channels) / freq_len
    return lax.all_to_all(conv_cols, "ctx", split_axis=0, concat_axis=1, tiled=True)


def per_device_general(q_proj, k_proj, v_proj, short_filter, skip_gain, filter_spec):
    devices = lax.axis_size("ctx")
    tail_rows = jnp.stack([q_proj[-2:], k_proj[-2:], v_proj[-2:]])
    rim_rows = shifted(tail_rows, "ctx", 1)
    query_seq = causal_short(q_proj, rim_rows[0], short_filter[0])
    key_seq = causal_short(k_proj, rim_rows[1], short_filter[1])
    value_seq = causal_short(v_proj, rim_rows[2], short_filter[2])
    mixed_in = key_seq * value_seq
    conv_out = channel_conv(mixed_in, filter_spec, devices)
    return query_seq * (conv_out + skip_gain[None, :] * mixed_in)


def split_np(table):
    high = table.astype(BF16)
    low = (table - high.astype(np.float64)).astype(BF16)
    return high, low


@functools.lru_cache(maxsize=None)
def tables(parts, devices, rows):
    outer, seq = 2 * devices, devices * rows
    freq = 2 * seq
    chunks = rows * 2 // parts // 64
    low_bit, chunk, dev, part = np.meshgrid(
        np.arange(2), np.arange(chunks), np.arange(devices), np.arange(parts), indexing="ij"
    )
    k = (dev * (2 * rows // outer) + part * (2 * rows // parts // outer) + 2 * chunk + low_bit).ravel()

    def angle(left, right, period):
        return 2.0 * np.pi * (np.outer(left, right) % period) / period

    s, r, half = np.arange(devices + 1), np.arange(rows), rows // 2
    twist = angle(s, r, freq)
    weight = np.where((s % 2 == 1) | (s % devices == 0), 2.0, 1.0)[:, None] / (2 * freq)
    turns = [np.cos(twist), np.sin(twist), weight * np.cos(twist), weight * np.sin(twist)]
    parity = angle([1], r[:half], rows)
    inner = angle(r[:half], k[:half] // 2, half)
    c, d = np.cos(inner), np.sin(inner)

    def tripled(table):
        high, low = split_np(table)
        return np.concatenate([high, high, low])

    fore = tripled(np.block([[c, -d], [d, c]]))
    back = tripled(np.block([[c.T, d.T], [-d.T, c.T]]))
    flip = np.concatenate([np.eye(LANES)[::-1]] * 2).astype(BF16)
    turns = np.stack(turns).astype(np.float32)
    parity = np.concatenate([np.cos(parity), np.sin(parity)]).astype(np.float32)
    return turns, parity, fore, back, flip


def split(x):
    high = x.astype(BF16)
    return high, (x - high.astype(F32)).astype(BF16)


def dot(a, b):
    return jnp.dot(a, b, preferred_element_type=F32)


def plus(a, b):
    return b if a is None else a if b is None else a + b


def minus(a, b):
    return a if b is None else -b if a is None else a - b


def times(a, scale):
    if a is None or abs(scale) < 1e-12:
        return None
    return a if scale == 1.0 else -a if scale == -1.0 else a * scale


def c_add(a, b):
    return plus(a[0], b[0]), plus(a[1], b[1])


def c_sub(a, b):
    return minus(a[0], b[0]), minus(a[1], b[1])


def c_conj(a):
    return a[0], None if a[1] is None else -a[1]


def c_turn(a, turn):
    c, d = math.cos(2 * math.pi * turn), math.sin(2 * math.pi * turn)
    c, d = (float(round(v)) if abs(v - round(v)) < 1e-12 else v for v in (c, d))
    return minus(times(a[0], c), times(a[1], d)), plus(times(a[0], d), times(a[1], c))


def fft_complex(z, sign):
    n = len(z)
    if n == 1:
        return z
    even, odd = fft_complex(z[::2], sign), fft_complex(z[1::2], sign)
    odd = [c_turn(v, sign * t / n) for t, v in enumerate(odd)]
    return [c_add(e, o) for e, o in zip(even, odd)] + [c_sub(e, o) for e, o in zip(even, odd)]


def fft_real(x):
    n = len(x)
    if n == 1:
        return [(x[0], None)]
    half = n // 2
    even, odd = fft_real(x[::2]), fft_real(x[1::2])
    out = [None] * (half + 1)
    for t, (e, o) in enumerate(zip(even, odd)):
        o = c_turn(o, -t / n)
        out[half - t] = c_conj(c_sub(e, o))
        out[t] = c_add(e, o)
    return out


def fft_to_real(z):
    half = len(z) - 1
    n = 2 * half
    if n == 2:
        return [plus(z[0][0], z[1][0]), minus(z[0][0], z[1][0])]
    even, odd = [], []
    for t in range(half // 2 + 1):
        other = c_conj(z[half - t])
        even.append(c_add(z[t], other))
        odd.append(c_turn(c_sub(z[t], other), t / n))
    out = [None] * n
    out[::2], out[1::2] = fft_to_real(even), fft_to_real(odd)
    return out


def spread(x):
    n = len(x)
    turned = [c_turn((v, None), -p / (2 * n)) for p, v in enumerate(x)]
    even, odd = fft_complex(turned[::2], -1), fft_complex(turned[1::2], -1)
    out = [None] * (n + 1)
    out[::2] = fft_real(x)
    out[1::2] = [c_add(e, c_turn(o, -t / n)) for t, (e, o) in enumerate(zip(even, odd))]
    return out


def gather(z):
    n = len(z) - 1
    ends = [(z[0][0], None), *z[2:n:2], (z[n][0], None)]
    even = fft_to_real(ends)
    odd = [None] * n
    odd[::2] = fft_complex(z[1::2], 1)
    odd[1::2] = fft_complex([c_turn(v, t / n) for t, v in enumerate(z[1::2])], 1)
    return [plus(e, c_turn(o, p / (2 * n))[0]) for p, (e, o) in enumerate(zip(even, odd))]


def causal(x, taps):
    return taps[0:1] * x + taps[1:2] * pltpu.roll(x, 1, 0) + taps[2:3] * pltpu.roll(x, 2, 0)


def block_turn(x, few):
    row = lax.broadcasted_iota(jnp.int32, x.shape, 0)
    block = lax.broadcasted_iota(jnp.int32, x.shape, 1) // few
    out = x
    for d in range(1, 8):
        moved = pltpu.roll(pltpu.roll(x, LANES - few * d, 1), d, 0)
        out = jnp.where((row - block + 8) % 8 == d, moved, out)
    return out


def pack_kernel(
    few, chunks, part_ref, q_ref, k_ref, v_ref, taps_ref, gain_ref, spec_ref,
    out_ref, ends, keys, values, taps, gain, held, sems, held_sems, key_sems,
):
    rows = q_ref.shape[0]
    near = LANES // few
    start = pl.multiple_of(part_ref[0] * (64 * chunks), 64 * chunks)
    blocks = k_ref.shape[1] // LANES
    base = few * chunks

    def columns(i):
        return slice(LANES * i, LANES * i + LANES)

    def chunk_rows(m):
        return spec_ref.at[:, pl.ds(start + 64 * m, 64), :]

    small = [(taps_ref, taps), (gain_ref, gain)]
    small += [(q_ref.at[0:8], ends.at[0:8]), (q_ref.at[rows - 8 : rows], ends.at[8:16])]
    small = [pltpu.make_async_copy(*pair, sems.at[i]) for i, pair in enumerate(small)]
    large = [pltpu.make_async_copy(chunk_rows(m), held.at[m], held_sems.at[m]) for m in range(chunks)]
    inputs = [
        [
            pltpu.make_async_copy(src.at[:, columns(i)], dst.at[:, columns(i)], key_sems.at[j, i])
            for j, (src, dst) in enumerate(((k_ref, keys), (v_ref, values)))
        ]
        for i in range(blocks)
    ]
    for copy in (large[0], *small, *inputs[0], *large[1:], *sum(inputs[1:], [])):
        copy.start()

    def turn_chunk(m):
        large[m].wait()
        for i in range(blocks):
            both = held[m, :, :, columns(i)].reshape(LANES, LANES)
            out_ref[near * i : near * i + near, few * m : few * m + few, :] = both.T.reshape(near, few, LANES)

    turn_chunk(0)
    for copy in small:
        copy.wait()
    for i in range(blocks):
        if i == 1:
            for m in range(1, chunks):
                turn_chunk(m)
        for copy in inputs[i]:
            copy.wait()
        col = columns(i)
        dests = slice(near * i, near * i + near)
        mixed_in = causal(keys[:, col], taps[1, :, col]) * causal(values[:, col], taps[2, :, col])
        for h in range(rows // LANES):
            turned = mixed_in[LANES * h : LANES * h + LANES].T
            at = base + few * h
            out_ref[dests, at : at + few, :] = turned.reshape(near, few, LANES)

        def known(first, last, j):
            t0, t1, t2 = taps[j, 0:1, col], taps[j, 1:2, col], taps[j, 2:3, col]
            own = t0 * first[0:1], t0 * first[1:2] + t1 * first[0:1]
            following = t1 * last[1:2] + t2 * last[0:1], t2 * last[1:2]
            return *own, *following

        k0, k1, next_k0, next_k1 = known(keys[0:2, col], keys[rows - 2 : rows, col], 1)
        v0, v1, next_v0, next_v1 = known(values[0:2, col], values[rows - 2 : rows, col], 2)
        q0, q1, next_q0, next_q1 = known(ends[0:2, col], ends[14:16, col], 0)
        nothing = jnp.zeros_like(q0)
        at = base + few * (rows // LANES)
        pairs = jnp.concatenate([k0, v0, k1, v1, next_k0, next_v0, next_k1, next_v1], axis=0)
        others = [q0, q1, next_q0, next_q1, gain[:, col], nothing, nothing, nothing]
        out_ref[dests, at, :] = block_turn(pairs, few)
        out_ref[dests, at + 1, :] = block_turn(jnp.concatenate(others, axis=0), few)
        for j in range(2, 8):
            out_ref[dests, at + j, :] = jnp.zeros((near, LANES), F32)


def local_kernel(q_ref, k_ref, v_ref, taps_ref, gain_ref, query_ref, direct_ref):
    for i in range(q_ref.shape[1] // LANES):
        col = slice(LANES * i, LANES * i + LANES)
        query_seq = causal(q_ref[:, col], taps_ref[0, :, col])
        key_seq = causal(k_ref[:, col], taps_ref[1, :, col])
        value_seq = causal(v_ref[:, col], taps_ref[2, :, col])
        direct = query_seq * (gain_ref[:, col] * (key_seq * value_seq))
        row = lax.broadcasted_iota(jnp.int32, direct.shape, 0)
        query_ref[:, col] = jnp.where(row < 2, 1.0, query_seq)
        direct_ref[:, col] = jnp.where(row < 2, 0.0, direct)


def gate_kernel(conv_ref, query_ref, direct_ref, out_ref, gated, sems):
    few = conv_ref.shape[1]
    near = LANES // few
    leaving = []
    for h in range(conv_ref.shape[2] // LANES):
        row = slice(LANES * h, LANES * h + LANES)
        for i in range(conv_ref.shape[0] // near):
            col = slice(LANES * i, LANES * i + LANES)
            conv = conv_ref[near * i : near * i + near, :, row].reshape(LANES, LANES)
            gated[row, col] = query_ref[row, col] * conv.T + direct_ref[row, col]
        leaving.append(pltpu.make_async_copy(gated.at[row], out_ref.at[row], sems.at[h]))
        leaving[h].start()
    for copy in leaving:
        copy.wait()


def conv_kernel(
    parts, few, chunks, in_ref, turn_ref, parity_ref, fore_ref, back_ref, flip_ref, out_ref, spec, triple, freq, undo, ends
):
    devices = in_ref.shape[0] // parts
    outer = 2 * devices
    kept = devices + 1
    base, pitch = few * chunks, few + 1
    left, right = slice(0, LANES), slice(LANES, 2 * LANES)
    lane_of = lax.broadcasted_iota(jnp.int32, (few, LANES), 1)

    everyone = in_ref.shape[0]
    begins = lax.broadcasted_iota(jnp.int32, (everyone, LANES), 0) < parts
    pairs, others = in_ref[:, base + 2 * few, :], in_ref[:, base + 2 * few + 1, :]

    def before(x, lanes):
        moved = pltpu.roll(pltpu.roll(x, parts, 0), LANES - lanes, 1)
        return jnp.where(begins, 0.0, moved)

    pairs = pairs + before(pairs, 4 * few)
    query = others + before(others, 2 * few)
    mixed = pairs * pltpu.roll(pairs, LANES - few, 1)
    gain = pltpu.roll(others, LANES - 4 * few, 1)
    mixed_second = pltpu.roll(mixed, LANES - 2 * few, 1)
    query_second = pltpu.roll(query, LANES - few, 1)
    direct = query * gain * mixed, query_second * gain * mixed_second
    for r, group in enumerate(((mixed, query, direct[0]), (mixed_second, query_second, direct[1]))):
        for j, x in enumerate(group):
            ends[pl.ds(2 * everyone * j + r, everyone, stride=2), :] = x
    ends_of = [ends[2 * everyone * j : 2 * everyone * (j + 1)].T[:few] for j in range(3)]

    def first_lanes(j, at):
        wide = jnp.concatenate([ends_of[j]] * (LANES // (2 * everyone)), axis=1)
        return pltpu.roll(wide, (LANES - 2 * at) % LANES, 1) if at else wide

    odd_cos, odd_sin = parity_ref[0:1], parity_ref[1:2]

    def row_of(low_bit, s, q):
        at = ((low_bit * kept + s) * parts + q) * few
        return slice(at, at + few)

    def keep(span, real, imag):
        for col, value in ((0, real), (LANES, imag)):
            high, low = split(value)
            for j, part in enumerate((high, low, high)):
                at = 2 * LANES * j + col
                triple[span, at : at + LANES] = part

    for q in range(parts):
        tiles = []
        for h in range(2):
            at = base + few * h
            x = [in_ref[p * parts + q, at : at + few, :] for p in range(devices)]
            if h == 0:
                x = [
                    jnp.where(lane_of < 2, first_lanes(0, p * parts + q), own)
                    for p, own in enumerate(x)
                ]
            tiles.append(spread(x))
        for s in range(kept):
            turned = []
            for (re, im), lane in zip((tiles[0][s], tiles[1][s]), (left, right)):
                cosine, sine = turn_ref[0, s : s + 1, lane], turn_ref[1, s : s + 1, lane]
                if im is None:
                    turned.append((re * cosine, -re * sine))
                else:
                    turned.append((re * cosine + im * sine, im * cosine - re * sine))
            keep(row_of(0, s, q), *c_add(*turned))
            re, im = c_sub(*turned)
            keep(row_of(1, s, q), re * odd_cos + im * odd_sin, im * odd_cos - re * odd_sin)

    pieces = 4
    size = freq.shape[0] // pieces
    for j in range(pieces):
        span = slice(j * size, (j + 1) * size)
        freq[span] = dot(triple[span], fore_ref[...])
        for c in range(j * few // pieces, (j + 1) * few // pieces):
            own = jnp.concatenate([in_ref[:, few * m + c, :] for m in range(chunks)], axis=0)
            spec[pl.ds(c, 4 * outer, stride=pitch), :] = own.T

    other = [[None, None], [None, None]]
    count = outer - kept
    for i in range(2):
        for low_bit in range(2):
            first = (2 * i + low_bit) * outer + kept
            pair = split(spec[first * pitch : (first + count) * pitch])
            other[i][low_bit] = dot(jnp.concatenate(pair, axis=1), flip_ref[...])

    def response(i, low_bit, s):
        at = ((2 * i + low_bit) * outer + s) * pitch
        own = spec[at : at + few]
        if 0 < s < devices:
            at = (outer - s - kept) * pitch
            mirror = other[i][1 - low_bit][at : at + few]
            own = own - mirror if i else own + mirror
        return own

    cuts = (0, kept // 2, kept)
    for low_bit, (begin, end) in itertools.product(range(2), zip(cuts[:-1], cuts[1:])):
        for s in range(begin, end):
            h_re, h_im = response(0, low_bit, s), response(1, low_bit, s)
            for q in range(parts):
                span = row_of(low_bit, s, q)
                re, im = freq[span, left], freq[span, right]
                keep(span, re * h_re - im * h_im, re * h_im + im * h_re)
        span = slice(row_of(low_bit, begin, 0).start, row_of(low_bit, end, 0).start)
        undo[span] = dot(triple[span], back_ref[...])

    for q in range(parts):
        tiles = [], []
        for s in range(kept):
            even, odd = row_of(0, s, q), row_of(1, s, q)
            base_value = undo[even, left], undo[even, right]
            re, im = undo[odd, left], undo[odd, right]
            odd_value = re * odd_cos - im * odd_sin, im * odd_cos + re * odd_sin
            both = c_add(base_value, odd_value), c_sub(base_value, odd_value)
            for tile, (re, im), lane in zip(tiles, both, (left, right)):
                cosine, sine = turn_ref[2, s : s + 1, lane], turn_ref[3, s : s + 1, lane]
                tile.append((re * cosine - im * sine, im * cosine + re * sine))
        for tile, lane in zip(tiles, (left, right)):
            for p, y in enumerate(gather(tile)):
                at = p * parts + q
                if lane == left:
                    finished = first_lanes(1, at) * y + first_lanes(2, at)
                    y = jnp.where(lane_of < 2, finished, y)
                out_ref[at, :, lane] = y


def per_device_tiled(q_proj, k_proj, v_proj, short_filter, skip_gain, filter_spec):
    parts, devices = lax.axis_size("dp"), lax.axis_size("ctx")
    everyone = parts * devices
    rows, channels = q_proj.shape
    few = channels // everyone
    chunks = 2 * rows // parts // 64
    halves = rows // LANES
    depth = few * (chunks + halves) + 8
    outer = 2 * devices
    whole = pl.BlockSpec(memory_space=pltpu.VMEM)
    in_hbm = pl.BlockSpec(memory_space=pltpu.HBM)
    small = pltpu.CompilerParams(vmem_limit_bytes=16 << 20)
    gain_row = skip_gain[None, :]

    part = lax.axis_index("dp").reshape(1)
    sources = (q_proj, k_proj, v_proj, short_filter, gain_row, filter_spec)
    sent = pl.pallas_call(
        functools.partial(pack_kernel, few, chunks),
        out_shape=jax.ShapeDtypeStruct((everyone, depth, LANES), F32),
        in_specs=[pl.BlockSpec(memory_space=pltpu.SMEM)] + [in_hbm] * 6,
        out_specs=whole,
        compiler_params=small,
        scratch_shapes=[
            pltpu.VMEM((16, channels), F32),
            pltpu.VMEM((rows, channels), F32),
            pltpu.VMEM((rows, channels), F32),
            pltpu.VMEM((3, 3, channels), F32),
            pltpu.VMEM((1, channels), F32),
            pltpu.VMEM((chunks, 2, 64, channels), F32),
            pltpu.SemaphoreType.DMA((4,)),
            pltpu.SemaphoreType.DMA((chunks,)),
            pltpu.SemaphoreType.DMA((2, channels // LANES)),
        ],
        cost_estimate=pl.CostEstimate(flops=0, bytes_accessed=1 << 22, transcendentals=0),
    )(part, *(pltpu.with_memory_space_constraint(x, pltpu.HBM) for x in sources))

    come = lax.all_to_all(sent, ("ctx", "dp"), 0, 0, tiled=True)

    query_seq, direct = pl.pallas_call(
        local_kernel,
        out_shape=[jax.ShapeDtypeStruct((rows, channels), F32)] * 2,
        in_specs=[whole] * 5,
        out_specs=[whole] * 2,
        compiler_params=small,
        cost_estimate=pl.CostEstimate(flops=0, bytes_accessed=5 << 19, transcendentals=0),
    )(q_proj, k_proj, v_proj, short_filter, gain_row)

    total = 2 * few * parts * (devices + 1)
    conv = pl.pallas_call(
        functools.partial(conv_kernel, parts, few, chunks),
        out_shape=jax.ShapeDtypeStruct((everyone, few, rows), F32),
        in_specs=[whole] * 6,
        out_specs=whole,
        scratch_shapes=[
            pltpu.VMEM((4 * outer * (few + 1), LANES), F32),
            pltpu.VMEM((total, 6 * LANES), BF16),
            pltpu.VMEM((total, 2 * LANES), F32),
            pltpu.VMEM((total, 2 * LANES), F32),
            pltpu.VMEM((6 * everyone, LANES), F32),
        ],
        compiler_params=small,
        cost_estimate=pl.CostEstimate(flops=0, bytes_accessed=4 << 20, transcendentals=0),
    )(come, *(jnp.asarray(t) for t in tables(parts, devices, rows)))

    back = lax.all_to_all(conv, ("ctx", "dp"), 0, 0, tiled=True)
    return pl.pallas_call(
        gate_kernel,
        out_shape=jax.ShapeDtypeStruct((rows, channels), F32),
        in_specs=[whole] * 3,
        out_specs=in_hbm,
        scratch_shapes=[pltpu.VMEM((rows, channels), F32), pltpu.SemaphoreType.DMA((halves,))],
        compiler_params=small,
        cost_estimate=pl.CostEstimate(flops=0, bytes_accessed=1 << 21, transcendentals=0),
    )(back, query_seq, direct)


def fits_tiles(mesh, rows, channels):
    parts, devices = mesh.shape["dp"], mesh.shape["ctx"]
    few, rest = divmod(channels, parts * devices)
    chunks = 2 * rows // parts // 64
    return (
        rest == 0
        and few == 16
        and devices == 16
        and rows == 2 * LANES
        and parts * devices * chunks == LANES
        and chunks % 2 == 0
    )


def solution(mesh):
    placed = (
        P(("dp", "ctx"), None),
        P(("dp", "ctx"), None),
        P(("dp", "ctx"), None),
        P(),
        P(),
        P(None, "ctx", None),
    )

    def per_device(q_proj, *rest):
        form = per_device_tiled if fits_tiles(mesh, *q_proj.shape) else per_device_general
        return form(q_proj, *rest)

    return jax.shard_map(
        per_device, mesh=mesh, in_specs=placed, out_specs=P(("dp", "ctx"), None), check_vma=False
    )
```

```python
import functools
import itertools
import math

import jax
import jax.numpy as jnp
import numpy as np
from jax import lax
from jax.experimental import pallas as pl
from jax.experimental.pallas import tpu as pltpu
from jax.sharding import PartitionSpec as P

precise_mode = lax.Precision.HIGHEST
LANES = 128
BF16 = jnp.bfloat16
F32 = jnp.float32


def causal_short(signal, rim_rows, tap_gains):
    padded = jnp.concatenate([rim_rows, signal], axis=0)
    return tap_gains[0] * signal + tap_gains[1] * padded[1:-1] + tap_gains[2] * padded[:-2]


def shifted(block, axis, distance):
    devices = range(lax.axis_size(axis))
    route = [(i - distance, i) for i in devices if i - distance in devices]
    return lax.ppermute(block, axis, route)


def channel_conv(mixed_in, filter_spec, devices):
    local_rows = mixed_in.shape[0]
    seq_len = local_rows * devices
    freq_len = 2 * seq_len
    outer_len = 2 * devices
    half_inner = local_rows // 2
    columns = lax.all_to_all(mixed_in, "ctx", split_axis=1, concat_axis=0, tiled=True)
    spec_cols = lax.all_to_all(filter_spec, "ctx", split_axis=2, concat_axis=1, tiled=True)
    few_channels = columns.shape[1]
    grid = columns.reshape(half_inner, outer_len, few_channels)
    row_index = lax.iota(jnp.int32, half_inner)
    inner_freq = lax.iota(jnp.int32, local_rows)
    outer_index = lax.iota(jnp.int32, outer_len)

    def cos_sin(left, right, period):
        turns = (left[:, None] * right[None, :] % period).astype(F32) / period
        return jnp.cos(2.0 * math.pi * turns), jnp.sin(2.0 * math.pi * turns)

    first_cos, first_sin = cos_sin(row_index, inner_freq, local_rows)
    twist_cos, twist_sin = cos_sin(inner_freq, outer_index, freq_len)
    twist_cos, twist_sin = twist_cos[:, :, None], twist_sin[:, :, None]
    last_cos, last_sin = cos_sin(outer_index, outer_index, outer_len)
    dots = functools.partial(jnp.einsum, precision=precise_mode)
    section_re = dots("bk,bac->kac", first_cos, grid)
    section_im = -dots("bk,bac->kac", first_sin, grid)
    turned_re = section_re * twist_cos + section_im * twist_sin
    turned_im = section_im * twist_cos - section_re * twist_sin
    fore = "kac,aj->kjc"
    spec_re = dots(fore, turned_re, last_cos) + dots(fore, turned_im, last_sin)
    spec_im = dots(fore, turned_im, last_cos) - dots(fore, turned_re, last_sin)
    resp = jnp.transpose(spec_cols.reshape(2, outer_len, local_rows, few_channels), (0, 2, 1, 3))
    prod_re = spec_re * resp[0] - spec_im * resp[1]
    prod_im = spec_re * resp[1] + spec_im * resp[0]
    back = "kjc,aj->kac"
    undo_re = dots(back, prod_re, last_cos) - dots(back, prod_im, last_sin)
    undo_im = dots(back, prod_im, last_cos) + dots(back, prod_re, last_sin)
    back_re = undo_re * twist_cos - undo_im * twist_sin
    back_im = undo_im * twist_cos + undo_re * twist_sin
    signal_out = dots("bk,kac->bac", first_cos, back_re) - dots("bk,kac->bac", first_sin, back_im)
    conv_cols = signal_out.reshape(seq_len, few_channels) / freq_len
    return lax.all_to_all(conv_cols, "ctx", split_axis=0, concat_axis=1, tiled=True)


def per_device_general(q_proj, k_proj, v_proj, short_filter, skip_gain, filter_spec):
    devices = lax.axis_size("ctx")
    tail_rows = jnp.stack([q_proj[-2:], k_proj[-2:], v_proj[-2:]])
    rim_rows = shifted(tail_rows, "ctx", 1)
    query_seq = causal_short(q_proj, rim_rows[0], short_filter[0])
    key_seq = causal_short(k_proj, rim_rows[1], short_filter[1])
    value_seq = causal_short(v_proj, rim_rows[2], short_filter[2])
    mixed_in = key_seq * value_seq
    conv_out = channel_conv(mixed_in, filter_spec, devices)
    return query_seq * (conv_out + skip_gain[None, :] * mixed_in)


def split_np(table):
    high = table.astype(BF16)
    low = (table - high.astype(np.float64)).astype(BF16)
    return high, low


@functools.lru_cache(maxsize=None)
def tables(parts, devices, rows):
    outer, seq = 2 * devices, devices * rows
    freq = 2 * seq
    chunks = rows * 2 // parts // 64
    low_bit, chunk, dev, part = np.meshgrid(
        np.arange(2), np.arange(chunks), np.arange(devices), np.arange(parts), indexing="ij"
    )
    k = (dev * (2 * rows // outer) + part * (2 * rows // parts // outer) + 2 * chunk + low_bit).ravel()

    def angle(left, right, period):
        return 2.0 * np.pi * (np.outer(left, right) % period) / period

    s, r, half = np.arange(devices + 1), np.arange(rows), rows // 2
    twist = angle(s, r, freq)
    weight = np.where((s % 2 == 1) | (s % devices == 0), 2.0, 1.0)[:, None] / (2 * freq)
    turns = [np.cos(twist), np.sin(twist), weight * np.cos(twist), weight * np.sin(twist)]
    parity = angle([1], r[:half], rows)
    inner = angle(r[:half], k[:half] // 2, half)
    c, d = np.cos(inner), np.sin(inner)

    def tripled(table):
        high, low = split_np(table)
        return np.concatenate([high, high, low])

    fore = tripled(np.block([[c, -d], [d, c]]))
    back = tripled(np.block([[c.T, d.T], [-d.T, c.T]]))
    flip = np.concatenate([np.eye(LANES)[::-1]] * 2).astype(BF16)
    turns = np.stack(turns).astype(np.float32)
    parity = np.concatenate([np.cos(parity), np.sin(parity)]).astype(np.float32)
    return turns, parity, fore, back, flip


def split(x):
    high = x.astype(BF16)
    return high, (x - high.astype(F32)).astype(BF16)


def dot(a, b):
    return jnp.dot(a, b, preferred_element_type=F32)


def plus(a, b):
    return b if a is None else a if b is None else a + b


def minus(a, b):
    return a if b is None else -b if a is None else a - b


def times(a, scale):
    if a is None or abs(scale) < 1e-12:
        return None
    return a if scale == 1.0 else -a if scale == -1.0 else a * scale


def c_add(a, b):
    return plus(a[0], b[0]), plus(a[1], b[1])


def c_sub(a, b):
    return minus(a[0], b[0]), minus(a[1], b[1])


def c_conj(a):
    return a[0], None if a[1] is None else -a[1]


def c_turn(a, turn):
    c, d = math.cos(2 * math.pi * turn), math.sin(2 * math.pi * turn)
    c, d = (float(round(v)) if abs(v - round(v)) < 1e-12 else v for v in (c, d))
    return minus(times(a[0], c), times(a[1], d)), plus(times(a[0], d), times(a[1], c))


def fft_complex(z, sign):
    n = len(z)
    if n == 1:
        return z
    even, odd = fft_complex(z[::2], sign), fft_complex(z[1::2], sign)
    odd = [c_turn(v, sign * t / n) for t, v in enumerate(odd)]
    return [c_add(e, o) for e, o in zip(even, odd)] + [c_sub(e, o) for e, o in zip(even, odd)]


def fft_real(x):
    n = len(x)
    if n == 1:
        return [(x[0], None)]
    half = n // 2
    even, odd = fft_real(x[::2]), fft_real(x[1::2])
    out = [None] * (half + 1)
    for t, (e, o) in enumerate(zip(even, odd)):
        o = c_turn(o, -t / n)
        out[half - t] = c_conj(c_sub(e, o))
        out[t] = c_add(e, o)
    return out


def fft_to_real(z):
    half = len(z) - 1
    n = 2 * half
    if n == 2:
        return [plus(z[0][0], z[1][0]), minus(z[0][0], z[1][0])]
    even, odd = [], []
    for t in range(half // 2 + 1):
        other = c_conj(z[half - t])
        even.append(c_add(z[t], other))
        odd.append(c_turn(c_sub(z[t], other), t / n))
    out = [None] * n
    out[::2], out[1::2] = fft_to_real(even), fft_to_real(odd)
    return out


def spread(x):
    n = len(x)
    turned = [c_turn((v, None), -p / (2 * n)) for p, v in enumerate(x)]
    even, odd = fft_complex(turned[::2], -1), fft_complex(turned[1::2], -1)
    out = [None] * (n + 1)
    out[::2] = fft_real(x)
    out[1::2] = [c_add(e, c_turn(o, -t / n)) for t, (e, o) in enumerate(zip(even, odd))]
    return out


def gather(z):
    n = len(z) - 1
    ends = [(z[0][0], None), *z[2:n:2], (z[n][0], None)]
    even = fft_to_real(ends)
    odd = [None] * n
    odd[::2] = fft_complex(z[1::2], 1)
    odd[1::2] = fft_complex([c_turn(v, t / n) for t, v in enumerate(z[1::2])], 1)
    return [plus(e, c_turn(o, p / (2 * n))[0]) for p, (e, o) in enumerate(zip(even, odd))]


def causal(x, taps):
    return taps[0:1] * x + taps[1:2] * pltpu.roll(x, 1, 0) + taps[2:3] * pltpu.roll(x, 2, 0)


def block_turn(x, few):
    row = lax.broadcasted_iota(jnp.int32, x.shape, 0)
    block = lax.broadcasted_iota(jnp.int32, x.shape, 1) // few
    out = x
    for d in range(1, 8):
        moved = pltpu.roll(pltpu.roll(x, LANES - few * d, 1), d, 0)
        out = jnp.where((row - block + 8) % 8 == d, moved, out)
    return out


def place(out_ref, near, i, at, value):
    few = value.shape[0] // near
    rows = slice(at // 2, (at + few) // 2)
    out_ref[near * i : near * i + near, rows] = value.reshape(near, few // 2, 2, LANES)


def pack_kernel(
    few, chunks, part_ref, q_ref, k_ref, v_ref, taps_ref, gain_ref, spec_ref,
    out_ref, ends, keys, values, taps, gain, held, sems, held_sems, key_sems,
):
    rows = q_ref.shape[0]
    near = LANES // few
    start = pl.multiple_of(part_ref[0] * (64 * chunks), 64 * chunks)
    blocks = k_ref.shape[1] // LANES
    base = few * chunks

    def columns(i):
        return slice(LANES * i, LANES * i + LANES)

    def chunk_rows(m):
        return spec_ref.at[:, pl.ds(start + 64 * m, 64), :]

    small = [(taps_ref, taps), (gain_ref, gain)]
    small += [(q_ref.at[0:8], ends.at[0:8]), (q_ref.at[rows - 8 : rows], ends.at[8:16])]
    small = [pltpu.make_async_copy(*pair, sems.at[i]) for i, pair in enumerate(small)]
    large = [pltpu.make_async_copy(chunk_rows(m), held.at[m], held_sems.at[m]) for m in range(chunks)]
    inputs = [
        [
            pltpu.make_async_copy(src.at[:, columns(i)], dst.at[:, columns(i)], key_sems.at[j, i])
            for j, (src, dst) in enumerate(((k_ref, keys), (v_ref, values)))
        ]
        for i in range(blocks)
    ]
    for copy in (large[0], *small, *inputs[0], *large[1:], *sum(inputs[1:], [])):
        copy.start()

    def turn_chunk(m):
        large[m].wait()
        for i in range(blocks):
            both = held[m, :, :, columns(i)].reshape(LANES, LANES)
            place(out_ref, near, i, few * m, both.T)

    turn_chunk(0)
    for copy in small:
        copy.wait()
    for i in range(blocks):
        if i == 1:
            for m in range(1, chunks):
                turn_chunk(m)
        for copy in inputs[i]:
            copy.wait()
        col = columns(i)
        dests = slice(near * i, near * i + near)
        mixed_in = causal(keys[:, col], taps[1, :, col]) * causal(values[:, col], taps[2, :, col])
        for h in range(rows // LANES):
            turned = mixed_in[LANES * h : LANES * h + LANES].T
            at = base + few * h
            place(out_ref, near, i, at, turned)

        def known(first, last, j):
            t0, t1, t2 = taps[j, 0:1, col], taps[j, 1:2, col], taps[j, 2:3, col]
            own = t0 * first[0:1], t0 * first[1:2] + t1 * first[0:1]
            following = t1 * last[1:2] + t2 * last[0:1], t2 * last[1:2]
            return *own, *following

        k0, k1, next_k0, next_k1 = known(keys[0:2, col], keys[rows - 2 : rows, col], 1)
        v0, v1, next_v0, next_v1 = known(values[0:2, col], values[rows - 2 : rows, col], 2)
        q0, q1, next_q0, next_q1 = known(ends[0:2, col], ends[14:16, col], 0)
        nothing = jnp.zeros_like(q0)
        at = base + few * (rows // LANES)
        pairs = jnp.concatenate([k0, v0, k1, v1, next_k0, next_v0, next_k1, next_v1], axis=0)
        others = [q0, q1, next_q0, next_q1, gain[:, col], nothing, nothing, nothing]
        out_ref[dests, at // 2, 0, :] = block_turn(pairs, few)
        out_ref[dests, at // 2, 1, :] = block_turn(jnp.concatenate(others, axis=0), few)


def local_kernel(q_ref, k_ref, v_ref, taps_ref, gain_ref, query_ref, direct_ref):
    for i in range(q_ref.shape[1] // LANES):
        col = slice(LANES * i, LANES * i + LANES)
        query_seq = causal(q_ref[:, col], taps_ref[0, :, col])
        key_seq = causal(k_ref[:, col], taps_ref[1, :, col])
        value_seq = causal(v_ref[:, col], taps_ref[2, :, col])
        direct = query_seq * (gain_ref[:, col] * (key_seq * value_seq))
        row = lax.broadcasted_iota(jnp.int32, direct.shape, 0)
        query_ref[:, col] = jnp.where(row < 2, 1.0, query_seq)
        direct_ref[:, col] = jnp.where(row < 2, 0.0, direct)


def gate_kernel(conv_ref, query_ref, direct_ref, out_ref, gated, sems):
    few = conv_ref.shape[1]
    near = LANES // few
    leaving = []
    for h in range(conv_ref.shape[2] // LANES):
        row = slice(LANES * h, LANES * h + LANES)
        for i in range(conv_ref.shape[0] // near):
            col = slice(LANES * i, LANES * i + LANES)
            conv = conv_ref[near * i : near * i + near, :, row].reshape(LANES, LANES)
            gated[row, col] = query_ref[row, col] * conv.T + direct_ref[row, col]
        leaving.append(pltpu.make_async_copy(gated.at[row], out_ref.at[row], sems.at[h]))
        leaving[h].start()
    for copy in leaving:
        copy.wait()


def conv_kernel(
    parts, few, chunks, in_ref, turn_ref, parity_ref, fore_ref, back_ref, flip_ref, out_ref, spec, triple, freq, undo, ends
):
    devices = in_ref.shape[0] // parts
    outer = 2 * devices
    kept = devices + 1
    base, pitch = few * chunks, few + 1
    left, right = slice(0, LANES), slice(LANES, 2 * LANES)
    lane_of = lax.broadcasted_iota(jnp.int32, (few, LANES), 1)

    everyone = in_ref.shape[0]
    begins = lax.broadcasted_iota(jnp.int32, (everyone, LANES), 0) < parts
    pairs, others = in_ref[:, base // 2 + few, 0, :], in_ref[:, base // 2 + few, 1, :]

    def before(x, lanes):
        moved = pltpu.roll(pltpu.roll(x, parts, 0), LANES - lanes, 1)
        return jnp.where(begins, 0.0, moved)

    pairs = pairs + before(pairs, 4 * few)
    query = others + before(others, 2 * few)
    mixed = pairs * pltpu.roll(pairs, LANES - few, 1)
    gain = pltpu.roll(others, LANES - 4 * few, 1)
    mixed_second = pltpu.roll(mixed, LANES - 2 * few, 1)
    query_second = pltpu.roll(query, LANES - few, 1)
    direct = query * gain * mixed, query_second * gain * mixed_second
    for r, group in enumerate(((mixed, query, direct[0]), (mixed_second, query_second, direct[1]))):
        for j, x in enumerate(group):
            ends[pl.ds(2 * everyone * j + r, everyone, stride=2), :] = x
    ends_of = [ends[2 * everyone * j : 2 * everyone * (j + 1)].T[:few] for j in range(3)]

    def first_lanes(j, at):
        wide = jnp.concatenate([ends_of[j]] * (LANES // (2 * everyone)), axis=1)
        return pltpu.roll(wide, (LANES - 2 * at) % LANES, 1) if at else wide

    odd_cos, odd_sin = parity_ref[0:1], parity_ref[1:2]

    def row_of(low_bit, s, q):
        at = ((low_bit * kept + s) * parts + q) * few
        return slice(at, at + few)

    def keep(span, real, imag):
        for col, value in ((0, real), (LANES, imag)):
            high, low = split(value)
            for j, part in enumerate((high, low, high)):
                at = 2 * LANES * j + col
                triple[span, at : at + LANES] = part

    for q in range(parts):
        tiles = []
        for h in range(2):
            at = base + few * h
            x = [
                in_ref[p * parts + q, at // 2 : (at + few) // 2].reshape(few, LANES)
                for p in range(devices)
            ]
            if h == 0:
                x = [
                    jnp.where(lane_of < 2, first_lanes(0, p * parts + q), own)
                    for p, own in enumerate(x)
                ]
            tiles.append(spread(x))
        for s in range(kept):
            turned = []
            for (re, im), lane in zip((tiles[0][s], tiles[1][s]), (left, right)):
                cosine, sine = turn_ref[0, s : s + 1, lane], turn_ref[1, s : s + 1, lane]
                if im is None:
                    turned.append((re * cosine, -re * sine))
                else:
                    turned.append((re * cosine + im * sine, im * cosine - re * sine))
            keep(row_of(0, s, q), *c_add(*turned))
            re, im = c_sub(*turned)
            keep(row_of(1, s, q), re * odd_cos + im * odd_sin, im * odd_cos - re * odd_sin)

    pieces = 4
    size = freq.shape[0] // pieces
    for j in range(pieces):
        span = slice(j * size, (j + 1) * size)
        freq[span] = dot(triple[span], fore_ref[...])
        for c in range(j * few // pieces, (j + 1) * few // pieces):
            own = jnp.concatenate([in_ref[:, (few * m + c) // 2, c % 2, :] for m in range(chunks)], axis=0)
            spec[pl.ds(c, 4 * outer, stride=pitch), :] = own.T

    other = [[None, None], [None, None]]
    count = outer - kept
    for i in range(2):
        for low_bit in range(2):
            first = (2 * i + low_bit) * outer + kept
            pair = split(spec[first * pitch : (first + count) * pitch])
            other[i][low_bit] = dot(jnp.concatenate(pair, axis=1), flip_ref[...])

    def response(i, low_bit, s):
        at = ((2 * i + low_bit) * outer + s) * pitch
        own = spec[at : at + few]
        if 0 < s < devices:
            at = (outer - s - kept) * pitch
            mirror = other[i][1 - low_bit][at : at + few]
            own = own - mirror if i else own + mirror
        return own

    cuts = (0, kept // 2, kept)
    for low_bit, (begin, end) in itertools.product(range(2), zip(cuts[:-1], cuts[1:])):
        for s in range(begin, end):
            h_re, h_im = response(0, low_bit, s), response(1, low_bit, s)
            for q in range(parts):
                span = row_of(low_bit, s, q)
                re, im = freq[span, left], freq[span, right]
                keep(span, re * h_re - im * h_im, re * h_im + im * h_re)
        span = slice(row_of(low_bit, begin, 0).start, row_of(low_bit, end, 0).start)
        undo[span] = dot(triple[span], back_ref[...])

    for q in range(parts):
        tiles = [], []
        for s in range(kept):
            even, odd = row_of(0, s, q), row_of(1, s, q)
            base_value = undo[even, left], undo[even, right]
            re, im = undo[odd, left], undo[odd, right]
            odd_value = re * odd_cos - im * odd_sin, im * odd_cos + re * odd_sin
            both = c_add(base_value, odd_value), c_sub(base_value, odd_value)
            for tile, (re, im), lane in zip(tiles, both, (left, right)):
                cosine, sine = turn_ref[2, s : s + 1, lane], turn_ref[3, s : s + 1, lane]
                tile.append((re * cosine - im * sine, im * cosine + re * sine))
        for tile, lane in zip(tiles, (left, right)):
            for p, y in enumerate(gather(tile)):
                at = p * parts + q
                if lane == left:
                    finished = first_lanes(1, at) * y + first_lanes(2, at)
                    y = jnp.where(lane_of < 2, finished, y)
                out_ref[at, :, lane] = y


def per_device_tiled(q_proj, k_proj, v_proj, short_filter, skip_gain, filter_spec):
    parts, devices = lax.axis_size("dp"), lax.axis_size("ctx")
    everyone = parts * devices
    rows, channels = q_proj.shape
    few = channels // everyone
    chunks = 2 * rows // parts // 64
    halves = rows // LANES
    depth = few * (chunks + halves) + 2
    outer = 2 * devices
    whole = pl.BlockSpec(memory_space=pltpu.VMEM)
    in_hbm = pl.BlockSpec(memory_space=pltpu.HBM)
    small = pltpu.CompilerParams(vmem_limit_bytes=16 << 20)
    gain_row = skip_gain[None, :]

    part = lax.axis_index("dp").reshape(1)
    sources = (q_proj, k_proj, v_proj, short_filter, gain_row, filter_spec)
    sent = pl.pallas_call(
        functools.partial(pack_kernel, few, chunks),
        out_shape=jax.ShapeDtypeStruct((everyone, depth // 2, 2, LANES), F32),
        in_specs=[pl.BlockSpec(memory_space=pltpu.SMEM)] + [in_hbm] * 6,
        out_specs=whole,
        compiler_params=small,
        scratch_shapes=[
            pltpu.VMEM((16, channels), F32),
            pltpu.VMEM((rows, channels), F32),
            pltpu.VMEM((rows, channels), F32),
            pltpu.VMEM((3, 3, channels), F32),
            pltpu.VMEM((1, channels), F32),
            pltpu.VMEM((chunks, 2, 64, channels), F32),
            pltpu.SemaphoreType.DMA((4,)),
            pltpu.SemaphoreType.DMA((chunks,)),
            pltpu.SemaphoreType.DMA((2, channels // LANES)),
        ],
        cost_estimate=pl.CostEstimate(flops=0, bytes_accessed=1 << 22, transcendentals=0),
    )(part, *(pltpu.with_memory_space_constraint(x, pltpu.HBM) for x in sources))

    come = lax.all_to_all(sent, ("ctx", "dp"), 0, 0, tiled=True)

    query_seq, direct = pl.pallas_call(
        local_kernel,
        out_shape=[jax.ShapeDtypeStruct((rows, channels), F32)] * 2,
        in_specs=[whole] * 5,
        out_specs=[whole] * 2,
        compiler_params=small,
        cost_estimate=pl.CostEstimate(flops=0, bytes_accessed=5 << 19, transcendentals=0),
    )(q_proj, k_proj, v_proj, short_filter, gain_row)

    total = 2 * few * parts * (devices + 1)
    conv = pl.pallas_call(
        functools.partial(conv_kernel, parts, few, chunks),
        out_shape=jax.ShapeDtypeStruct((everyone, few, rows), F32),
        in_specs=[whole] * 6,
        out_specs=whole,
        scratch_shapes=[
            pltpu.VMEM((4 * outer * (few + 1), LANES), F32),
            pltpu.VMEM((total, 6 * LANES), BF16),
            pltpu.VMEM((total, 2 * LANES), F32),
            pltpu.VMEM((total, 2 * LANES), F32),
            pltpu.VMEM((6 * everyone, LANES), F32),
        ],
        compiler_params=small,
        cost_estimate=pl.CostEstimate(flops=0, bytes_accessed=4 << 20, transcendentals=0),
    )(come, *(jnp.asarray(t) for t in tables(parts, devices, rows)))

    back = lax.all_to_all(conv, ("ctx", "dp"), 0, 0, tiled=True)
    return pl.pallas_call(
        gate_kernel,
        out_shape=jax.ShapeDtypeStruct((rows, channels), F32),
        in_specs=[whole] * 3,
        out_specs=in_hbm,
        scratch_shapes=[pltpu.VMEM((rows, channels), F32), pltpu.SemaphoreType.DMA((halves,))],
        compiler_params=small,
        cost_estimate=pl.CostEstimate(flops=0, bytes_accessed=1 << 21, transcendentals=0),
    )(back, query_seq, direct)


def fits_tiles(mesh, rows, channels):
    parts, devices = mesh.shape["dp"], mesh.shape["ctx"]
    few, rest = divmod(channels, parts * devices)
    chunks = 2 * rows // parts // 64
    return (
        rest == 0
        and few == 16
        and devices == 16
        and rows == 2 * LANES
        and parts * devices * chunks == LANES
        and chunks % 2 == 0
    )


def solution(mesh):
    placed = (
        P(("dp", "ctx"), None),
        P(("dp", "ctx"), None),
        P(("dp", "ctx"), None),
        P(),
        P(),
        P(None, "ctx", None),
    )

    def per_device(q_proj, *rest):
        form = per_device_tiled if fits_tiles(mesh, *q_proj.shape) else per_device_general
        return form(q_proj, *rest)

    return jax.shard_map(
        per_device, mesh=mesh, in_specs=placed, out_specs=P(("dp", "ctx"), None), check_vma=False
    )
```

```python
import functools
import itertools
import math

import jax
import jax.numpy as jnp
import numpy as np
from jax import lax
from jax.experimental import pallas as pl
from jax.experimental.pallas import tpu as pltpu
from jax.sharding import PartitionSpec as P

precise_mode = lax.Precision.HIGHEST
LANES = 128
BF16 = jnp.bfloat16
F32 = jnp.float32


def causal_short(signal, rim_rows, tap_gains):
    padded = jnp.concatenate([rim_rows, signal], axis=0)
    return tap_gains[0] * signal + tap_gains[1] * padded[1:-1] + tap_gains[2] * padded[:-2]


def shifted(block, axis, distance):
    devices = range(lax.axis_size(axis))
    route = [(i - distance, i) for i in devices if i - distance in devices]
    return lax.ppermute(block, axis, route)


def channel_conv(mixed_in, filter_spec, devices):
    local_rows = mixed_in.shape[0]
    seq_len = local_rows * devices
    freq_len = 2 * seq_len
    outer_len = 2 * devices
    half_inner = local_rows // 2
    columns = lax.all_to_all(mixed_in, "ctx", split_axis=1, concat_axis=0, tiled=True)
    spec_cols = lax.all_to_all(filter_spec, "ctx", split_axis=2, concat_axis=1, tiled=True)
    few_channels = columns.shape[1]
    grid = columns.reshape(half_inner, outer_len, few_channels)
    row_index = lax.iota(jnp.int32, half_inner)
    inner_freq = lax.iota(jnp.int32, local_rows)
    outer_index = lax.iota(jnp.int32, outer_len)

    def cos_sin(left, right, period):
        turns = (left[:, None] * right[None, :] % period).astype(F32) / period
        return jnp.cos(2.0 * math.pi * turns), jnp.sin(2.0 * math.pi * turns)

    first_cos, first_sin = cos_sin(row_index, inner_freq, local_rows)
    twist_cos, twist_sin = cos_sin(inner_freq, outer_index, freq_len)
    twist_cos, twist_sin = twist_cos[:, :, None], twist_sin[:, :, None]
    last_cos, last_sin = cos_sin(outer_index, outer_index, outer_len)
    dots = functools.partial(jnp.einsum, precision=precise_mode)
    section_re = dots("bk,bac->kac", first_cos, grid)
    section_im = -dots("bk,bac->kac", first_sin, grid)
    turned_re = section_re * twist_cos + section_im * twist_sin
    turned_im = section_im * twist_cos - section_re * twist_sin
    fore = "kac,aj->kjc"
    spec_re = dots(fore, turned_re, last_cos) + dots(fore, turned_im, last_sin)
    spec_im = dots(fore, turned_im, last_cos) - dots(fore, turned_re, last_sin)
    resp = jnp.transpose(spec_cols.reshape(2, outer_len, local_rows, few_channels), (0, 2, 1, 3))
    prod_re = spec_re * resp[0] - spec_im * resp[1]
    prod_im = spec_re * resp[1] + spec_im * resp[0]
    back = "kjc,aj->kac"
    undo_re = dots(back, prod_re, last_cos) - dots(back, prod_im, last_sin)
    undo_im = dots(back, prod_im, last_cos) + dots(back, prod_re, last_sin)
    back_re = undo_re * twist_cos - undo_im * twist_sin
    back_im = undo_im * twist_cos + undo_re * twist_sin
    signal_out = dots("bk,kac->bac", first_cos, back_re) - dots("bk,kac->bac", first_sin, back_im)
    conv_cols = signal_out.reshape(seq_len, few_channels) / freq_len
    return lax.all_to_all(conv_cols, "ctx", split_axis=0, concat_axis=1, tiled=True)


def per_device_general(q_proj, k_proj, v_proj, short_filter, skip_gain, filter_spec):
    devices = lax.axis_size("ctx")
    tail_rows = jnp.stack([q_proj[-2:], k_proj[-2:], v_proj[-2:]])
    rim_rows = shifted(tail_rows, "ctx", 1)
    query_seq = causal_short(q_proj, rim_rows[0], short_filter[0])
    key_seq = causal_short(k_proj, rim_rows[1], short_filter[1])
    value_seq = causal_short(v_proj, rim_rows[2], short_filter[2])
    mixed_in = key_seq * value_seq
    conv_out = channel_conv(mixed_in, filter_spec, devices)
    return query_seq * (conv_out + skip_gain[None, :] * mixed_in)


def split_np(table):
    high = table.astype(BF16)
    low = (table - high.astype(np.float64)).astype(BF16)
    return high, low


@functools.lru_cache(maxsize=None)
def tables(parts, devices, rows):
    outer, seq = 2 * devices, devices * rows
    freq = 2 * seq
    chunks = rows * 2 // parts // 64
    low_bit, chunk, dev, part = np.meshgrid(
        np.arange(2), np.arange(chunks), np.arange(devices), np.arange(parts), indexing="ij"
    )
    k = (dev * (2 * rows // outer) + part * (2 * rows // parts // outer) + 2 * chunk + low_bit).ravel()

    def angle(left, right, period):
        return 2.0 * np.pi * (np.outer(left, right) % period) / period

    s, r, half = np.arange(devices + 1), np.arange(rows), rows // 2
    twist = angle(s, r, freq)
    weight = np.where((s % 2 == 1) | (s % devices == 0), 2.0, 1.0)[:, None] / (2 * freq)
    turns = [np.cos(twist), np.sin(twist), weight * np.cos(twist), weight * np.sin(twist)]
    parity = angle([1], r[:half], rows)
    inner = angle(r[:half], k[:half] // 2, half)
    c, d = np.cos(inner), np.sin(inner)

    def tripled(table):
        high, low = split_np(table)
        return np.concatenate([high, high, low])

    fore = tripled(np.block([[c, -d], [d, c]]))
    back = tripled(np.block([[c.T, d.T], [-d.T, c.T]]))
    flip = np.concatenate([np.eye(LANES)[::-1]] * 2).astype(BF16)
    turns = np.stack(turns).astype(np.float32)
    parity = np.concatenate([np.cos(parity), np.sin(parity)]).astype(np.float32)
    return turns, parity, fore, back, flip


def split(x):
    high = x.astype(BF16)
    return high, (x - high.astype(F32)).astype(BF16)


def dot(a, b):
    return jnp.dot(a, b, preferred_element_type=F32)


def plus(a, b):
    return b if a is None else a if b is None else a + b


def minus(a, b):
    return a if b is None else -b if a is None else a - b


def times(a, scale):
    if a is None or abs(scale) < 1e-12:
        return None
    return a if scale == 1.0 else -a if scale == -1.0 else a * scale


def c_add(a, b):
    return plus(a[0], b[0]), plus(a[1], b[1])


def c_sub(a, b):
    return minus(a[0], b[0]), minus(a[1], b[1])


def c_conj(a):
    return a[0], None if a[1] is None else -a[1]


def c_turn(a, turn):
    c, d = math.cos(2 * math.pi * turn), math.sin(2 * math.pi * turn)
    c, d = (float(round(v)) if abs(v - round(v)) < 1e-12 else v for v in (c, d))
    return minus(times(a[0], c), times(a[1], d)), plus(times(a[0], d), times(a[1], c))


def fft_complex(z, sign):
    n = len(z)
    if n == 1:
        return z
    even, odd = fft_complex(z[::2], sign), fft_complex(z[1::2], sign)
    odd = [c_turn(v, sign * t / n) for t, v in enumerate(odd)]
    return [c_add(e, o) for e, o in zip(even, odd)] + [c_sub(e, o) for e, o in zip(even, odd)]


def fft_real(x):
    n = len(x)
    if n == 1:
        return [(x[0], None)]
    half = n // 2
    even, odd = fft_real(x[::2]), fft_real(x[1::2])
    out = [None] * (half + 1)
    for t, (e, o) in enumerate(zip(even, odd)):
        o = c_turn(o, -t / n)
        out[half - t] = c_conj(c_sub(e, o))
        out[t] = c_add(e, o)
    return out


def fft_to_real(z):
    half = len(z) - 1
    n = 2 * half
    if n == 2:
        return [plus(z[0][0], z[1][0]), minus(z[0][0], z[1][0])]
    even, odd = [], []
    for t in range(half // 2 + 1):
        other = c_conj(z[half - t])
        even.append(c_add(z[t], other))
        odd.append(c_turn(c_sub(z[t], other), t / n))
    out = [None] * n
    out[::2], out[1::2] = fft_to_real(even), fft_to_real(odd)
    return out


def spread(x):
    n = len(x)
    turned = [c_turn((v, None), -p / (2 * n)) for p, v in enumerate(x)]
    even, odd = fft_complex(turned[::2], -1), fft_complex(turned[1::2], -1)
    out = [None] * (n + 1)
    out[::2] = fft_real(x)
    out[1::2] = [c_add(e, c_turn(o, -t / n)) for t, (e, o) in enumerate(zip(even, odd))]
    return out


def gather(z):
    n = len(z) - 1
    ends = [(z[0][0], None), *z[2:n:2], (z[n][0], None)]
    even = fft_to_real(ends)
    odd = [None] * n
    odd[::2] = fft_complex(z[1::2], 1)
    odd[1::2] = fft_complex([c_turn(v, t / n) for t, v in enumerate(z[1::2])], 1)
    return [plus(e, c_turn(o, p / (2 * n))[0]) for p, (e, o) in enumerate(zip(even, odd))]


def causal(x, taps):
    return taps[0:1] * x + taps[1:2] * pltpu.roll(x, 1, 0) + taps[2:3] * pltpu.roll(x, 2, 0)


def block_turn(x, few):
    row = lax.broadcasted_iota(jnp.int32, x.shape, 0)
    block = lax.broadcasted_iota(jnp.int32, x.shape, 1) // few
    out = x
    for d in range(1, 8):
        moved = pltpu.roll(pltpu.roll(x, LANES - few * d, 1), d, 0)
        out = jnp.where((row - block + 8) % 8 == d, moved, out)
    return out


def place(out_ref, near, i, at, value):
    few = value.shape[0] // near
    rows = slice(at // 2, (at + few) // 2)
    out_ref[near * i : near * i + near, rows] = value.reshape(near, few // 2, 2, LANES)


def pack_kernel(
    few, chunks, part_ref, q_ref, k_ref, v_ref, taps_ref, gain_ref, spec_ref,
    out_ref, ends, keys, values, taps, gain, held, sems, held_sems, key_sems,
):
    rows = q_ref.shape[0]
    near = LANES // few
    start = pl.multiple_of(part_ref[0] * (64 * chunks), 64 * chunks)
    blocks = k_ref.shape[1] // LANES
    base = few * chunks

    def columns(i):
        return slice(LANES * i, LANES * i + LANES)

    def chunk_rows(m):
        return spec_ref.at[:, pl.ds(start + 64 * m, 64), :]

    small = [(taps_ref, taps), (gain_ref, gain)]
    small += [(q_ref.at[0:8], ends.at[0:8]), (q_ref.at[rows - 8 : rows], ends.at[8:16])]
    small = [pltpu.make_async_copy(*pair, sems.at[i]) for i, pair in enumerate(small)]
    large = [pltpu.make_async_copy(chunk_rows(m), held.at[m], held_sems.at[m]) for m in range(chunks)]
    inputs = [
        [
            pltpu.make_async_copy(src.at[:, columns(i)], dst.at[:, columns(i)], key_sems.at[j, i])
            for j, (src, dst) in enumerate(((k_ref, keys), (v_ref, values)))
        ]
        for i in range(blocks)
    ]
    for copy in (large[0], *small, *inputs[0], *large[1:], *sum(inputs[1:], [])):
        copy.start()

    def turn_chunk(m):
        large[m].wait()
        for i in range(blocks):
            both = held[m, :, :, columns(i)].reshape(LANES, LANES)
            place(out_ref, near, i, few * m, both.T)

    turn_chunk(0)
    for copy in small:
        copy.wait()
    for i in range(blocks):
        if i == 1:
            for m in range(1, chunks):
                turn_chunk(m)
        for copy in inputs[i]:
            copy.wait()
        col = columns(i)
        dests = slice(near * i, near * i + near)
        mixed_in = causal(keys[:, col], taps[1, :, col]) * causal(values[:, col], taps[2, :, col])
        for h in range(rows // LANES):
            turned = mixed_in[LANES * h : LANES * h + LANES].T
            at = base + few * h
            place(out_ref, near, i, at, turned)

        def known(first, last, j):
            t0, t1, t2 = taps[j, 0:1, col], taps[j, 1:2, col], taps[j, 2:3, col]
            own = t0 * first[0:1], t0 * first[1:2] + t1 * first[0:1]
            following = t1 * last[1:2] + t2 * last[0:1], t2 * last[1:2]
            return *own, *following

        k0, k1, next_k0, next_k1 = known(keys[0:2, col], keys[rows - 2 : rows, col], 1)
        v0, v1, next_v0, next_v1 = known(values[0:2, col], values[rows - 2 : rows, col], 2)
        q0, q1, next_q0, next_q1 = known(ends[0:2, col], ends[14:16, col], 0)
        nothing = jnp.zeros_like(q0)
        at = base + few * (rows // LANES)
        pairs = jnp.concatenate([k0, v0, k1, v1, next_k0, next_v0, next_k1, next_v1], axis=0)
        others = [q0, q1, next_q0, next_q1, gain[:, col], nothing, nothing, nothing]
        out_ref[dests, at // 2, 0, :] = block_turn(pairs, few)
        out_ref[dests, at // 2, 1, :] = block_turn(jnp.concatenate(others, axis=0), few)


def local_kernel(q_ref, k_ref, v_ref, taps_ref, gain_ref, query_ref, direct_ref):
    for i in range(q_ref.shape[1] // LANES):
        col = slice(LANES * i, LANES * i + LANES)
        query_seq = causal(q_ref[:, col], taps_ref[0, :, col])
        key_seq = causal(k_ref[:, col], taps_ref[1, :, col])
        value_seq = causal(v_ref[:, col], taps_ref[2, :, col])
        direct = query_seq * (gain_ref[:, col] * (key_seq * value_seq))
        row = lax.broadcasted_iota(jnp.int32, direct.shape, 0)
        query_ref[:, col] = jnp.where(row < 2, 1.0, query_seq)
        direct_ref[:, col] = jnp.where(row < 2, 0.0, direct)


def gate_kernel(conv_ref, query_ref, direct_ref, out_ref, gated, sems):
    few = conv_ref.shape[1]
    near = LANES // few
    leaving = []
    for h in range(conv_ref.shape[2] // LANES):
        row = slice(LANES * h, LANES * h + LANES)
        for i in range(conv_ref.shape[0] // near):
            col = slice(LANES * i, LANES * i + LANES)
            conv = conv_ref[near * i : near * i + near, :, row].reshape(LANES, LANES)
            gated[row, col] = query_ref[row, col] * conv.T + direct_ref[row, col]
        leaving.append(pltpu.make_async_copy(gated.at[row], out_ref.at[row], sems.at[h]))
        leaving[h].start()
    for copy in leaving:
        copy.wait()


def conv_kernel(
    parts, few, chunks, in_ref, turn_ref, parity_ref, fore_ref, back_ref, flip_ref, out_ref, spec, triple, freq, undo, ends, blocks
):
    devices = in_ref.shape[0] // parts
    outer = 2 * devices
    kept = devices + 1
    base, pitch = few * chunks, few + 1
    left, right = slice(0, LANES), slice(LANES, 2 * LANES)
    lane_of = lax.broadcasted_iota(jnp.int32, (few, LANES), 1)

    everyone = in_ref.shape[0]
    begins = lax.broadcasted_iota(jnp.int32, (everyone, LANES), 0) < parts
    pairs, others = in_ref[:, base // 2 + few, 0, :], in_ref[:, base // 2 + few, 1, :]

    def before(x, lanes):
        moved = pltpu.roll(pltpu.roll(x, parts, 0), LANES - lanes, 1)
        return jnp.where(begins, 0.0, moved)

    pairs = pairs + before(pairs, 4 * few)
    query = others + before(others, 2 * few)
    mixed = pairs * pltpu.roll(pairs, LANES - few, 1)
    gain = pltpu.roll(others, LANES - 4 * few, 1)
    mixed_second = pltpu.roll(mixed, LANES - 2 * few, 1)
    query_second = pltpu.roll(query, LANES - few, 1)
    direct = query * gain * mixed, query_second * gain * mixed_second
    for r, group in enumerate(((mixed, query, direct[0]), (mixed_second, query_second, direct[1]))):
        for j, x in enumerate(group):
            ends[pl.ds(2 * everyone * j + r, everyone, stride=2), :] = x
    ends_of = [ends[2 * everyone * j : 2 * everyone * (j + 1)].T[:few] for j in range(3)]

    def first_lanes(j, at):
        wide = jnp.concatenate([ends_of[j]] * (LANES // (2 * everyone)), axis=1)
        return pltpu.roll(wide, (LANES - 2 * at) % LANES, 1) if at else wide

    odd_cos, odd_sin = parity_ref[0:1], parity_ref[1:2]

    def row_of(low_bit, s, q):
        at = ((low_bit * kept + s) * parts + q) * few
        return slice(at, at + few)

    def keep(span, real, imag):
        for col, value in ((0, real), (LANES, imag)):
            high, low = split(value)
            for j, part in enumerate((high, low, high)):
                at = 2 * LANES * j + col
                triple[span, at : at + LANES] = part

    for j in range(2 * few):
        h, c = divmod(j, few)
        span = pl.ds(h * everyone * pitch + c, everyone, stride=pitch)
        blocks[span, :] = in_ref[:, (base + j) // 2, j % 2, :]

    for q in range(parts):
        tiles = []
        for h in range(2):
            first = [(h * everyone + p * parts + q) * pitch for p in range(devices)]
            x = [blocks[at : at + few] for at in first]
            if h == 0:
                x = [
                    jnp.where(lane_of < 2, first_lanes(0, p * parts + q), own)
                    for p, own in enumerate(x)
                ]
            tiles.append(spread(x))
        for s in range(kept):
            turned = []
            for (re, im), lane in zip((tiles[0][s], tiles[1][s]), (left, right)):
                cosine, sine = turn_ref[0, s : s + 1, lane], turn_ref[1, s : s + 1, lane]
                if im is None:
                    turned.append((re * cosine, -re * sine))
                else:
                    turned.append((re * cosine + im * sine, im * cosine - re * sine))
            keep(row_of(0, s, q), *c_add(*turned))
            re, im = c_sub(*turned)
            keep(row_of(1, s, q), re * odd_cos + im * odd_sin, im * odd_cos - re * odd_sin)

    pieces = 4
    size = freq.shape[0] // pieces
    for j in range(pieces):
        span = slice(j * size, (j + 1) * size)
        freq[span] = dot(triple[span], fore_ref[...])
        for c in range(j * few // pieces, (j + 1) * few // pieces):
            own = jnp.concatenate([in_ref[:, (few * m + c) // 2, c % 2, :] for m in range(chunks)], axis=0)
            spec[pl.ds(c, 4 * outer, stride=pitch), :] = own.T

    other = [[None, None], [None, None]]
    count = outer - kept
    for i in range(2):
        for low_bit in range(2):
            first = (2 * i + low_bit) * outer + kept
            pair = split(spec[first * pitch : (first + count) * pitch])
            other[i][low_bit] = dot(jnp.concatenate(pair, axis=1), flip_ref[...])

    def response(i, low_bit, s):
        at = ((2 * i + low_bit) * outer + s) * pitch
        own = spec[at : at + few]
        if 0 < s < devices:
            at = (outer - s - kept) * pitch
            mirror = other[i][1 - low_bit][at : at + few]
            own = own - mirror if i else own + mirror
        return own

    cuts = (0, kept // 2, kept)
    for low_bit, (begin, end) in itertools.product(range(2), zip(cuts[:-1], cuts[1:])):
        for s in range(begin, end):
            h_re, h_im = response(0, low_bit, s), response(1, low_bit, s)
            for q in range(parts):
                span = row_of(low_bit, s, q)
                re, im = freq[span, left], freq[span, right]
                keep(span, re * h_re - im * h_im, re * h_im + im * h_re)
        span = slice(row_of(low_bit, begin, 0).start, row_of(low_bit, end, 0).start)
        undo[span] = dot(triple[span], back_ref[...])

    for q in range(parts):
        tiles = [], []
        for s in range(kept):
            even, odd = row_of(0, s, q), row_of(1, s, q)
            base_value = undo[even, left], undo[even, right]
            re, im = undo[odd, left], undo[odd, right]
            odd_value = re * odd_cos - im * odd_sin, im * odd_cos + re * odd_sin
            both = c_add(base_value, odd_value), c_sub(base_value, odd_value)
            for tile, (re, im), lane in zip(tiles, both, (left, right)):
                cosine, sine = turn_ref[2, s : s + 1, lane], turn_ref[3, s : s + 1, lane]
                tile.append((re * cosine - im * sine, im * cosine + re * sine))
        for tile, lane in zip(tiles, (left, right)):
            for p, y in enumerate(gather(tile)):
                at = p * parts + q
                if lane == left:
                    finished = first_lanes(1, at) * y + first_lanes(2, at)
                    y = jnp.where(lane_of < 2, finished, y)
                out_ref[at, :, lane] = y


def per_device_tiled(q_proj, k_proj, v_proj, short_filter, skip_gain, filter_spec):
    parts, devices = lax.axis_size("dp"), lax.axis_size("ctx")
    everyone = parts * devices
    rows, channels = q_proj.shape
    few = channels // everyone
    chunks = 2 * rows // parts // 64
    halves = rows // LANES
    depth = few * (chunks + halves) + 2
    outer = 2 * devices
    whole = pl.BlockSpec(memory_space=pltpu.VMEM)
    in_hbm = pl.BlockSpec(memory_space=pltpu.HBM)
    small = pltpu.CompilerParams(vmem_limit_bytes=16 << 20)
    gain_row = skip_gain[None, :]

    part = lax.axis_index("dp").reshape(1)
    sources = (q_proj, k_proj, v_proj, short_filter, gain_row, filter_spec)
    sent = pl.pallas_call(
        functools.partial(pack_kernel, few, chunks),
        out_shape=jax.ShapeDtypeStruct((everyone, depth // 2, 2, LANES), F32),
        in_specs=[pl.BlockSpec(memory_space=pltpu.SMEM)] + [in_hbm] * 6,
        out_specs=whole,
        compiler_params=small,
        scratch_shapes=[
            pltpu.VMEM((16, channels), F32),
            pltpu.VMEM((rows, channels), F32),
            pltpu.VMEM((rows, channels), F32),
            pltpu.VMEM((3, 3, channels), F32),
            pltpu.VMEM((1, channels), F32),
            pltpu.VMEM((chunks, 2, 64, channels), F32),
            pltpu.SemaphoreType.DMA((4,)),
            pltpu.SemaphoreType.DMA((chunks,)),
            pltpu.SemaphoreType.DMA((2, channels // LANES)),
        ],
        cost_estimate=pl.CostEstimate(flops=0, bytes_accessed=1 << 22, transcendentals=0),
    )(part, *(pltpu.with_memory_space_constraint(x, pltpu.HBM) for x in sources))

    come = lax.all_to_all(sent, ("ctx", "dp"), 0, 0, tiled=True)

    query_seq, direct = pl.pallas_call(
        local_kernel,
        out_shape=[jax.ShapeDtypeStruct((rows, channels), F32)] * 2,
        in_specs=[whole] * 5,
        out_specs=[whole] * 2,
        compiler_params=small,
        cost_estimate=pl.CostEstimate(flops=0, bytes_accessed=5 << 19, transcendentals=0),
    )(q_proj, k_proj, v_proj, short_filter, gain_row)

    total = 2 * few * parts * (devices + 1)
    conv = pl.pallas_call(
        functools.partial(conv_kernel, parts, few, chunks),
        out_shape=jax.ShapeDtypeStruct((everyone, few, rows), F32),
        in_specs=[whole] * 6,
        out_specs=whole,
        scratch_shapes=[
            pltpu.VMEM((4 * outer * (few + 1), LANES), F32),
            pltpu.VMEM((total, 6 * LANES), BF16),
            pltpu.VMEM((total, 2 * LANES), F32),
            pltpu.VMEM((total, 2 * LANES), F32),
            pltpu.VMEM((6 * everyone, LANES), F32),
            pltpu.VMEM((2 * everyone * (few + 1), LANES), F32),
        ],
        compiler_params=small,
        cost_estimate=pl.CostEstimate(flops=0, bytes_accessed=4 << 20, transcendentals=0),
    )(come, *(jnp.asarray(t) for t in tables(parts, devices, rows)))

    back = lax.all_to_all(conv, ("ctx", "dp"), 0, 0, tiled=True)
    return pl.pallas_call(
        gate_kernel,
        out_shape=jax.ShapeDtypeStruct((rows, channels), F32),
        in_specs=[whole] * 3,
        out_specs=in_hbm,
        scratch_shapes=[pltpu.VMEM((rows, channels), F32), pltpu.SemaphoreType.DMA((halves,))],
        compiler_params=small,
        cost_estimate=pl.CostEstimate(flops=0, bytes_accessed=1 << 21, transcendentals=0),
    )(back, query_seq, direct)


def fits_tiles(mesh, rows, channels):
    parts, devices = mesh.shape["dp"], mesh.shape["ctx"]
    few, rest = divmod(channels, parts * devices)
    chunks = 2 * rows // parts // 64
    return (
        rest == 0
        and few == 16
        and devices == 16
        and rows == 2 * LANES
        and parts * devices * chunks == LANES
        and chunks % 2 == 0
    )


def solution(mesh):
    placed = (
        P(("dp", "ctx"), None),
        P(("dp", "ctx"), None),
        P(("dp", "ctx"), None),
        P(),
        P(),
        P(None, "ctx", None),
    )

    def per_device(q_proj, *rest):
        form = per_device_tiled if fits_tiles(mesh, *q_proj.shape) else per_device_general
        return form(q_proj, *rest)

    return jax.shard_map(
        per_device, mesh=mesh, in_specs=placed, out_specs=P(("dp", "ctx"), None), check_vma=False
    )
```

```python
import functools
import itertools
import math

import jax
import jax.numpy as jnp
import numpy as np
from jax import lax
from jax.experimental import pallas as pl
from jax.experimental.pallas import tpu as pltpu
from jax.sharding import PartitionSpec as P

precise_mode = lax.Precision.HIGHEST
LANES = 128
BF16 = jnp.bfloat16
F32 = jnp.float32


def causal_short(signal, rim_rows, tap_gains):
    padded = jnp.concatenate([rim_rows, signal], axis=0)
    return tap_gains[0] * signal + tap_gains[1] * padded[1:-1] + tap_gains[2] * padded[:-2]


def shifted(block, axis, distance):
    devices = range(lax.axis_size(axis))
    route = [(i - distance, i) for i in devices if i - distance in devices]
    return lax.ppermute(block, axis, route)


def channel_conv(mixed_in, filter_spec, devices):
    local_rows = mixed_in.shape[0]
    seq_len = local_rows * devices
    freq_len = 2 * seq_len
    outer_len = 2 * devices
    half_inner = local_rows // 2
    columns = lax.all_to_all(mixed_in, "ctx", split_axis=1, concat_axis=0, tiled=True)
    spec_cols = lax.all_to_all(filter_spec, "ctx", split_axis=2, concat_axis=1, tiled=True)
    few_channels = columns.shape[1]
    grid = columns.reshape(half_inner, outer_len, few_channels)
    row_index = lax.iota(jnp.int32, half_inner)
    inner_freq = lax.iota(jnp.int32, local_rows)
    outer_index = lax.iota(jnp.int32, outer_len)

    def cos_sin(left, right, period):
        turns = (left[:, None] * right[None, :] % period).astype(F32) / period
        return jnp.cos(2.0 * math.pi * turns), jnp.sin(2.0 * math.pi * turns)

    first_cos, first_sin = cos_sin(row_index, inner_freq, local_rows)
    twist_cos, twist_sin = cos_sin(inner_freq, outer_index, freq_len)
    twist_cos, twist_sin = twist_cos[:, :, None], twist_sin[:, :, None]
    last_cos, last_sin = cos_sin(outer_index, outer_index, outer_len)
    dots = functools.partial(jnp.einsum, precision=precise_mode)
    section_re = dots("bk,bac->kac", first_cos, grid)
    section_im = -dots("bk,bac->kac", first_sin, grid)
    turned_re = section_re * twist_cos + section_im * twist_sin
    turned_im = section_im * twist_cos - section_re * twist_sin
    fore = "kac,aj->kjc"
    spec_re = dots(fore, turned_re, last_cos) + dots(fore, turned_im, last_sin)
    spec_im = dots(fore, turned_im, last_cos) - dots(fore, turned_re, last_sin)
    resp = jnp.transpose(spec_cols.reshape(2, outer_len, local_rows, few_channels), (0, 2, 1, 3))
    prod_re = spec_re * resp[0] - spec_im * resp[1]
    prod_im = spec_re * resp[1] + spec_im * resp[0]
    back = "kjc,aj->kac"
    undo_re = dots(back, prod_re, last_cos) - dots(back, prod_im, last_sin)
    undo_im = dots(back, prod_im, last_cos) + dots(back, prod_re, last_sin)
    back_re = undo_re * twist_cos - undo_im * twist_sin
    back_im = undo_im * twist_cos + undo_re * twist_sin
    signal_out = dots("bk,kac->bac", first_cos, back_re) - dots("bk,kac->bac", first_sin, back_im)
    conv_cols = signal_out.reshape(seq_len, few_channels) / freq_len
    return lax.all_to_all(conv_cols, "ctx", split_axis=0, concat_axis=1, tiled=True)


def per_device_general(q_proj, k_proj, v_proj, short_filter, skip_gain, filter_spec):
    devices = lax.axis_size("ctx")
    tail_rows = jnp.stack([q_proj[-2:], k_proj[-2:], v_proj[-2:]])
    rim_rows = shifted(tail_rows, "ctx", 1)
    query_seq = causal_short(q_proj, rim_rows[0], short_filter[0])
    key_seq = causal_short(k_proj, rim_rows[1], short_filter[1])
    value_seq = causal_short(v_proj, rim_rows[2], short_filter[2])
    mixed_in = key_seq * value_seq
    conv_out = channel_conv(mixed_in, filter_spec, devices)
    return query_seq * (conv_out + skip_gain[None, :] * mixed_in)


def split_np(table):
    high = table.astype(BF16)
    low = (table - high.astype(np.float64)).astype(BF16)
    return high, low


@functools.lru_cache(maxsize=None)
def tables(parts, devices, rows):
    outer, seq = 2 * devices, devices * rows
    freq = 2 * seq
    chunks = rows * 2 // parts // 64
    low_bit, chunk, dev, part = np.meshgrid(
        np.arange(2), np.arange(chunks), np.arange(devices), np.arange(parts), indexing="ij"
    )
    k = (dev * (2 * rows // outer) + part * (2 * rows // parts // outer) + 2 * chunk + low_bit).ravel()

    def angle(left, right, period):
        return 2.0 * np.pi * (np.outer(left, right) % period) / period

    s, r, half = np.arange(devices + 1), np.arange(rows), rows // 2
    twist = angle(s, r, freq)
    weight = np.where((s % 2 == 1) | (s % devices == 0), 2.0, 1.0)[:, None] / (2 * freq)
    turns = [np.cos(twist), np.sin(twist), weight * np.cos(twist), weight * np.sin(twist)]
    parity = angle([1], r[:half], rows)
    inner = angle(r[:half], k[:half] // 2, half)
    c, d = np.cos(inner), np.sin(inner)

    def tripled(table):
        high, low = split_np(table)
        return np.concatenate([high, high, low])

    fore = tripled(np.block([[c, -d], [d, c]]))
    back = tripled(np.block([[c.T, d.T], [-d.T, c.T]]))
    flip = np.concatenate([np.eye(LANES)[::-1]] * 2).astype(BF16)
    turns = np.stack(turns).astype(np.float32)
    parity = np.concatenate([np.cos(parity), np.sin(parity)]).astype(np.float32)
    return turns, parity, fore, back, flip


def split(x):
    high = x.astype(BF16)
    return high, (x - high.astype(F32)).astype(BF16)


def dot(a, b):
    return jnp.dot(a, b, preferred_element_type=F32)


def plus(a, b):
    return b if a is None else a if b is None else a + b


def minus(a, b):
    return a if b is None else -b if a is None else a - b


def times(a, scale):
    if a is None or abs(scale) < 1e-12:
        return None
    return a if scale == 1.0 else -a if scale == -1.0 else a * scale


def c_add(a, b):
    return plus(a[0], b[0]), plus(a[1], b[1])


def c_sub(a, b):
    return minus(a[0], b[0]), minus(a[1], b[1])


def c_conj(a):
    return a[0], None if a[1] is None else -a[1]


def c_turn(a, turn):
    c, d = math.cos(2 * math.pi * turn), math.sin(2 * math.pi * turn)
    c, d = (float(round(v)) if abs(v - round(v)) < 1e-12 else v for v in (c, d))
    return minus(times(a[0], c), times(a[1], d)), plus(times(a[0], d), times(a[1], c))


def fft_complex(z, sign):
    n = len(z)
    if n == 1:
        return z
    even, odd = fft_complex(z[::2], sign), fft_complex(z[1::2], sign)
    odd = [c_turn(v, sign * t / n) for t, v in enumerate(odd)]
    return [c_add(e, o) for e, o in zip(even, odd)] + [c_sub(e, o) for e, o in zip(even, odd)]


def fft_real(x):
    n = len(x)
    if n == 1:
        return [(x[0], None)]
    half = n // 2
    even, odd = fft_real(x[::2]), fft_real(x[1::2])
    out = [None] * (half + 1)
    for t, (e, o) in enumerate(zip(even, odd)):
        o = c_turn(o, -t / n)
        out[half - t] = c_conj(c_sub(e, o))
        out[t] = c_add(e, o)
    return out


def fft_to_real(z):
    half = len(z) - 1
    n = 2 * half
    if n == 2:
        return [plus(z[0][0], z[1][0]), minus(z[0][0], z[1][0])]
    even, odd = [], []
    for t in range(half // 2 + 1):
        other = c_conj(z[half - t])
        even.append(c_add(z[t], other))
        odd.append(c_turn(c_sub(z[t], other), t / n))
    out = [None] * n
    out[::2], out[1::2] = fft_to_real(even), fft_to_real(odd)
    return out


def spread(x):
    n = len(x)
    turned = [c_turn((v, None), -p / (2 * n)) for p, v in enumerate(x)]
    even, odd = fft_complex(turned[::2], -1), fft_complex(turned[1::2], -1)
    out = [None] * (n + 1)
    out[::2] = fft_real(x)
    out[1::2] = [c_add(e, c_turn(o, -t / n)) for t, (e, o) in enumerate(zip(even, odd))]
    return out


def gather(z):
    n = len(z) - 1
    ends = [(z[0][0], None), *z[2:n:2], (z[n][0], None)]
    even = fft_to_real(ends)
    odd = [None] * n
    odd[::2] = fft_complex(z[1::2], 1)
    odd[1::2] = fft_complex([c_turn(v, t / n) for t, v in enumerate(z[1::2])], 1)
    return [plus(e, c_turn(o, p / (2 * n))[0]) for p, (e, o) in enumerate(zip(even, odd))]


def causal(x, taps):
    return taps[0:1] * x + taps[1:2] * pltpu.roll(x, 1, 0) + taps[2:3] * pltpu.roll(x, 2, 0)


def block_turn(x, few):
    row = lax.broadcasted_iota(jnp.int32, x.shape, 0)
    block = lax.broadcasted_iota(jnp.int32, x.shape, 1) // few
    out = x
    for d in range(1, 8):
        moved = pltpu.roll(pltpu.roll(x, LANES - few * d, 1), d, 0)
        out = jnp.where((row - block + 8) % 8 == d, moved, out)
    return out


def place(out_ref, near, i, at, value):
    few = value.shape[0] // near
    rows = slice(at // 2, (at + few) // 2)
    out_ref[near * i : near * i + near, rows] = value.reshape(near, few // 2, 2, LANES)


def pack_kernel(
    few, chunks, part_ref, q_ref, k_ref, v_ref, taps_ref, gain_ref, spec_ref,
    out_ref, ends, keys, values, taps, gain, held, sems, held_sems, key_sems,
):
    rows = q_ref.shape[0]
    near = LANES // few
    start = pl.multiple_of(part_ref[0] * (64 * chunks), 64 * chunks)
    blocks = k_ref.shape[1] // LANES
    base = few * chunks

    def columns(i):
        return slice(LANES * i, LANES * i + LANES)

    def chunk_rows(m):
        return spec_ref.at[:, pl.ds(start + 64 * m, 64), :]

    small = [(taps_ref, taps), (gain_ref, gain)]
    small += [(q_ref.at[0:8], ends.at[0:8]), (q_ref.at[rows - 8 : rows], ends.at[8:16])]
    small = [pltpu.make_async_copy(*pair, sems.at[i]) for i, pair in enumerate(small)]
    large = [pltpu.make_async_copy(chunk_rows(m), held.at[m], held_sems.at[m]) for m in range(chunks)]
    inputs = [
        pltpu.make_async_copy(src, dst, key_sems.at[j])
        for j, (src, dst) in enumerate(((k_ref, keys), (v_ref, values)))
    ]
    for copy in (*large, *small, *inputs):
        copy.start()

    def turn_chunk(m):
        for i in range(blocks):
            both = held[m, :, :, columns(i)].reshape(LANES, LANES)
            place(out_ref, near, i, few * m, both.T)

    for copy in large:
        copy.wait()
    for m in range(chunks):
        turn_chunk(m)
    for copy in (*small, *inputs):
        copy.wait()
    for i in range(blocks):
        col = columns(i)
        dests = slice(near * i, near * i + near)
        mixed_in = causal(keys[:, col], taps[1, :, col]) * causal(values[:, col], taps[2, :, col])
        for h in range(rows // LANES):
            turned = mixed_in[LANES * h : LANES * h + LANES].T
            at = base + few * h
            place(out_ref, near, i, at, turned)

        def known(first, last, j):
            t0, t1, t2 = taps[j, 0:1, col], taps[j, 1:2, col], taps[j, 2:3, col]
            own = t0 * first[0:1], t0 * first[1:2] + t1 * first[0:1]
            following = t1 * last[1:2] + t2 * last[0:1], t2 * last[1:2]
            return *own, *following

        k0, k1, next_k0, next_k1 = known(keys[0:2, col], keys[rows - 2 : rows, col], 1)
        v0, v1, next_v0, next_v1 = known(values[0:2, col], values[rows - 2 : rows, col], 2)
        q0, q1, next_q0, next_q1 = known(ends[0:2, col], ends[14:16, col], 0)
        nothing = jnp.zeros_like(q0)
        at = base + few * (rows // LANES)
        pairs = jnp.concatenate([k0, v0, k1, v1, next_k0, next_v0, next_k1, next_v1], axis=0)
        others = [q0, q1, next_q0, next_q1, gain[:, col], nothing, nothing, nothing]
        out_ref[dests, at // 2, 0, :] = block_turn(pairs, few)
        out_ref[dests, at // 2, 1, :] = block_turn(jnp.concatenate(others, axis=0), few)


def local_kernel(q_ref, k_ref, v_ref, taps_ref, gain_ref, query_ref, direct_ref):
    for i in range(q_ref.shape[1] // LANES):
        col = slice(LANES * i, LANES * i + LANES)
        query_seq = causal(q_ref[:, col], taps_ref[0, :, col])
        key_seq = causal(k_ref[:, col], taps_ref[1, :, col])
        value_seq = causal(v_ref[:, col], taps_ref[2, :, col])
        direct = query_seq * (gain_ref[:, col] * (key_seq * value_seq))
        row = lax.broadcasted_iota(jnp.int32, direct.shape, 0)
        query_ref[:, col] = jnp.where(row < 2, 1.0, query_seq)
        direct_ref[:, col] = jnp.where(row < 2, 0.0, direct)


def gate_kernel(conv_ref, query_ref, direct_ref, out_ref, gated, sems):
    few = conv_ref.shape[1]
    near = LANES // few
    leaving = []
    for h in range(conv_ref.shape[2] // LANES):
        row = slice(LANES * h, LANES * h + LANES)
        for i in range(conv_ref.shape[0] // near):
            col = slice(LANES * i, LANES * i + LANES)
            conv = conv_ref[near * i : near * i + near, :, row].reshape(LANES, LANES)
            gated[row, col] = query_ref[row, col] * conv.T + direct_ref[row, col]
        leaving.append(pltpu.make_async_copy(gated.at[row], out_ref.at[row], sems.at[h]))
        leaving[h].start()
    for copy in leaving:
        copy.wait()


def conv_kernel(
    parts, few, chunks, in_ref, turn_ref, parity_ref, fore_ref, back_ref, flip_ref, out_ref, spec, triple, freq, undo, ends, blocks, leaving, sems
):
    devices = in_ref.shape[0] // parts
    outer = 2 * devices
    kept = devices + 1
    base, pitch = few * chunks, few + 1
    left, right = slice(0, LANES), slice(LANES, 2 * LANES)
    lane_of = lax.broadcasted_iota(jnp.int32, (few, LANES), 1)

    everyone = in_ref.shape[0]
    begins = lax.broadcasted_iota(jnp.int32, (everyone, LANES), 0) < parts
    pairs, others = in_ref[:, base // 2 + few, 0, :], in_ref[:, base // 2 + few, 1, :]

    def before(x, lanes):
        moved = pltpu.roll(pltpu.roll(x, parts, 0), LANES - lanes, 1)
        return jnp.where(begins, 0.0, moved)

    pairs = pairs + before(pairs, 4 * few)
    query = others + before(others, 2 * few)
    mixed = pairs * pltpu.roll(pairs, LANES - few, 1)
    gain = pltpu.roll(others, LANES - 4 * few, 1)
    mixed_second = pltpu.roll(mixed, LANES - 2 * few, 1)
    query_second = pltpu.roll(query, LANES - few, 1)
    direct = query * gain * mixed, query_second * gain * mixed_second
    for r, group in enumerate(((mixed, query, direct[0]), (mixed_second, query_second, direct[1]))):
        for j, x in enumerate(group):
            ends[pl.ds(2 * everyone * j + r, everyone, stride=2), :] = x
    ends_of = [ends[2 * everyone * j : 2 * everyone * (j + 1)].T[:few] for j in range(3)]

    def first_lanes(j, at):
        wide = jnp.concatenate([ends_of[j]] * (LANES // (2 * everyone)), axis=1)
        return pltpu.roll(wide, (LANES - 2 * at) % LANES, 1) if at else wide

    odd_cos, odd_sin = parity_ref[0:1], parity_ref[1:2]

    def row_of(low_bit, s, q):
        at = ((low_bit * kept + s) * parts + q) * few
        return slice(at, at + few)

    def keep(span, real, imag):
        for col, value in ((0, real), (LANES, imag)):
            high, low = split(value)
            for j, part in enumerate((high, low, high)):
                at = 2 * LANES * j + col
                triple[span, at : at + LANES] = part

    for j in range(2 * few):
        h, c = divmod(j, few)
        span = pl.ds(h * everyone * pitch + c, everyone, stride=pitch)
        blocks[span, :] = in_ref[:, (base + j) // 2, j % 2, :]

    for q in range(parts):
        tiles = []
        for h in range(2):
            first = [(h * everyone + p * parts + q) * pitch for p in range(devices)]
            x = [blocks[at : at + few] for at in first]
            if h == 0:
                x = [
                    jnp.where(lane_of < 2, first_lanes(0, p * parts + q), own)
                    for p, own in enumerate(x)
                ]
            tiles.append(spread(x))
        for s in range(kept):
            turned = []
            for (re, im), lane in zip((tiles[0][s], tiles[1][s]), (left, right)):
                cosine, sine = turn_ref[0, s : s + 1, lane], turn_ref[1, s : s + 1, lane]
                if im is None:
                    turned.append((re * cosine, -re * sine))
                else:
                    turned.append((re * cosine + im * sine, im * cosine - re * sine))
            keep(row_of(0, s, q), *c_add(*turned))
            re, im = c_sub(*turned)
            keep(row_of(1, s, q), re * odd_cos + im * odd_sin, im * odd_cos - re * odd_sin)

    pieces = 4
    size = freq.shape[0] // pieces
    for j in range(pieces):
        span = slice(j * size, (j + 1) * size)
        freq[span] = dot(triple[span], fore_ref[...])
        for c in range(j * few // pieces, (j + 1) * few // pieces):
            own = jnp.concatenate([in_ref[:, (few * m + c) // 2, c % 2, :] for m in range(chunks)], axis=0)
            spec[pl.ds(c, 4 * outer, stride=pitch), :] = own.T

    other = [[None, None], [None, None]]
    count = outer - kept
    for i in range(2):
        for low_bit in range(2):
            first = (2 * i + low_bit) * outer + kept
            pair = split(spec[first * pitch : (first + count) * pitch])
            other[i][low_bit] = dot(jnp.concatenate(pair, axis=1), flip_ref[...])

    def response(i, low_bit, s):
        at = ((2 * i + low_bit) * outer + s) * pitch
        own = spec[at : at + few]
        if 0 < s < devices:
            at = (outer - s - kept) * pitch
            mirror = other[i][1 - low_bit][at : at + few]
            own = own - mirror if i else own + mirror
        return own

    cuts = (0, kept // 2, kept)
    for low_bit, (begin, end) in itertools.product(range(2), zip(cuts[:-1], cuts[1:])):
        for s in range(begin, end):
            h_re, h_im = response(0, low_bit, s), response(1, low_bit, s)
            for q in range(parts):
                span = row_of(low_bit, s, q)
                re, im = freq[span, left], freq[span, right]
                keep(span, re * h_re - im * h_im, re * h_im + im * h_re)
        span = slice(row_of(low_bit, begin, 0).start, row_of(low_bit, end, 0).start)
        undo[span] = dot(triple[span], back_ref[...])

    copies = []
    for q in range(parts):
        tiles = [], []
        for s in range(kept):
            even, odd = row_of(0, s, q), row_of(1, s, q)
            base_value = undo[even, left], undo[even, right]
            re, im = undo[odd, left], undo[odd, right]
            odd_value = re * odd_cos - im * odd_sin, im * odd_cos + re * odd_sin
            both = c_add(base_value, odd_value), c_sub(base_value, odd_value)
            for tile, (re, im), lane in zip(tiles, both, (left, right)):
                cosine, sine = turn_ref[2, s : s + 1, lane], turn_ref[3, s : s + 1, lane]
                tile.append((re * cosine - im * sine, im * cosine + re * sine))
        for tile, lane in zip(tiles, (left, right)):
            for p, y in enumerate(gather(tile)):
                at = p * parts + q
                if lane == left:
                    finished = first_lanes(1, at) * y + first_lanes(2, at)
                    y = jnp.where(lane_of < 2, finished, y)
                leaving[p, q, :, lane] = y
        copies.append(pltpu.make_async_copy(leaving.at[:, q], out_ref.at[:, q], sems.at[q]))
        copies[q].start()
    for copy in copies:
        copy.wait()


def per_device_tiled(q_proj, k_proj, v_proj, short_filter, skip_gain, filter_spec):
    parts, devices = lax.axis_size("dp"), lax.axis_size("ctx")
    everyone = parts * devices
    rows, channels = q_proj.shape
    few = channels // everyone
    chunks = 2 * rows // parts // 64
    halves = rows // LANES
    depth = few * (chunks + halves) + 2
    outer = 2 * devices
    whole = pl.BlockSpec(memory_space=pltpu.VMEM)
    in_hbm = pl.BlockSpec(memory_space=pltpu.HBM)
    small = pltpu.CompilerParams(vmem_limit_bytes=16 << 20)
    gain_row = skip_gain[None, :]

    part = lax.axis_index("dp").reshape(1)
    sources = (q_proj, k_proj, v_proj, short_filter, gain_row, filter_spec)
    sent = pl.pallas_call(
        functools.partial(pack_kernel, few, chunks),
        out_shape=jax.ShapeDtypeStruct((everyone, depth // 2, 2, LANES), F32),
        in_specs=[pl.BlockSpec(memory_space=pltpu.SMEM)] + [in_hbm] * 6,
        out_specs=whole,
        compiler_params=small,
        scratch_shapes=[
            pltpu.VMEM((16, channels), F32),
            pltpu.VMEM((rows, channels), F32),
            pltpu.VMEM((rows, channels), F32),
            pltpu.VMEM((3, 3, channels), F32),
            pltpu.VMEM((1, channels), F32),
            pltpu.VMEM((chunks, 2, 64, channels), F32),
            pltpu.SemaphoreType.DMA((4,)),
            pltpu.SemaphoreType.DMA((chunks,)),
            pltpu.SemaphoreType.DMA((2,)),
        ],
        cost_estimate=pl.CostEstimate(flops=0, bytes_accessed=1 << 22, transcendentals=0),
    )(part, *(pltpu.with_memory_space_constraint(x, pltpu.HBM) for x in sources))

    come = lax.all_to_all(sent, ("ctx", "dp"), 0, 0, tiled=True)

    query_seq, direct = pl.pallas_call(
        local_kernel,
        out_shape=[jax.ShapeDtypeStruct((rows, channels), F32)] * 2,
        in_specs=[whole] * 5,
        out_specs=[whole] * 2,
        compiler_params=small,
        cost_estimate=pl.CostEstimate(flops=0, bytes_accessed=5 << 19, transcendentals=0),
    )(q_proj, k_proj, v_proj, short_filter, gain_row)

    total = 2 * few * parts * (devices + 1)
    conv = pl.pallas_call(
        functools.partial(conv_kernel, parts, few, chunks),
        out_shape=jax.ShapeDtypeStruct((devices, parts, few, rows), F32),
        in_specs=[whole] * 6,
        out_specs=in_hbm,
        scratch_shapes=[
            pltpu.VMEM((4 * outer * (few + 1), LANES), F32),
            pltpu.VMEM((total, 6 * LANES), BF16),
            pltpu.VMEM((total, 2 * LANES), F32),
            pltpu.VMEM((total, 2 * LANES), F32),
            pltpu.VMEM((6 * everyone, LANES), F32),
            pltpu.VMEM((2 * everyone * (few + 1), LANES), F32),
            pltpu.VMEM((devices, parts, few, rows), F32),
            pltpu.SemaphoreType.DMA((parts,)),
        ],
        compiler_params=small,
        cost_estimate=pl.CostEstimate(flops=0, bytes_accessed=4 << 20, transcendentals=0),
    )(come, *(jnp.asarray(t) for t in tables(parts, devices, rows)))

    back = lax.all_to_all(conv.reshape(everyone, few, rows), ("ctx", "dp"), 0, 0, tiled=True)
    return pl.pallas_call(
        gate_kernel,
        out_shape=jax.ShapeDtypeStruct((rows, channels), F32),
        in_specs=[whole] * 3,
        out_specs=in_hbm,
        scratch_shapes=[pltpu.VMEM((rows, channels), F32), pltpu.SemaphoreType.DMA((halves,))],
        compiler_params=small,
        cost_estimate=pl.CostEstimate(flops=0, bytes_accessed=1 << 21, transcendentals=0),
    )(back, query_seq, direct)


def fits_tiles(mesh, rows, channels):
    parts, devices = mesh.shape["dp"], mesh.shape["ctx"]
    few, rest = divmod(channels, parts * devices)
    chunks = 2 * rows // parts // 64
    return (
        rest == 0
        and few == 16
        and devices == 16
        and rows == 2 * LANES
        and parts * devices * chunks == LANES
        and chunks % 2 == 0
    )


def solution(mesh):
    placed = (
        P(("dp", "ctx"), None),
        P(("dp", "ctx"), None),
        P(("dp", "ctx"), None),
        P(),
        P(),
        P(None, "ctx", None),
    )

    def per_device(q_proj, *rest):
        form = per_device_tiled if fits_tiles(mesh, *q_proj.shape) else per_device_general
        return form(q_proj, *rest)

    return jax.shard_map(
        per_device, mesh=mesh, in_specs=placed, out_specs=P(("dp", "ctx"), None), check_vma=False
    )
```

```python
import functools
import itertools
import math

import jax
import jax.numpy as jnp
import numpy as np
from jax import lax
from jax.experimental import pallas as pl
from jax.experimental.pallas import tpu as pltpu
from jax.sharding import PartitionSpec as P

precise_mode = lax.Precision.HIGHEST
LANES = 128
BF16 = jnp.bfloat16
F32 = jnp.float32


def causal_short(signal, rim_rows, tap_gains):
    padded = jnp.concatenate([rim_rows, signal], axis=0)
    return tap_gains[0] * signal + tap_gains[1] * padded[1:-1] + tap_gains[2] * padded[:-2]


def shifted(block, axis, distance):
    devices = range(lax.axis_size(axis))
    route = [(i - distance, i) for i in devices if i - distance in devices]
    return lax.ppermute(block, axis, route)


def channel_conv(mixed_in, filter_spec, devices):
    local_rows = mixed_in.shape[0]
    seq_len = local_rows * devices
    freq_len = 2 * seq_len
    outer_len = 2 * devices
    half_inner = local_rows // 2
    columns = lax.all_to_all(mixed_in, "ctx", split_axis=1, concat_axis=0, tiled=True)
    spec_cols = lax.all_to_all(filter_spec, "ctx", split_axis=2, concat_axis=1, tiled=True)
    few_channels = columns.shape[1]
    grid = columns.reshape(half_inner, outer_len, few_channels)
    row_index = lax.iota(jnp.int32, half_inner)
    inner_freq = lax.iota(jnp.int32, local_rows)
    outer_index = lax.iota(jnp.int32, outer_len)

    def cos_sin(left, right, period):
        turns = (left[:, None] * right[None, :] % period).astype(F32) / period
        return jnp.cos(2.0 * math.pi * turns), jnp.sin(2.0 * math.pi * turns)

    first_cos, first_sin = cos_sin(row_index, inner_freq, local_rows)
    twist_cos, twist_sin = cos_sin(inner_freq, outer_index, freq_len)
    twist_cos, twist_sin = twist_cos[:, :, None], twist_sin[:, :, None]
    last_cos, last_sin = cos_sin(outer_index, outer_index, outer_len)
    dots = functools.partial(jnp.einsum, precision=precise_mode)
    section_re = dots("bk,bac->kac", first_cos, grid)
    section_im = -dots("bk,bac->kac", first_sin, grid)
    turned_re = section_re * twist_cos + section_im * twist_sin
    turned_im = section_im * twist_cos - section_re * twist_sin
    fore = "kac,aj->kjc"
    spec_re = dots(fore, turned_re, last_cos) + dots(fore, turned_im, last_sin)
    spec_im = dots(fore, turned_im, last_cos) - dots(fore, turned_re, last_sin)
    resp = jnp.transpose(spec_cols.reshape(2, outer_len, local_rows, few_channels), (0, 2, 1, 3))
    prod_re = spec_re * resp[0] - spec_im * resp[1]
    prod_im = spec_re * resp[1] + spec_im * resp[0]
    back = "kjc,aj->kac"
    undo_re = dots(back, prod_re, last_cos) - dots(back, prod_im, last_sin)
    undo_im = dots(back, prod_im, last_cos) + dots(back, prod_re, last_sin)
    back_re = undo_re * twist_cos - undo_im * twist_sin
    back_im = undo_im * twist_cos + undo_re * twist_sin
    signal_out = dots("bk,kac->bac", first_cos, back_re) - dots("bk,kac->bac", first_sin, back_im)
    conv_cols = signal_out.reshape(seq_len, few_channels) / freq_len
    return lax.all_to_all(conv_cols, "ctx", split_axis=0, concat_axis=1, tiled=True)


def per_device_general(q_proj, k_proj, v_proj, short_filter, skip_gain, filter_spec):
    devices = lax.axis_size("ctx")
    tail_rows = jnp.stack([q_proj[-2:], k_proj[-2:], v_proj[-2:]])
    rim_rows = shifted(tail_rows, "ctx", 1)
    query_seq = causal_short(q_proj, rim_rows[0], short_filter[0])
    key_seq = causal_short(k_proj, rim_rows[1], short_filter[1])
    value_seq = causal_short(v_proj, rim_rows[2], short_filter[2])
    mixed_in = key_seq * value_seq
    conv_out = channel_conv(mixed_in, filter_spec, devices)
    return query_seq * (conv_out + skip_gain[None, :] * mixed_in)


def split_np(table):
    high = table.astype(BF16)
    low = (table - high.astype(np.float64)).astype(BF16)
    return high, low


@functools.lru_cache(maxsize=None)
def tables(parts, devices, rows):
    outer, seq = 2 * devices, devices * rows
    freq = 2 * seq
    chunks = rows * 2 // parts // 64
    low_bit, chunk, dev, part = np.meshgrid(
        np.arange(2), np.arange(chunks), np.arange(devices), np.arange(parts), indexing="ij"
    )
    k = (dev * (2 * rows // outer) + part * (2 * rows // parts // outer) + 2 * chunk + low_bit).ravel()

    def angle(left, right, period):
        return 2.0 * np.pi * (np.outer(left, right) % period) / period

    s, r, half = np.arange(devices + 1), np.arange(rows), rows // 2
    twist = angle(s, r, freq)
    weight = np.where((s % 2 == 1) | (s % devices == 0), 2.0, 1.0)[:, None] / (2 * freq)
    turns = [np.cos(twist), np.sin(twist), weight * np.cos(twist), weight * np.sin(twist)]
    parity = angle([1], r[:half], rows)
    inner = angle(r[:half], k[:half] // 2, half)
    c, d = np.cos(inner), np.sin(inner)

    def tripled(table):
        high, low = split_np(table)
        return np.concatenate([high, high, low])

    fore = tripled(np.block([[c, -d], [d, c]]))
    back = tripled(np.block([[c.T, d.T], [-d.T, c.T]]))
    flip = np.concatenate([np.eye(LANES)[::-1]] * 2).astype(BF16)
    turns = np.stack(turns).astype(np.float32)
    parity = np.concatenate([np.cos(parity), np.sin(parity)]).astype(np.float32)
    return turns, parity, fore, back, flip


def split(x):
    high = x.astype(BF16)
    return high, (x - high.astype(F32)).astype(BF16)


def dot(a, b):
    return jnp.dot(a, b, preferred_element_type=F32)


def plus(a, b):
    return b if a is None else a if b is None else a + b


def minus(a, b):
    return a if b is None else -b if a is None else a - b


def times(a, scale):
    if a is None or abs(scale) < 1e-12:
        return None
    return a if scale == 1.0 else -a if scale == -1.0 else a * scale


def c_add(a, b):
    return plus(a[0], b[0]), plus(a[1], b[1])


def c_sub(a, b):
    return minus(a[0], b[0]), minus(a[1], b[1])


def c_conj(a):
    return a[0], None if a[1] is None else -a[1]


def c_turn(a, turn):
    c, d = math.cos(2 * math.pi * turn), math.sin(2 * math.pi * turn)
    c, d = (float(round(v)) if abs(v - round(v)) < 1e-12 else v for v in (c, d))
    return minus(times(a[0], c), times(a[1], d)), plus(times(a[0], d), times(a[1], c))


def fft_complex(z, sign):
    n = len(z)
    if n == 1:
        return z
    even, odd = fft_complex(z[::2], sign), fft_complex(z[1::2], sign)
    odd = [c_turn(v, sign * t / n) for t, v in enumerate(odd)]
    return [c_add(e, o) for e, o in zip(even, odd)] + [c_sub(e, o) for e, o in zip(even, odd)]


def fft_real(x):
    n = len(x)
    if n == 1:
        return [(x[0], None)]
    half = n // 2
    even, odd = fft_real(x[::2]), fft_real(x[1::2])
    out = [None] * (half + 1)
    for t, (e, o) in enumerate(zip(even, odd)):
        o = c_turn(o, -t / n)
        out[half - t] = c_conj(c_sub(e, o))
        out[t] = c_add(e, o)
    return out


def fft_to_real(z):
    half = len(z) - 1
    n = 2 * half
    if n == 2:
        return [plus(z[0][0], z[1][0]), minus(z[0][0], z[1][0])]
    even, odd = [], []
    for t in range(half // 2 + 1):
        other = c_conj(z[half - t])
        even.append(c_add(z[t], other))
        odd.append(c_turn(c_sub(z[t], other), t / n))
    out = [None] * n
    out[::2], out[1::2] = fft_to_real(even), fft_to_real(odd)
    return out


def spread(x):
    n = len(x)
    turned = [c_turn((v, None), -p / (2 * n)) for p, v in enumerate(x)]
    even, odd = fft_complex(turned[::2], -1), fft_complex(turned[1::2], -1)
    out = [None] * (n + 1)
    out[::2] = fft_real(x)
    out[1::2] = [c_add(e, c_turn(o, -t / n)) for t, (e, o) in enumerate(zip(even, odd))]
    return out


def gather(z):
    n = len(z) - 1
    ends = [(z[0][0], None), *z[2:n:2], (z[n][0], None)]
    even = fft_to_real(ends)
    odd = [None] * n
    odd[::2] = fft_complex(z[1::2], 1)
    odd[1::2] = fft_complex([c_turn(v, t / n) for t, v in enumerate(z[1::2])], 1)
    return [plus(e, c_turn(o, p / (2 * n))[0]) for p, (e, o) in enumerate(zip(even, odd))]


def causal(x, taps):
    return taps[0:1] * x + taps[1:2] * pltpu.roll(x, 1, 0) + taps[2:3] * pltpu.roll(x, 2, 0)


def block_turn(x, few):
    row = lax.broadcasted_iota(jnp.int32, x.shape, 0)
    block = lax.broadcasted_iota(jnp.int32, x.shape, 1) // few
    out = x
    for d in range(1, 8):
        moved = pltpu.roll(pltpu.roll(x, LANES - few * d, 1), d, 0)
        out = jnp.where((row - block + 8) % 8 == d, moved, out)
    return out


def place(out_ref, near, i, at, value):
    few = value.shape[0] // near
    rows = slice(at // 2, (at + few) // 2)
    out_ref[near * i : near * i + near, rows] = value.reshape(near, few // 2, 2, LANES)


def pack_kernel(
    few, chunks, part_ref, q_ref, k_ref, v_ref, taps_ref, gain_ref, spec_ref,
    out_ref, ends, keys, values, taps, gain, held, sems, held_sems, key_sems,
):
    rows = q_ref.shape[0]
    near = LANES // few
    start = pl.multiple_of(part_ref[0] * (64 * chunks), 64 * chunks)
    blocks = k_ref.shape[1] // LANES
    base = few * chunks

    def columns(i):
        return slice(LANES * i, LANES * i + LANES)

    small = [(taps_ref, taps), (gain_ref, gain)]
    small += [(q_ref.at[0:8], ends.at[0:8]), (q_ref.at[rows - 8 : rows], ends.at[8:16])]
    small = [pltpu.make_async_copy(*pair, sems.at[i]) for i, pair in enumerate(small)]
    large = [pltpu.make_async_copy(spec_ref.at[:, pl.ds(start, 64 * chunks), :], held, held_sems.at[0])]
    inputs = [
        pltpu.make_async_copy(src, dst, key_sems.at[j])
        for j, (src, dst) in enumerate(((k_ref, keys), (v_ref, values)))
    ]
    for copy in (*large, *small, *inputs):
        copy.start()

    def turn_chunk(m):
        for i in range(blocks):
            both = held[:, 64 * m : 64 * m + 64, columns(i)].reshape(LANES, LANES)
            place(out_ref, near, i, few * m, both.T)

    for copy in large:
        copy.wait()
    for m in range(chunks):
        turn_chunk(m)
    for copy in (*small, *inputs):
        copy.wait()
    for i in range(blocks):
        col = columns(i)
        dests = slice(near * i, near * i + near)
        mixed_in = causal(keys[:, col], taps[1, :, col]) * causal(values[:, col], taps[2, :, col])
        for h in range(rows // LANES):
            turned = mixed_in[LANES * h : LANES * h + LANES].T
            at = base + few * h
            place(out_ref, near, i, at, turned)

        def known(first, last, j):
            t0, t1, t2 = taps[j, 0:1, col], taps[j, 1:2, col], taps[j, 2:3, col]
            own = t0 * first[0:1], t0 * first[1:2] + t1 * first[0:1]
            following = t1 * last[1:2] + t2 * last[0:1], t2 * last[1:2]
            return *own, *following

        k0, k1, next_k0, next_k1 = known(keys[0:2, col], keys[rows - 2 : rows, col], 1)
        v0, v1, next_v0, next_v1 = known(values[0:2, col], values[rows - 2 : rows, col], 2)
        q0, q1, next_q0, next_q1 = known(ends[0:2, col], ends[14:16, col], 0)
        nothing = jnp.zeros_like(q0)
        at = base + few * (rows // LANES)
        pairs = jnp.concatenate([k0, v0, k1, v1, next_k0, next_v0, next_k1, next_v1], axis=0)
        others = [q0, q1, next_q0, next_q1, gain[:, col], nothing, nothing, nothing]
        out_ref[dests, at // 2, 0, :] = block_turn(pairs, few)
        out_ref[dests, at // 2, 1, :] = block_turn(jnp.concatenate(others, axis=0), few)


def local_kernel(q_ref, k_ref, v_ref, taps_ref, gain_ref, query_ref, direct_ref):
    for i in range(q_ref.shape[1] // LANES):
        col = slice(LANES * i, LANES * i + LANES)
        query_seq = causal(q_ref[:, col], taps_ref[0, :, col])
        key_seq = causal(k_ref[:, col], taps_ref[1, :, col])
        value_seq = causal(v_ref[:, col], taps_ref[2, :, col])
        direct = query_seq * (gain_ref[:, col] * (key_seq * value_seq))
        row = lax.broadcasted_iota(jnp.int32, direct.shape, 0)
        query_ref[:, col] = jnp.where(row < 2, 1.0, query_seq)
        direct_ref[:, col] = jnp.where(row < 2, 0.0, direct)


def gate_kernel(conv_ref, query_ref, direct_ref, out_ref, gated, sems):
    few = conv_ref.shape[1]
    near = LANES // few
    leaving = []
    for h in range(conv_ref.shape[2] // LANES):
        row = slice(LANES * h, LANES * h + LANES)
        for i in range(conv_ref.shape[0] // near):
            col = slice(LANES * i, LANES * i + LANES)
            conv = conv_ref[near * i : near * i + near, :, row].reshape(LANES, LANES)
            gated[row, col] = query_ref[row, col] * conv.T + direct_ref[row, col]
        leaving.append(pltpu.make_async_copy(gated.at[row], out_ref.at[row], sems.at[h]))
        leaving[h].start()
    for copy in leaving:
        copy.wait()


def conv_kernel(
    parts, few, chunks, in_ref, turn_ref, parity_ref, fore_ref, back_ref, flip_ref, out_ref, spec, triple, freq, undo, ends, blocks, leaving, sems
):
    devices = in_ref.shape[0] // parts
    outer = 2 * devices
    kept = devices + 1
    base, pitch = few * chunks, few + 1
    left, right = slice(0, LANES), slice(LANES, 2 * LANES)
    lane_of = lax.broadcasted_iota(jnp.int32, (few, LANES), 1)

    everyone = in_ref.shape[0]
    begins = lax.broadcasted_iota(jnp.int32, (everyone, LANES), 0) < parts
    pairs, others = in_ref[:, base // 2 + few, 0, :], in_ref[:, base // 2 + few, 1, :]

    def before(x, lanes):
        moved = pltpu.roll(pltpu.roll(x, parts, 0), LANES - lanes, 1)
        return jnp.where(begins, 0.0, moved)

    pairs = pairs + before(pairs, 4 * few)
    query = others + before(others, 2 * few)
    mixed = pairs * pltpu.roll(pairs, LANES - few, 1)
    gain = pltpu.roll(others, LANES - 4 * few, 1)
    mixed_second = pltpu.roll(mixed, LANES - 2 * few, 1)
    query_second = pltpu.roll(query, LANES - few, 1)
    direct = query * gain * mixed, query_second * gain * mixed_second
    for r, group in enumerate(((mixed, query, direct[0]), (mixed_second, query_second, direct[1]))):
        for j, x in enumerate(group):
            ends[pl.ds(2 * everyone * j + r, everyone, stride=2), :] = x
    ends_of = [ends[2 * everyone * j : 2 * everyone * (j + 1)].T[:few] for j in range(3)]

    def first_lanes(j, at):
        wide = jnp.concatenate([ends_of[j]] * (LANES // (2 * everyone)), axis=1)
        return pltpu.roll(wide, (LANES - 2 * at) % LANES, 1) if at else wide

    odd_cos, odd_sin = parity_ref[0:1], parity_ref[1:2]

    def row_of(low_bit, s, q):
        at = ((low_bit * kept + s) * parts + q) * few
        return slice(at, at + few)

    def keep(span, real, imag):
        for col, value in ((0, real), (LANES, imag)):
            high, low = split(value)
            for j, part in enumerate((high, low, high)):
                at = 2 * LANES * j + col
                triple[span, at : at + LANES] = part

    for j in range(2 * few):
        h, c = divmod(j, few)
        span = pl.ds(h * everyone * pitch + c, everyone, stride=pitch)
        blocks[span, :] = in_ref[:, (base + j) // 2, j % 2, :]

    for q in range(parts):
        tiles = []
        for h in range(2):
            first = [(h * everyone + p * parts + q) * pitch for p in range(devices)]
            x = [blocks[at : at + few] for at in first]
            if h == 0:
                x = [
                    jnp.where(lane_of < 2, first_lanes(0, p * parts + q), own)
                    for p, own in enumerate(x)
                ]
            tiles.append(spread(x))
        for s in range(kept):
            turned = []
            for (re, im), lane in zip((tiles[0][s], tiles[1][s]), (left, right)):
                cosine, sine = turn_ref[0, s : s + 1, lane], turn_ref[1, s : s + 1, lane]
                if im is None:
                    turned.append((re * cosine, -re * sine))
                else:
                    turned.append((re * cosine + im * sine, im * cosine - re * sine))
            keep(row_of(0, s, q), *c_add(*turned))
            re, im = c_sub(*turned)
            keep(row_of(1, s, q), re * odd_cos + im * odd_sin, im * odd_cos - re * odd_sin)

    pieces = 4
    size = freq.shape[0] // pieces
    for j in range(pieces):
        span = slice(j * size, (j + 1) * size)
        freq[span] = dot(triple[span], fore_ref[...])
        for c in range(j * few // pieces, (j + 1) * few // pieces):
            own = jnp.concatenate([in_ref[:, (few * m + c) // 2, c % 2, :] for m in range(chunks)], axis=0)
            spec[pl.ds(c, 4 * outer, stride=pitch), :] = own.T

    other = [[None, None], [None, None]]
    count = outer - kept
    for i in range(2):
        for low_bit in range(2):
            first = (2 * i + low_bit) * outer + kept
            pair = split(spec[first * pitch : (first + count) * pitch])
            other[i][low_bit] = dot(jnp.concatenate(pair, axis=1), flip_ref[...])

    def response(i, low_bit, s):
        at = ((2 * i + low_bit) * outer + s) * pitch
        own = spec[at : at + few]
        if 0 < s < devices:
            at = (outer - s - kept) * pitch
            mirror = other[i][1 - low_bit][at : at + few]
            own = own - mirror if i else own + mirror
        return own

    cuts = (0, kept // 2, kept)
    for low_bit, (begin, end) in itertools.product(range(2), zip(cuts[:-1], cuts[1:])):
        for s in range(begin, end):
            h_re, h_im = response(0, low_bit, s), response(1, low_bit, s)
            for q in range(parts):
                span = row_of(low_bit, s, q)
                re, im = freq[span, left], freq[span, right]
                keep(span, re * h_re - im * h_im, re * h_im + im * h_re)
        span = slice(row_of(low_bit, begin, 0).start, row_of(low_bit, end, 0).start)
        undo[span] = dot(triple[span], back_ref[...])

    copies = []
    for q in range(parts):
        tiles = [], []
        for s in range(kept):
            even, odd = row_of(0, s, q), row_of(1, s, q)
            base_value = undo[even, left], undo[even, right]
            re, im = undo[odd, left], undo[odd, right]
            odd_value = re * odd_cos - im * odd_sin, im * odd_cos + re * odd_sin
            both = c_add(base_value, odd_value), c_sub(base_value, odd_value)
            for tile, (re, im), lane in zip(tiles, both, (left, right)):
                cosine, sine = turn_ref[2, s : s + 1, lane], turn_ref[3, s : s + 1, lane]
                tile.append((re * cosine - im * sine, im * cosine + re * sine))
        for tile, lane in zip(tiles, (left, right)):
            for p, y in enumerate(gather(tile)):
                at = p * parts + q
                if lane == left:
                    finished = first_lanes(1, at) * y + first_lanes(2, at)
                    y = jnp.where(lane_of < 2, finished, y)
                leaving[p, q, :, lane] = y
        copies.append(pltpu.make_async_copy(leaving.at[:, q], out_ref.at[:, q], sems.at[q]))
        copies[q].start()
    for copy in copies:
        copy.wait()


def per_device_tiled(q_proj, k_proj, v_proj, short_filter, skip_gain, filter_spec):
    parts, devices = lax.axis_size("dp"), lax.axis_size("ctx")
    everyone = parts * devices
    rows, channels = q_proj.shape
    few = channels // everyone
    chunks = 2 * rows // parts // 64
    halves = rows // LANES
    depth = few * (chunks + halves) + 2
    outer = 2 * devices
    whole = pl.BlockSpec(memory_space=pltpu.VMEM)
    in_hbm = pl.BlockSpec(memory_space=pltpu.HBM)
    small = pltpu.CompilerParams(vmem_limit_bytes=16 << 20)
    gain_row = skip_gain[None, :]

    part = lax.axis_index("dp").reshape(1)
    sources = (q_proj, k_proj, v_proj, short_filter, gain_row, filter_spec)
    sent = pl.pallas_call(
        functools.partial(pack_kernel, few, chunks),
        out_shape=jax.ShapeDtypeStruct((everyone, depth // 2, 2, LANES), F32),
        in_specs=[pl.BlockSpec(memory_space=pltpu.SMEM)] + [in_hbm] * 6,
        out_specs=whole,
        compiler_params=small,
        scratch_shapes=[
            pltpu.VMEM((16, channels), F32),
            pltpu.VMEM((rows, channels), F32),
            pltpu.VMEM((rows, channels), F32),
            pltpu.VMEM((3, 3, channels), F32),
            pltpu.VMEM((1, channels), F32),
            pltpu.VMEM((2, 64 * chunks, channels), F32),
            pltpu.SemaphoreType.DMA((4,)),
            pltpu.SemaphoreType.DMA((1,)),
            pltpu.SemaphoreType.DMA((2,)),
        ],
        cost_estimate=pl.CostEstimate(flops=0, bytes_accessed=1 << 22, transcendentals=0),
    )(part, *(pltpu.with_memory_space_constraint(x, pltpu.HBM) for x in sources))

    come = lax.all_to_all(sent, ("ctx", "dp"), 0, 0, tiled=True)

    query_seq, direct = pl.pallas_call(
        local_kernel,
        out_shape=[jax.ShapeDtypeStruct((rows, channels), F32)] * 2,
        in_specs=[whole] * 5,
        out_specs=[whole] * 2,
        compiler_params=small,
        cost_estimate=pl.CostEstimate(flops=0, bytes_accessed=5 << 19, transcendentals=0),
    )(q_proj, k_proj, v_proj, short_filter, gain_row)

    total = 2 * few * parts * (devices + 1)
    conv = pl.pallas_call(
        functools.partial(conv_kernel, parts, few, chunks),
        out_shape=jax.ShapeDtypeStruct((devices, parts, few, rows), F32),
        in_specs=[whole] * 6,
        out_specs=in_hbm,
        scratch_shapes=[
            pltpu.VMEM((4 * outer * (few + 1), LANES), F32),
            pltpu.VMEM((total, 6 * LANES), BF16),
            pltpu.VMEM((total, 2 * LANES), F32),
            pltpu.VMEM((total, 2 * LANES), F32),
            pltpu.VMEM((6 * everyone, LANES), F32),
            pltpu.VMEM((2 * everyone * (few + 1), LANES), F32),
            pltpu.VMEM((devices, parts, few, rows), F32),
            pltpu.SemaphoreType.DMA((parts,)),
        ],
        compiler_params=small,
        cost_estimate=pl.CostEstimate(flops=0, bytes_accessed=4 << 20, transcendentals=0),
    )(come, *(jnp.asarray(t) for t in tables(parts, devices, rows)))

    back = lax.all_to_all(conv.reshape(everyone, few, rows), ("ctx", "dp"), 0, 0, tiled=True)
    return pl.pallas_call(
        gate_kernel,
        out_shape=jax.ShapeDtypeStruct((rows, channels), F32),
        in_specs=[whole] * 3,
        out_specs=in_hbm,
        scratch_shapes=[pltpu.VMEM((rows, channels), F32), pltpu.SemaphoreType.DMA((halves,))],
        compiler_params=small,
        cost_estimate=pl.CostEstimate(flops=0, bytes_accessed=1 << 21, transcendentals=0),
    )(back, query_seq, direct)


def fits_tiles(mesh, rows, channels):
    parts, devices = mesh.shape["dp"], mesh.shape["ctx"]
    few, rest = divmod(channels, parts * devices)
    chunks = 2 * rows // parts // 64
    return (
        rest == 0
        and few == 16
        and devices == 16
        and rows == 2 * LANES
        and parts * devices * chunks == LANES
        and chunks % 2 == 0
    )


def solution(mesh):
    placed = (
        P(("dp", "ctx"), None),
        P(("dp", "ctx"), None),
        P(("dp", "ctx"), None),
        P(),
        P(),
        P(None, "ctx", None),
    )

    def per_device(q_proj, *rest):
        form = per_device_tiled if fits_tiles(mesh, *q_proj.shape) else per_device_general
        return form(q_proj, *rest)

    return jax.shard_map(
        per_device, mesh=mesh, in_specs=placed, out_specs=P(("dp", "ctx"), None), check_vma=False
    )
```
